32 devices in a mesh: basin: 8 (over z, x), event: 4 (over y, core).
Axes of the slice: x: 2, y: 2, z: 4, core: 2. Of those that a mesh axis runs over, the one named last changes fastest.
Arguments:
- reach_attrs: bfloat16 [12288, 32], P('basin'), may hold values from -6 to 6
- w_first: bfloat16 [32, 768], replicated, may hold values from -1 to 1
- b_first: float32 [768], replicated, may hold values from -3 to 3
- w_second: bfloat16 [768, 768], replicated, may hold values from -0.21875 to 0.21875
- b_second: float32 [768], replicated, may hold values from -3 to 3
- w_out: bfloat16 [768], replicated, may hold values from -0.21875 to 0.21875
- section_factor: float32 [10], replicated, may hold values from 0.5 to 2
- bed_slope: float32 [12288], P('basin'), may hold values from 0.0001 to 0.004
- seg_count: int32 [12288], P('basin'), may hold values from 1 to 8
- section_class: int32 [12288], P('basin'), may hold values from 0 to 9
- down_local: int32 [12288], P('basin'), may hold values from 0 to 1536, as said below
- send_list: int32 [8, 8, 24], P('basin'), may hold values from 0 to 1536, as said below
- recv_list: int32 [8, 8, 24], P('basin'), may hold values from 0 to 1536, as said below
- area_start: float32 [128, 12288], P('event', 'basin'), may hold values from 0.2 to 2
- lateral: float32 [3, 128, 12288], P(None, 'event', 'basin'), may hold values from 0.05 to 1
- cotangent: float32 [128, 12288], P('event', 'basin'), may hold values from -6 to 6
Outputs:
- outflow: float32 [128, 12288], P('event', 'basin')
- grad_lateral: float32 [3, 128, 12288], P(None, 'event', 'basin')
- grad_w_first: float32 [32, 768], replicated
- grad_b_first: float32 [768], replicated
- grad_w_second: float32 [768, 768], replicated
- grad_b_second: float32 [768], replicated
- grad_w_out: float32 [768], replicated
The draws below stay inside these ranges and needn't reach their ends.
Inputs may be any that keep to these rules, and one draw needn't show every extreme that they name: `down_local`: the downstream reach of a reach in its own sub-basin, as a local index 1 to 8 above the reach's own; 1536 where the reach drains into another sub-basin (it is then listed in send_list) or leaves the network. send_list[s, d, c] is a local reach of sub-basin s whose end flow enters sub-basin d, or 1536 for an empty slot; live slots come first in each list and no reach is listed twice. Only the lists from s to (s + 1), (s + 2), (s + 4) and (s + 7) mod 8 can hold live slots; those to (s + 1), (s + 4) and (s + 7) are always full, the one to (s + 2) is empty or holds 12 or more. One sub-basin receives 24 from each of the four sub-basins that can drain into it. recv_list[d, s, c] is the local reach of sub-basin d that receives slot c of send_list[s, d], and is 1536 exactly where that slot is empty; no reach is a target twice.
All inputs are finite; a program needn't handle non-finite values.
Results may differ from the reference program's by a relative error of at most 0.02.
Values sent between devices are 32-bit elements; how exact they have to be, the bound alone decides.
A program may use at most 64 MiB of HBM per device.

```python
import math
import jax
import jax.numpy as jnp
from jax import lax

FEAT = 32
HID = 768
NCLASS = 10
SEGMAX = 8
STEPS = 3
CAP = 24
R_DEV = 1536
REACHES = 12288
EVENTS = 128


def topology(key):
    basins = REACHES // R_DEV
    base_key = jax.random.fold_in(key, 11)
    key_two = jax.random.fold_in(base_key, 0)
    key_on = jax.random.fold_in(base_key, 2)
    key_busy = jax.random.fold_in(base_key, 3)
    key_send = jax.random.fold_in(base_key, 4)
    key_recv = jax.random.fold_in(base_key, 5)
    key_down = jax.random.fold_in(base_key, 6)
    row_index = jnp.arange(basins, dtype=jnp.int32)[:, None]
    col_index = jnp.arange(basins, dtype=jnp.int32)[None, :]
    offset = (col_index - row_index) % basins
    count_two = jax.random.randint(key_two, (basins, basins), CAP // 2, CAP + 1)
    switch_on = jax.random.randint(key_on, (basins, basins), 0, 2)
    count_two = jnp.where(switch_on == 1, count_two, 0)
    always_full = (offset == 1) | (offset == basins // 2) | (offset == basins - 1)
    slot_count = jnp.where(always_full, CAP, jnp.where(offset == 2, count_two, 0))
    busiest = jax.random.randint(key_busy, (), 0, basins)
    full_pair = (col_index == busiest) & (offset == 2)
    slot_count = jnp.where(full_pair, CAP, slot_count)
    live_slot = jnp.arange(CAP, dtype=jnp.int32)[None, None, :] < slot_count[:, :, None]
    send_order = jax.vmap(lambda one_key: jax.random.permutation(one_key, R_DEV))(jax.random.split(key_send, basins))
    send_pick = send_order[:, :basins * CAP].reshape(basins, basins, CAP)
    send_list = jnp.where(live_slot, send_pick, R_DEV).astype(jnp.int32)
    recv_order = jax.vmap(lambda one_key: jax.random.permutation(one_key, R_DEV))(jax.random.split(key_recv, basins))
    recv_pick = recv_order[:, :basins * CAP].reshape(basins, basins, CAP)
    recv_list = jnp.where(jnp.transpose(live_slot, (1, 0, 2)), recv_pick, R_DEV).astype(jnp.int32)
    hop_sizes = jax.random.randint(key_down, (basins, R_DEV), 1, 9)
    next_reach = jnp.arange(R_DEV, dtype=jnp.int32)[None, :] + hop_sizes
    next_reach = jnp.where(next_reach >= R_DEV, R_DEV, next_reach)
    sender_mark = jnp.zeros((basins, R_DEV + 1), jnp.int32).at[row_index, send_list.reshape(basins, basins * CAP)].set(1)
    down_local = jnp.where(sender_mark[:, :R_DEV] == 1, R_DEV, next_reach).reshape(REACHES).astype(jnp.int32)
    return (down_local, send_list, recv_list)


def draw_down_local(key, part):
    return topology(key)[0]


def draw_send_list(key, part):
    return topology(key)[1]


def draw_recv_list(key, part):
    return topology(key)[2]


def set_ends(result, own_key, low, top_value):
    longest = result.shape.index(max(result.shape))
    spots = []
    for shift in (0, 1):
        where = [jax.random.randint(jax.random.fold_in(own_key, axis), (), 0, length) for axis, length in enumerate(result.shape)]
        where[longest] = (where[longest] + shift) % result.shape[longest]
        spots.append(tuple(where))
    return result.at[spots[0]].set(low).at[spots[1]].set(top_value)


def levels(own_key, extent, shards, low, largest):
    loudness, own = 1.0, jax.random.fold_in(own_key, 6)
    for position, shards_of in shards:
        heights = jnp.exp(jax.random.uniform(jax.random.fold_in(own, position), (shards_of,), jnp.float32, low / len(shards), largest / len(shards)))
        loudness = loudness * jnp.repeat(heights, extent[position] // shards_of).reshape([-1 if axis == position else 1 for axis in range(len(extent))])
    return loudness


def bell_draw(own_key, extent, scale, most, cuts=(), held_as=jnp.bfloat16):
    drawn = scale * jax.random.normal(own_key, extent, jnp.float32)
    if cuts:
        drawn = drawn * levels(own_key, extent, cuts, -0.22, 0.18)
    return jnp.clip(drawn, -most, most).astype(held_as)


def setup_inputs(seed: int = 0) -> dict:
    keys = jax.random.split(jax.random.key(seed), 17)
    return {
        "reach_attrs": bell_draw(keys[0], (REACHES, FEAT), 1.0, 6.0, ((0, 8),)),
        "w_first": bell_draw(keys[1], (FEAT, HID), FEAT ** -0.5, 1.0),
        "b_first": bell_draw(keys[2], (HID,), 0.5, 3.0, (), jnp.float32),
        "w_second": bell_draw(keys[3], (HID, HID), HID ** -0.5, 0.21875),
        "b_second": bell_draw(keys[4], (HID,), 0.5, 3.0, (), jnp.float32),
        "w_out": bell_draw(keys[5], (HID,), HID ** -0.5, 0.21875),
        "section_factor": jnp.clip(jnp.exp(jax.random.uniform(keys[6], (NCLASS,), jnp.float32, math.log(0.5), math.log(2.0))), 0.5, 2.0),
        "bed_slope": jnp.clip(jnp.exp(math.log(0.004) - 3.6888795 * jax.random.uniform(keys[7], (REACHES,), jnp.float32) ** levels(keys[7], (REACHES,), ((0, 8),), -0.2, 0.2)), 0.0001, 0.004),
        "seg_count": set_ends(jax.random.randint(keys[8], (REACHES,), 1, SEGMAX + 1), jax.random.fold_in(keys[8], 1), 1, SEGMAX).astype(jnp.int32),
        "section_class": set_ends(jax.random.randint(keys[9], (REACHES,), 0, NCLASS), jax.random.fold_in(keys[9], 1), 0, NCLASS - 1).astype(jnp.int32),
        "down_local": draw_down_local(jax.random.fold_in(keys[16], 71), 0),
        "send_list": draw_send_list(jax.random.fold_in(keys[16], 71), 0),
        "recv_list": draw_recv_list(jax.random.fold_in(keys[16], 71), 0),
        "area_start": jnp.clip(jnp.exp(math.log(2.0) - 2.3025851 * jax.random.uniform(keys[13], (EVENTS, REACHES), jnp.float32) ** levels(keys[13], (EVENTS, REACHES), ((0, 4), (1, 8)), -0.2, 0.2)), 0.2, 2.0),
        "lateral": jnp.clip(jnp.exp(math.log(1.0) - 2.9957323 * jax.random.uniform(keys[14], (STEPS, EVENTS, REACHES), jnp.float32) ** levels(keys[14], (STEPS, EVENTS, REACHES), ((1, 4), (2, 8)), -0.2, 0.2)), 0.05, 1.0),
        "cotangent": bell_draw(keys[15], (EVENTS, REACHES), 1.0, 6.0, ((0, 4), (1, 8)), jnp.float32),
    }


def emit(area_now, flow_rate):
    return flow_rate * area_now ** (5.0 / 3.0)

def advance(area_now, inflow, lateral_now, flow_rate, beta_step):
    return (area_now + beta_step * (inflow + lateral_now)) / (1.0 + beta_step * flow_rate * area_now ** (2.0 / 3.0))

def network_forward(reach_attrs, w_first, b_first, w_second, b_second, w_out):
    tanh_one = jnp.tanh(jnp.dot(reach_attrs, w_first, preferred_element_type=jnp.float32) + b_first)
    hid_one = tanh_one.astype(jnp.bfloat16)
    tanh_two = jnp.tanh(jnp.dot(hid_one, w_second, preferred_element_type=jnp.float32) + b_second)
    hid_two = tanh_two.astype(jnp.bfloat16)
    squash = jax.nn.sigmoid(jnp.dot(hid_two, w_out, preferred_element_type=jnp.float32))
    return (0.02 + 0.08 * squash, (tanh_one, hid_one, tanh_two, hid_two, squash))

def upper_grads(saved_acts, w_out, g_rough, scale):
    tanh_one, hid_one, tanh_two, hid_two, squash = saved_acts
    g_logit = (g_rough * scale * 0.08 * squash * (1.0 - squash)).astype(jnp.bfloat16)
    grad_w_out = jnp.dot(g_logit, hid_two, preferred_element_type=jnp.float32)
    g_pre_two = g_logit.astype(jnp.float32)[:, None] * w_out.astype(jnp.float32)[None, :] * (1.0 - tanh_two * tanh_two)
    g_two = g_pre_two.astype(jnp.bfloat16)
    grad_w_second = jnp.dot(hid_one.T, g_two, preferred_element_type=jnp.float32)
    return (g_two, (grad_w_out, lax.optimization_barrier(jnp.sum(g_pre_two, axis=0)), grad_w_second))

def lower_grads(reach_attrs, w_second, saved_acts, g_two):
    tanh_one = saved_acts[0]
    g_pre_one = jnp.dot(g_two, w_second.T, preferred_element_type=jnp.float32) * (1.0 - tanh_one * tanh_one)
    grad_w_first = jnp.dot(reach_attrs.T, g_pre_one.astype(jnp.bfloat16), preferred_element_type=jnp.float32)
    return (lax.optimization_barrier(jnp.sum(g_pre_one, axis=0)), grad_w_first)

def reference(reach_attrs, w_first, b_first, w_second, b_second, w_out, section_factor, bed_slope, seg_count, section_class, down_local, send_list, recv_list, area_start, lateral, cotangent):
    basins = REACHES // R_DEV
    width_in = reach_attrs.shape[1]
    block_attrs = reach_attrs.reshape(basins, R_DEV, width_in)

    def rough_block(attr_block):
        return network_forward(attr_block, w_first, b_first, w_second, b_second, w_out)[0]
    roughness = lax.map(rough_block, block_attrs).reshape(REACHES)
    one_hot = (section_class[:, None] == jnp.arange(NCLASS, dtype=jnp.int32)[None, :]).astype(jnp.float32)
    k_base = jnp.sqrt(bed_slope) * lax.optimization_barrier(jnp.sum(one_hot * section_factor[None, :], axis=1))
    beta_step = 1.0 / seg_count.astype(jnp.float32)
    owner = jnp.arange(REACHES, dtype=jnp.int32) // R_DEV
    down_global = jnp.where(down_local == R_DEV, REACHES, owner * R_DEV + down_local).astype(jnp.int32)
    source_idx = jnp.arange(basins, dtype=jnp.int32)[:, None, None]
    send_src = jnp.where(send_list == R_DEV, REACHES, source_idx * R_DEV + send_list).astype(jnp.int32).reshape(-1)
    recv_pairs = jnp.transpose(recv_list, (1, 0, 2))
    target_idx = jnp.arange(basins, dtype=jnp.int32)[None, :, None]
    recv_dst = jnp.where(recv_pairs == R_DEV, REACHES, target_idx * R_DEV + recv_pairs).astype(jnp.int32).reshape(-1)

    def confluence(flow_now):
        events_here = flow_now.shape[0]
        padded = jnp.concatenate([flow_now, jnp.zeros((events_here, 1), flow_now.dtype)], axis=1)
        inflow = jnp.zeros((events_here, REACHES + 1), flow_now.dtype).at[:, down_global].add(flow_now)
        inflow = inflow.at[:, recv_dst].add(padded[:, send_src])
        return inflow[:, :REACHES]

    def route(lateral_all, rough_all):
        flow_rate = k_base / rough_all
        area_now = area_start
        flow_now = emit(area_now, flow_rate)
        for step in range(STEPS):
            area_now = advance(area_now, confluence(flow_now), lateral_all[step], flow_rate, beta_step)
            flow_now = emit(area_now, flow_rate)
        return flow_now
    outflow, pull_back = jax.vjp(route, lateral, roughness)
    grad_lateral, g_rough = pull_back(cotangent)
    scale = 32.0 / math.sqrt(EVENTS * REACHES)
    block_grads = g_rough.reshape(basins, R_DEV)

    def add_block(totals, pieces):
        attr_block, g_block = pieces
        saved_acts = network_forward(attr_block, w_first, b_first, w_second, b_second, w_out)[1]
        g_two, upper = upper_grads(saved_acts, w_out, g_block, scale)
        lower = lower_grads(attr_block, w_second, saved_acts, g_two)
        return (jax.tree.map(jnp.add, totals, upper + lower), None)
    start_sums = (jnp.zeros((HID,), jnp.float32), jnp.zeros((HID,), jnp.float32), jnp.zeros((HID, HID), jnp.float32), jnp.zeros((HID,), jnp.float32), jnp.zeros((width_in, HID), jnp.float32))
    totals, _ = lax.scan(add_block, start_sums, (block_attrs, block_grads))
    grad_w_out, grad_b_second, grad_w_second, grad_b_first, grad_w_first = totals
    return (outflow, grad_lateral, grad_w_first, grad_b_first, grad_w_second, grad_b_second, grad_w_out)
```

```python
import functools
import math

import jax
import jax.numpy as jnp
from jax import lax
from jax.experimental import pallas as pl
from jax.experimental.pallas import tpu as pltpu
from jax.sharding import PartitionSpec as P

STEPS = 3
LINKS = 4
GROUP = 32
PLACES = 48
MESH = pl.DeviceIdType.MESH
NT = (((1,), (1,)), ((), ()))


def split_two(x):
    high = x.astype(jnp.bfloat16)
    low = (x - high.astype(jnp.float32)).astype(jnp.bfloat16)
    return jnp.concatenate([high, low], axis=0)


def kernel(
    n, n_event, owners, chunk, scale,
    attrs_h, w_first_h, b_first_h, w_second_h, b_second_h, w_out_h, section_factor,
    bed_slope_h, seg_count_h, section_class_h, down_local_h, send_list_h, recv_list_h,
    area_start_h, lateral_h, cotangent_h,
    outflow, grad_lateral, full,
    attrs, w_first, b_first, w_second, b_second, w_out,
    bed_slope, seg_count, section_class, down_local, send_list, recv_list,
    area_start, lateral, cotangent, load_sem,
    w_firstT, w_secondT, cols,
    t_one, h_one, d_two, h_two, lower, squash_all, take_send, take_recv,
    out_msg, in_msg, rate_out, rate_in, slab, rs_pair, rs_line,
    s_send, s_recv,
    x_send, x_recv, r_send, r_recv, px_send, px_recv, pz_send, pz_recv,
    az_send, az_recv, ax_send, ax_recv, ay_send, ay_recv,
    fa_send, fa_recv, fb_send, fb_recv, tw_send, tw_recv,
):
    f32, bf16 = jnp.float32, jnp.bfloat16
    me = lax.axis_index("basin")
    ev = lax.axis_index("event")
    events, reaches = area_start.shape
    hid = w_second.shape[0]
    feat = w_first.shape[0]
    part = hid // n_event
    offsets = (1, 2, n // 2, n - 1)
    base = pl.multiple_of(ev * part, 64)
    mine = pl.ds(base, part)
    width = reaches // n_event

    loads = {}
    for name, source, target in (
        ("w_first", w_first_h, w_first),
        ("attrs", attrs_h, attrs.at[pl.ds(0, feat)]),
        ("b_first", b_first_h, b_first),
        ("b_second", b_second_h, b_second),
        ("w_out", w_out_h, w_out),
        ("w_second", w_second_h, w_second),
        ("send_list", send_list_h, send_list),
        ("recv_list", recv_list_h, recv_list),
        ("bed_slope", bed_slope_h, bed_slope),
        ("section_class", section_class_h, section_class),
        ("seg_count", seg_count_h, seg_count),
        ("down_local", down_local_h, down_local),
        ("area_start", area_start_h, area_start),
        ("lateral", lateral_h, lateral),
        ("cotangent", cotangent_h, cotangent),
    ):
        loads[name] = pltpu.make_async_copy(source, target, load_sem.at[len(loads)])
        loads[name].start()

    barrier = pltpu.get_barrier_semaphore()

    @pl.loop(1, n)
    def _(i):
        pl.semaphore_signal(barrier, inc=1, device_id={"basin": lax.rem(me + i, n)}, device_id_type=MESH)

    for i in range(1, n_event):
        pl.semaphore_signal(
            barrier, inc=1, device_id={"event": lax.rem(ev + i, n_event)}, device_id_type=MESH
        )

    for name in ("w_first", "attrs", "b_first", "b_second", "w_out", "w_second"):
        loads[name].wait()

    extra = attrs.shape[0] - feat
    attrs[feat:, :] = jnp.where(
        lax.broadcasted_iota(jnp.int32, (extra, reaches), 0) == 0, 1.0, 0.0
    ).astype(bf16)
    w_firstT[...] = jnp.transpose(w_first[...])
    w_secondT[...] = jnp.transpose(w_second[...])
    w_out_row = w_out[...].astype(f32).reshape(1, hid)
    cols[...] = jnp.transpose(jnp.concatenate(
        [b_first[...].reshape(1, hid), b_second[...].reshape(1, hid), w_out_row,
         jnp.zeros((5, hid), f32)], axis=0
    ))
    w_out_rows = jnp.broadcast_to(w_out_row, (16, hid)).astype(bf16)

    def network(block):
        where = pl.ds(pl.multiple_of(block * width, 128), width)
        one = jnp.tanh(
            jnp.dot(w_firstT[...], attrs[0:feat, where], preferred_element_type=f32) + cols[:, 0:1]
        )
        t_one[:, where] = one
        hidden = one.astype(bf16)
        h_one[:, where] = hidden
        two = jnp.tanh(
            jnp.dot(w_secondT[...], hidden, preferred_element_type=f32) + cols[:, 1:2]
        )
        rounded = two.astype(bf16)
        h_two[:, where] = rounded
        factor = (cols[:, 2:3] * (1.0 - two * two)).astype(bf16)
        d_two[:, where] = factor
        first = t_one[mine, where]
        lower[:, where] = (
            jnp.dot(w_second[mine, :], factor, preferred_element_type=f32) * (1.0 - first * first)
        )
        return rounded

    logit = jnp.dot(w_out_rows, network(ev), preferred_element_type=f32)[0:1]
    squash_all[ev] = 1.0 / (1.0 + jnp.exp(-logit))

    pl.semaphore_wait(barrier, n - 1 + n_event - 1)

    def squash_copy(i):
        return pltpu.make_async_remote_copy(
            src_ref=squash_all.at[ev],
            dst_ref=squash_all.at[ev],
            send_sem=s_send.at[i],
            recv_sem=s_recv.at[i],
            device_id={"event": lax.rem(ev + 1 + i, n_event)},
            device_id_type=MESH,
        )

    for i in range(n_event - 1):
        squash_copy(i).start()

    for name in ("send_list", "recv_list", "bed_slope", "section_class", "seg_count", "down_local",
                 "area_start"):
        loads[name].wait()

    slot_row = lax.broadcasted_iota(jnp.int32, (LINKS * GROUP, 1), 0)
    slot = slot_row % GROUP
    cap = send_list.shape[2]
    spread = (
        slot == lax.broadcasted_iota(jnp.int32, (LINKS * GROUP, cap), 1)
    ).astype(f32)
    lane_reach = lax.broadcasted_iota(jnp.int32, (LINKS * GROUP, reaches), 1).astype(f32)
    lane_basin = lax.broadcasted_iota(jnp.int32, (LINKS * GROUP, n), 1)

    def one_hot_of(lists, sign):
        table = lax.dot_general(
            spread, lists[0].astype(f32), NT, precision=lax.Precision.HIGHEST,
            preferred_element_type=f32,
        )
        peer = jnp.zeros((LINKS * GROUP, 1), jnp.int32)
        for k, off in enumerate(offsets):
            peer = jnp.where(slot_row // GROUP == k, lax.rem(me + sign * off + n, n), peer)
        column = jnp.sum(jnp.where(lane_basin == peer, table, 0.0), axis=1, keepdims=True)
        column = jnp.where(slot < cap, column, float(reaches))
        return (jnp.abs(lane_reach - column) < 0.5).astype(bf16)

    take_send[...] = one_hot_of(send_list, 1)
    take_recv[...] = one_hot_of(recv_list, -1)

    kind = section_class[...].reshape(1, reaches)
    conveyance = jnp.zeros((1, reaches), f32)
    for c in range(section_factor.shape[0]):
        conveyance = jnp.where(kind == c, section_factor[c], conveyance)
    k_base = jnp.sqrt(bed_slope[...].reshape(1, reaches)) * conveyance
    beta = 1.0 / seg_count[...].reshape(1, reaches).astype(f32)
    down = down_local[...].reshape(1, reaches)
    hop = jnp.where(down < reaches, down - lax.broadcasted_iota(jnp.int32, (1, reaches), 1), 0)
    masks = [(hop == d).astype(f32) for d in range(1, 9)]

    network(lax.rem(ev + 1, n_event))

    for i in range(n_event - 1):
        squash_copy(i).wait_recv()
    squash = jnp.concatenate([squash_all[e] for e in range(n_event)], axis=1)
    rough = 0.02 + 0.08 * squash
    rate = k_base / rough
    lane_group = lax.broadcasted_iota(jnp.int32, (8, 128), 1) // GROUP
    blocks = events // 8

    def message(index, k, sign):
        return pltpu.make_async_remote_copy(
            src_ref=out_msg.at[index, k],
            dst_ref=in_msg.at[index, k],
            send_sem=x_send.at[index, k],
            recv_sem=x_recv.at[index, k],
            device_id={"basin": lax.rem(me + sign * offsets[k] + n, n)},
            device_id_type=MESH,
        )

    def send(index, field, matrix, sign):
        both = lax.dot_general(split_two(field), matrix[...], NT, preferred_element_type=f32)
        picked = both[:events] + both[events:]
        for k in range(LINKS):
            packed = jnp.zeros((8, 128), f32)
            for q in range(blocks):
                piece = picked[8 * q : 8 * q + 8]
                shift = ((q - k) * GROUP) % 128
                if shift:
                    piece = pltpu.roll(piece, shift, 1)
                packed = jnp.where(lane_group == q, piece, packed)
            out_msg[index, k] = packed
            message(index, k, sign).start()

    def receive(index, matrix, sign):
        for k in range(LINKS):
            message(index, k, sign).wait_recv()
        pieces = []
        for q in range(blocks):
            got = jnp.zeros((8, 128), f32)
            for k in range(LINKS):
                piece = in_msg[index, k]
                shift = ((k - q) * GROUP) % 128
                if shift:
                    piece = pltpu.roll(piece, shift, 1)
                got = jnp.where(lane_group == k, piece, got)
            pieces.append(got)
        both = jnp.dot(
            split_two(jnp.concatenate(pieces, axis=0)), matrix[...], preferred_element_type=f32
        )
        return both[:events] + both[events:]

    def power(area):
        return jnp.exp((2.0 / 3.0) * jnp.log(area))

    areas = [area_start[...]]
    powers = [power(areas[0])]
    shrinks = []
    for t in range(STEPS):
        area, p = areas[t], powers[t]
        flow = rate * area * p
        send(t, flow, take_send, 1)
        if t == 0:
            loads["lateral"].wait()
        inflow = lateral[t]
        for d in range(1, 9):
            inflow = inflow + pltpu.roll(flow * masks[d - 1], d, 1)
        shrink = 1.0 / (1.0 + beta * rate * p)
        shrinks.append(shrink)
        if t < n_event - 2:
            network(lax.rem(ev + 2 + t, n_event))
        inflow = inflow + receive(t, take_recv, 1)
        areas.append((area + beta * inflow) * shrink)
        powers.append(power(areas[t + 1]))
    emitted = areas[STEPS] * powers[STEPS]
    outflow[...] = rate * emitted
    loads["cotangent"].wait()
    g_area = cotangent[...] * rate * (5.0 / 3.0) * powers[STEPS]
    g_rate = cotangent[...] * emitted
    for t in reversed(range(STEPS)):
        index = 2 * STEPS - 1 - t
        inner = g_area * shrinks[t]
        g_inflow = inner * beta
        grad_lateral[t] = g_inflow
        send(index, g_inflow, take_recv, -1)
        g_flow = jnp.zeros((events, reaches), f32)
        for d in range(1, 9):
            g_flow = g_flow + masks[d - 1] * pltpu.roll(g_inflow, reaches - d, 1)
        drop = g_inflow * areas[t + 1] * powers[t]
        g_rate = g_rate - drop
        g_area = inner - (2.0 / 3.0) * rate * drop / areas[t]
        g_flow = g_flow + receive(index, take_send, -1)
        g_rate = g_rate + g_flow * areas[t] * powers[t]
        g_area = g_area + (5.0 / 3.0) * rate * powers[t] * g_flow
    rate_out[...] = jnp.sum(g_rate, axis=0, keepdims=True)

    def rate_copy(i):
        return pltpu.make_async_remote_copy(
            src_ref=rate_out,
            dst_ref=rate_in.at[i],
            send_sem=r_send.at[i],
            recv_sem=r_recv.at[i],
            device_id={"event": lax.rem(ev + 1 + i, n_event)},
            device_id_type=MESH,
        )

    for i in range(n_event - 1):
        rate_copy(i).start()
    for i in range(n_event - 1):
        rate_copy(i).wait_recv()
    terms = [rate_out[...]] + [rate_in[i] for i in range(n_event - 1)]
    g_sum = jnp.zeros((1, reaches), f32)
    for e in range(n_event):
        term = terms[0]
        for i in range(n_event - 1):
            term = jnp.where(lax.rem(e + 1 + i, n_event) == ev, terms[i + 1], term)
        g_sum = g_sum + term
    g_logit = (
        g_sum * (-rate / rough) * (scale * 0.08) * squash * (1.0 - squash)
    ).astype(bf16)
    g_logit32 = g_logit.astype(f32)

    scaled = (h_one[mine, :].astype(f32) * g_logit32).astype(bf16)
    large = lax.dot_general(scaled, d_two[...], NT, preferred_element_type=f32)
    tiles = hid // 128
    for d in range(owners):
        for r in range(chunk // 8):
            for c in range(tiles):
                top = d * chunk + 8 * r
                slab[d, r * tiles + c] = large[top : top + 8, 128 * c : 128 * c + 128]

    g_pre = (lower[...] * g_logit32).astype(bf16)
    place = lax.broadcasted_iota(jnp.int32, (PLACES, reaches), 0)
    row_two = jnp.where(place == feat + 1, g_logit32, 0.0).astype(bf16)
    row_out = jnp.where(place == feat + 2, g_logit32, 0.0).astype(bf16)
    g_two = d_two[mine, :]
    second = h_two[mine, :]

    def narrow(low):
        high = low + 128
        return (
            lax.dot_general(attrs[...], g_pre[low:high], NT, preferred_element_type=f32)
            + lax.dot_general(row_two, g_two[low:high], NT, preferred_element_type=f32)
            + lax.dot_general(row_out, second[low:high], NT, preferred_element_type=f32)
        )

    left = narrow(0)
    right = narrow(part - 128)
    first_half = lax.broadcasted_iota(jnp.int32, (8, 128), 1) < 64
    last = slab.shape[1] - 1
    for k in range(5):
        slab[k, last] = left[8 * k : 8 * k + 8]
    for k in range(3):
        even = pltpu.roll(right[16 * k : 16 * k + 8], 64, 1)
        slab[5 + k, last] = jnp.where(first_half, even, right[16 * k + 8 : 16 * k + 16])
    for d in range(8, owners):
        slab[d, last] = jnp.zeros((8, 128), f32)

    def when_owner(index, work):
        if owners == n:
            work()
        else:
            pl.when(index < owners)(work)

    line = n // 2
    low = lax.rem(me, 2)
    spot = me // 2
    pair = me + 1 - 2 * low
    half = lax.rem(ev + n_event // 2, n_event)
    twin = ev + 1 - 2 * lax.rem(ev, 2)
    twin_half = lax.rem(twin + n_event // 2, n_event)
    span = slab.shape[1]
    cut = (span + 1) // 2

    def each(first, last, work):
        if last - first <= 4:
            for j in range(first, last):
                work(j)
        else:
            pl.loop(first, last)(work)

    def near(j):
        if line != 4:
            return lax.rem(spot + j, line)
        if isinstance(j, int) and j == 0:
            return spot
        orders = ((1, 2, 3), (2, 0, 3), (1, 3, 0), (2, 1, 0))
        code = sum(orders[s][j - 1] * 4 ** s for s in range(4))
        power_of = (1 + 3 * lax.rem(spot, 2)) * (1 + 15 * (spot // 2))
        return lax.rem(code // power_of, 4)

    def device(z, parity):
        return 2 * z + parity

    def pair_sum(z, parity):
        return pltpu.make_async_remote_copy(
            src_ref=slab.at[device(z, parity)], dst_ref=rs_pair.at[z],
            send_sem=px_send.at[z], recv_sem=px_recv.at[z],
            device_id={"basin": pair}, device_id_type=MESH,
        )

    def line_sum(z, sender):
        return pltpu.make_async_remote_copy(
            src_ref=rs_pair.at[z], dst_ref=rs_line.at[sender],
            send_sem=pz_send.at[z], recv_sem=pz_recv.at[sender],
            device_id={"basin": device(z, low)}, device_id_type=MESH,
        )

    def far(j):
        return near(line - 1 - j)

    def start_pair(j):
        z = far(j)
        when_owner(device(z, 1 - low), lambda: pair_sum(z, 1 - low).start())

    each(0, line, start_pair)

    def add_pair(j):
        z = far(j)

        def go():
            pair_sum(z, 1 - low).wait_recv()
            rs_pair[z] = rs_pair[z] + slab[device(z, low)]

            @pl.when(z != spot)
            def _():
                line_sum(z, spot).start()

        when_owner(device(z, low), go)

    each(0, line, add_pair)

    whole = pl.ds(0, span)
    upper = pl.ds(0, cut)
    under = pl.ds(cut, span - cut)

    def move(event, at, rows, sems, slot, target):
        ref = full.at[event, at, rows]
        return pltpu.make_async_remote_copy(
            src_ref=ref, dst_ref=ref, send_sem=sems[0].at[slot], recv_sem=sems[1].at[slot],
            device_id=target, device_id_type=MESH,
        )

    def to_line(source, peer):
        ref = full.at[ev, device(source, low)]
        return pltpu.make_async_remote_copy(
            src_ref=ref, dst_ref=ref, send_sem=az_send.at[peer], recv_sem=az_recv.at[source],
            device_id={"basin": device(peer, low)}, device_id_type=MESH,
        )

    def to_pair(z, parity):
        return move(ev, device(z, parity), whole, (ax_send, ax_recv), z, {"basin": pair})

    def to_half(event, z):
        return move(event, device(z, low), whole, (ay_send, ay_recv), z, {"event": half})

    def on_half(event, z):
        return move(event, device(z, 1 - low), upper, (fa_send, fa_recv), z, {"event": half})

    def on_pair(z, parity):
        return move(half, device(z, parity), under, (fb_send, fb_recv), z, {"basin": pair})

    def to_twin(side, event, z):
        ref = full.at[event, pl.ds(2 * z, 2)]
        return pltpu.make_async_remote_copy(
            src_ref=ref, dst_ref=ref, send_sem=tw_send.at[side, z], recv_sem=tw_recv.at[side, z],
            device_id={"event": twin}, device_id_type=MESH,
        )

    def own():
        def add(i, total):
            sender = lax.rem(spot + line - i, line)
            line_sum(spot, sender).wait_recv()
            return total + rs_line[sender]

        full[ev, me] = lax.fori_loop(1, line, add, rs_pair[spot])
        each(1, line, lambda j: to_line(spot, near(j)).start())
        to_pair(spot, low).start()
        to_half(ev, spot).start()

    when_owner(me, own)

    def from_line(j):
        z = near(j)

        def go():
            to_line(z, spot).wait_recv()
            to_pair(z, low).start()
            to_half(ev, z).start()

        when_owner(device(z, low), go)

    def second_hop(j):
        z = near(j)

        def go():
            to_pair(z, 1 - low).wait_recv()
            on_half(ev, z).start()
            to_twin(0, ev, z).start()
            to_half(half, z).wait_recv()
            on_pair(z, low).start()

        when_owner(2 * z, go)

    def corner(j):
        z = near(j)

        def go():
            on_half(half, z).wait_recv()
            on_pair(z, 1 - low).wait_recv()
            to_twin(1, half, z).start()

        when_owner(2 * z, go)

    if line <= 4:
        for j in range(1, line):
            from_line(j)
            second_hop(j - 1)
            if j >= 2:
                corner(j - 2)
        second_hop(line - 1)
        corner(line - 2)
        corner(line - 1)
    else:
        pl.loop(1, line)(from_line)
        pl.loop(0, line)(second_hop)
        pl.loop(0, line)(corner)

    for i in range(n_event - 1):
        squash_copy(i).wait_send()
    for index in range(2 * STEPS):
        for k in range(LINKS):
            message(index, k, 1).wait_send()
    for i in range(n_event - 1):
        rate_copy(i).wait_send()

    def drain(z):
        when_owner(device(z, 1 - low), lambda: pair_sum(z, 1 - low).wait_send())

        @pl.when(z != spot)
        def _():
            when_owner(device(z, low), lambda: line_sum(z, spot).wait_send())
            when_owner(me, lambda: to_line(spot, z).wait_send())

        def go():
            to_pair(z, low).wait_send()
            to_half(ev, z).wait_send()
            on_half(ev, z).wait_send()
            on_pair(z, low).wait_send()
            to_twin(0, ev, z).wait_send()
            to_twin(1, half, z).wait_send()

        when_owner(2 * z, go)

    each(0, line, drain)

    def arrive(j):
        z = near(j)

        def go():
            to_twin(0, twin, z).wait_recv()
            to_twin(1, twin_half, z).wait_recv()

        when_owner(2 * z, go)

    each(0, line, arrive)


def finish(
    feat, full, flow_in, lateral_in,
    large, flow_out, lateral_out, w_first, b_first, b_second, w_out, sems,
):
    last = full.shape[2] - 1
    copies = [
        pltpu.make_async_copy(full.at[:, :, pl.ds(0, last)], large, sems.at[0]),
        pltpu.make_async_copy(lateral_in, lateral_out, sems.at[1]),
        pltpu.make_async_copy(flow_in, flow_out, sems.at[2]),
    ]
    for copy in copies:
        copy.start()
    n_event = full.shape[0]
    first_half = lax.broadcasted_iota(jnp.int32, (8, 128), 1) < 64
    for k in range(5):
        columns = []
        for e in range(0, n_event, 2):
            tails = []
            for s in range(2):
                tail = full[e + s, 5 + k // 2, last]
                tails.append(pltpu.roll(tail, 64, 1) if k % 2 != s else tail)
            turned = pltpu.roll(full[e + 1, k, last], 64, 1)
            columns += [
                full[e, k, last],
                jnp.where(first_half, tails[0], turned),
                jnp.where(first_half, turned, tails[1]),
            ]
        rows = jnp.concatenate(columns, axis=1)
        if k < 4:
            w_first[8 * k : 8 * k + 8, :] = rows
        else:
            b_first[...] = rows[0:1].reshape(rows.shape[1])
            b_second[...] = rows[1:2].reshape(rows.shape[1])
            w_out[...] = rows[2:3].reshape(rows.shape[1])
    for copy in copies:
        copy.wait()


def body(
    n,
    n_event,
    reach_attrs,
    w_first,
    b_first,
    w_second,
    b_second,
    w_out,
    section_factor,
    bed_slope,
    seg_count,
    section_class,
    down_local,
    send_list,
    recv_list,
    area_start,
    lateral,
    cotangent,
):
    f32, bf16 = jnp.float32, jnp.bfloat16
    events, reaches = area_start.shape
    feat, hid = w_first.shape
    part = hid // n_event
    owners = n if part % (8 * n) == 0 else part // 8
    chunk = part // owners
    span = (chunk // 8) * (hid // 128) + 1
    line = n // 2
    scale = 32.0 / math.sqrt(events * n_event * reaches * n)
    vmem = pl.BlockSpec(memory_space=pltpu.VMEM)
    hbm = pl.BlockSpec(memory_space=pltpu.HBM)
    smem = pl.BlockSpec(memory_space=pltpu.SMEM)
    dma = pltpu.SemaphoreType.DMA
    held = lambda x: pltpu.VMEM(x.shape, x.dtype)
    outflow, grad_lateral, full = pl.pallas_call(
        functools.partial(kernel, n, n_event, owners, chunk, scale),
        out_shape=(
            jax.ShapeDtypeStruct((events, reaches), f32),
            jax.ShapeDtypeStruct((STEPS, events, reaches), f32),
            jax.ShapeDtypeStruct((n_event, owners, span, 8, 128), f32),
        ),
        in_specs=[hbm] * 6 + [smem] + [hbm] * 9,
        out_specs=(vmem,) * 3,
        scratch_shapes=[
            pltpu.VMEM((PLACES, reaches), bf16),
            held(w_first), held(b_first), held(w_second), held(b_second), held(w_out),
            held(bed_slope), held(seg_count), held(section_class), held(down_local),
            held(send_list), held(recv_list), held(area_start), held(lateral), held(cotangent),
            dma((15,)),
            pltpu.VMEM((hid, feat), bf16),
            pltpu.VMEM((hid, hid), bf16),
            pltpu.VMEM((hid, 8), f32),
            pltpu.VMEM((hid, reaches), f32),
            pltpu.VMEM((hid, reaches), bf16),
            pltpu.VMEM((hid, reaches), bf16),
            pltpu.VMEM((hid, reaches), bf16),
            pltpu.VMEM((part, reaches), f32),
            pltpu.VMEM((n_event, 1, reaches // n_event), f32),
            pltpu.VMEM((LINKS * GROUP, reaches), bf16),
            pltpu.VMEM((LINKS * GROUP, reaches), bf16),
            pltpu.VMEM((2 * STEPS, LINKS, 8, 128), f32),
            pltpu.VMEM((2 * STEPS, LINKS, 8, 128), f32),
            pltpu.VMEM((1, reaches), f32),
            pltpu.VMEM((n_event - 1, 1, reaches), f32),
            pltpu.VMEM((owners, span, 8, 128), f32),
            pltpu.VMEM((line, span, 8, 128), f32),
            pltpu.VMEM((line, span, 8, 128), f32),
            dma((n_event - 1,)), dma((n_event - 1,)),
            dma((2 * STEPS, LINKS)), dma((2 * STEPS, LINKS)),
            dma((n_event - 1,)), dma((n_event - 1,)),
            dma((line,)), dma((line,)), dma((line,)), dma((line,)),
            dma((line,)), dma((line,)), dma((line,)), dma((line,)), dma((line,)), dma((line,)),
            dma((line,)), dma((line,)), dma((line,)), dma((line,)), dma((2, line)), dma((2, line)),
        ],
        compiler_params=pltpu.CompilerParams(
            collective_id=0, has_side_effects=True, vmem_limit_bytes=63 * 1024 * 1024
        ),
    )(
        reach_attrs.T, w_first, b_first, w_second, b_second, w_out, section_factor,
        bed_slope, seg_count, section_class, down_local, send_list, recv_list,
        area_start, lateral, cotangent,
    )
    vector = jax.ShapeDtypeStruct((hid,), f32)
    large, outflow, grad_lateral, g_first, g_b_first, g_b_second, g_out = pl.pallas_call(
        functools.partial(finish, feat),
        out_shape=(
            jax.ShapeDtypeStruct((n_event, owners, span - 1, 8, 128), f32),
            jax.ShapeDtypeStruct((events, reaches), f32),
            jax.ShapeDtypeStruct((STEPS, events, reaches), f32),
            jax.ShapeDtypeStruct((feat, hid), f32),
            vector,
            vector,
            vector,
        ),
        in_specs=[vmem] * 3,
        out_specs=(hbm, hbm, hbm, vmem, vmem, vmem, vmem),
        scratch_shapes=[dma((3,))],
    )(full, outflow, grad_lateral)
    g_second = large.reshape(hid // 8, hid // 128, 8, 128).transpose(0, 2, 1, 3).reshape(hid, hid)
    return outflow, grad_lateral, g_first, g_b_first, g_second, g_b_second, g_out


def solution(mesh):
    return jax.shard_map(
        functools.partial(body, mesh.shape["basin"], mesh.shape["event"]),
        mesh=mesh,
        in_specs=(
            P("basin", None),
            P(),
            P(),
            P(),
            P(),
            P(),
            P(),
            P("basin"),
            P("basin"),
            P("basin"),
            P("basin"),
            P("basin", None, None),
            P("basin", None, None),
            P("event", "basin"),
            P(None, "event", "basin"),
            P("event", "basin"),
        ),
        out_specs=(P("event", "basin"), P(None, "event", "basin"), P(), P(), P(), P(), P()),
        check_vma=False,
    )
```

```python
import functools
import math

import jax
import jax.numpy as jnp
from jax import lax
from jax.experimental import pallas as pl
from jax.experimental.pallas import tpu as pltpu
from jax.sharding import PartitionSpec as P

STEPS = 3
HALO = 2 * STEPS
LINKS = 4
GROUP = 32
PLACES = 48
MESH = pl.DeviceIdType.MESH
NT = (((1,), (1,)), ((), ()))


def split_two(x):
    high = x.astype(jnp.bfloat16)
    low = (x - high.astype(jnp.float32)).astype(jnp.bfloat16)
    return jnp.concatenate([high, low], axis=0)


def kernel(
    n, n_event, owners, chunk, scale,
    attrs_h, w_first_h, b_first_h, w_second_h, b_second_h, w_out_h, section_factor,
    bed_slope_h, seg_count_h, section_class_h, down_local_h, send_list_h, recv_list_h,
    area_start_h, lateral_h, cotangent_h,
    outflow_h, grad_lateral_h, full_h,
    outflow, grad_lateral, full, out_sem,
    attrs, w_first, b_first, w_second, b_second, w_out,
    bed_slope, seg_count, section_class, down_local, send_list, recv_list,
    area_start, lateral, cotangent, load_sem,
    w_firstT, w_secondT, cols,
    t_one, h_one, d_two, h_two, lower, squash_all, take_send, take_recv,
    out_msg, in_msg, rate_out, rate_in, slab, rs_pair, rs_line,
    s_send, s_recv,
    x_send, x_recv, r_send, r_recv, px_send, px_recv, pz_send, pz_recv,
    az_send, az_recv, ax_send, ax_recv, ay_send, ay_recv,
    fa_send, fa_recv, fb_send, fb_recv, tw_send, tw_recv, write_sem,
):
    f32, bf16 = jnp.float32, jnp.bfloat16
    me = lax.axis_index("basin")
    ev = lax.axis_index("event")
    events, reaches = area_start.shape
    hid = w_second.shape[0]
    feat = w_first.shape[0]
    part = hid // n_event
    offsets = (1, 2, n // 2, n - 1)
    base = pl.multiple_of(ev * part, 64)
    mine = pl.ds(base, part)
    width = reaches // n_event

    loads = {}
    for name, source, target in (
        ("w_first", w_first_h, w_first),
        ("attrs", attrs_h, attrs.at[pl.ds(0, feat)]),
        ("b_first", b_first_h, b_first),
        ("b_second", b_second_h, b_second),
        ("w_out", w_out_h, w_out),
        ("w_second", w_second_h, w_second),
        ("send_list", send_list_h, send_list),
        ("recv_list", recv_list_h, recv_list),
        ("bed_slope", bed_slope_h, bed_slope),
        ("section_class", section_class_h, section_class),
        ("seg_count", seg_count_h, seg_count),
        ("down_local", down_local_h, down_local),
        ("area_start", area_start_h, area_start),
        ("lateral", lateral_h, lateral),
        ("cotangent", cotangent_h, cotangent),
    ):
        loads[name] = pltpu.make_async_copy(source, target, load_sem.at[len(loads)])
        loads[name].start()

    barrier = pltpu.get_barrier_semaphore()

    @pl.loop(1, n)
    def _(i):
        pl.semaphore_signal(barrier, inc=1, device_id={"basin": lax.rem(me + i, n)}, device_id_type=MESH)

    for i in range(1, n_event):
        pl.semaphore_signal(
            barrier, inc=1, device_id={"event": lax.rem(ev + i, n_event)}, device_id_type=MESH
        )

    for name in ("send_list", "attrs", "area_start", "bed_slope", "section_class"):
        loads[name].wait()

    extra = attrs.shape[0] - feat
    attrs[feat:, :] = jnp.where(
        lax.broadcasted_iota(jnp.int32, (extra, reaches), 0) == 0, 1.0, 0.0
    ).astype(bf16)
    slot_row = lax.broadcasted_iota(jnp.int32, (LINKS * GROUP, 1), 0)
    slot = slot_row % GROUP
    cap = send_list.shape[2]
    spread = (
        slot == lax.broadcasted_iota(jnp.int32, (LINKS * GROUP, cap), 1)
    ).astype(f32)
    lane_reach = lax.broadcasted_iota(jnp.int32, (LINKS * GROUP, reaches), 1).astype(f32)
    lane_basin = lax.broadcasted_iota(jnp.int32, (LINKS * GROUP, n), 1)

    def one_hot_of(lists, sign):
        table = lax.dot_general(
            spread, lists[0].astype(f32), NT, precision=lax.Precision.HIGHEST,
            preferred_element_type=f32,
        )
        peer = jnp.zeros((LINKS * GROUP, 1), jnp.int32)
        for k, off in enumerate(offsets):
            peer = jnp.where(slot_row // GROUP == k, lax.rem(me + sign * off + n, n), peer)
        column = jnp.sum(jnp.where(lane_basin == peer, table, 0.0), axis=1, keepdims=True)
        column = jnp.where(slot < cap, column, float(reaches))
        return (jnp.abs(lane_reach - column) < 0.5).astype(bf16)


    take_send[...] = one_hot_of(send_list, 1)

    kind = section_class[...].reshape(1, reaches)
    conveyance = jnp.zeros((1, reaches), f32)
    for c in range(section_factor.shape[0]):
        conveyance = jnp.where(kind == c, section_factor[c], conveyance)
    k_base = jnp.sqrt(bed_slope[...].reshape(1, reaches)) * conveyance
    lane_group = lax.broadcasted_iota(jnp.int32, (8, 128), 1) // GROUP
    blocks = events // 8

    def message(index, k, sign):
        return pltpu.make_async_remote_copy(
            src_ref=out_msg.at[index, k],
            dst_ref=in_msg.at[index, k],
            send_sem=x_send.at[index, k],
            recv_sem=x_recv.at[index, k],
            device_id={"basin": lax.rem(me + sign * offsets[k] + n, n)},
            device_id_type=MESH,
        )

    def pick(field, matrix):
        both = lax.dot_general(split_two(field), matrix[...], NT, preferred_element_type=f32)
        return both[:events] + both[events:]

    def send(index, picked, sign):
        for k in range(LINKS):
            packed = jnp.zeros((8, 128), f32)
            for q in range(blocks):
                piece = picked[8 * q : 8 * q + 8]
                shift = ((q - k) * GROUP) % 128
                if shift:
                    piece = pltpu.roll(piece, shift, 1)
                packed = jnp.where(lane_group == q, piece, packed)
            out_msg[index, k] = packed
            message(index, k, sign).start()

    def receive(index, sign):
        for k in range(LINKS):
            message(index, k, sign).wait_recv()
        pieces = []
        for q in range(blocks):
            got = jnp.zeros((8, 128), f32)
            for k in range(LINKS):
                piece = in_msg[index, k]
                shift = ((k - q) * GROUP) % 128
                if shift:
                    piece = pltpu.roll(piece, shift, 1)
                got = jnp.where(lane_group == k, piece, got)
            pieces.append(got)
        return jnp.concatenate(pieces, axis=0)

    def scatter(got, matrix):
        both = jnp.dot(split_two(got), matrix[...], preferred_element_type=f32)
        return both[:events] + both[events:]

    def power(area):
        return jnp.exp((2.0 / 3.0) * jnp.log(area))


    areas = [area_start[...]]
    powers = [power(areas[0])]
    plain = areas[0] * powers[0]
    outer = pick(k_base * plain, take_send)
    inputs = lax.dot_general(attrs[0:feat, :], take_send[...], NT, preferred_element_type=f32)

    pl.semaphore_wait(barrier, n - 1 + n_event - 1)
    send(HALO, inputs, 1)
    send(0, outer, 1)

    for name in ("w_first", "b_first", "b_second", "w_out", "w_second"):
        loads[name].wait()

    w_firstT[...] = jnp.transpose(w_first[...])
    w_secondT[...] = jnp.transpose(w_second[...])
    w_out_row = w_out[...].astype(f32).reshape(1, hid)
    cols[...] = jnp.transpose(jnp.concatenate(
        [b_first[...].reshape(1, hid), b_second[...].reshape(1, hid), w_out_row,
         jnp.zeros((5, hid), f32)], axis=0
    ))
    w_out_rows = jnp.broadcast_to(w_out_row, (16, hid)).astype(bf16)

    def network(block):
        where = pl.ds(pl.multiple_of(block * width, 128), width)
        one = jnp.tanh(
            jnp.dot(w_firstT[...], attrs[0:feat, where], preferred_element_type=f32) + cols[:, 0:1]
        )
        t_one[:, where] = one
        hidden = one.astype(bf16)
        h_one[:, where] = hidden
        two = jnp.tanh(
            jnp.dot(w_secondT[...], hidden, preferred_element_type=f32) + cols[:, 1:2]
        )
        rounded = two.astype(bf16)
        h_two[:, where] = rounded
        factor = (cols[:, 2:3] * (1.0 - two * two)).astype(bf16)
        d_two[:, where] = factor
        first = t_one[mine, where]
        lower[:, where] = (
            jnp.dot(w_second[mine, :], factor, preferred_element_type=f32) * (1.0 - first * first)
        )
        return rounded

    logit = jnp.dot(w_out_rows, network(ev), preferred_element_type=f32)[0:1]
    squash_all[ev] = 1.0 / (1.0 + jnp.exp(-logit))

    def squash_copy(i):
        return pltpu.make_async_remote_copy(
            src_ref=squash_all.at[ev],
            dst_ref=squash_all.at[ev],
            send_sem=s_send.at[i],
            recv_sem=s_recv.at[i],
            device_id={"event": lax.rem(ev + 1 + i, n_event)},
            device_id_type=MESH,
        )

    for i in range(n_event - 1):
        squash_copy(i).start()

    for name in ("recv_list", "seg_count", "down_local", "lateral"):
        loads[name].wait()
    take_recv[...] = one_hot_of(recv_list, -1)
    beta = 1.0 / seg_count[...].reshape(1, reaches).astype(f32)
    down = down_local[...].reshape(1, reaches)
    hop = jnp.where(down < reaches, down - lax.broadcasted_iota(jnp.int32, (1, reaches), 1), 0)
    masks = [(hop == d).astype(f32) for d in range(1, 9)]


    def hidden_of(weight, x, column):
        return jnp.tanh(
            jnp.dot(weight[...], x, preferred_element_type=f32) + cols[:, column : column + 1]
        ).astype(bf16)

    around = receive(HALO, 1).astype(bf16)
    around = hidden_of(w_secondT, hidden_of(w_firstT, around, 0), 1)
    around = jnp.dot(w_out_rows, around, preferred_element_type=f32)[0:1]
    flow_in = receive(0, 1) / (0.02 + 0.08 * (1.0 / (1.0 + jnp.exp(-around))))
    flow_in = scatter(flow_in, take_recv)

    for i in range(n_event - 1):
        squash_copy(i).wait_recv()
    squash = jnp.concatenate([squash_all[e] for e in range(n_event)], axis=1)
    rough = 0.02 + 0.08 * squash
    rate = k_base / rough
    shrinks = []
    for t in range(STEPS):
        area, p = areas[t], powers[t]
        flow = rate * area * p
        if t > 0:
            send(t, pick(flow, take_send), 1)
        inflow = lateral[t]
        for d in range(1, 9):
            inflow = inflow + pltpu.roll(flow * masks[d - 1], d, 1)
        shrink = 1.0 / (1.0 + beta * rate * p)
        shrinks.append(shrink)
        if t > 0:
            if t < n_event:
                network(lax.rem(ev + t, n_event))
            flow_in = scatter(receive(t, 1), take_recv)
        inflow = inflow + flow_in
        areas.append((area + beta * inflow) * shrink)
        powers.append(power(areas[t + 1]))
    emitted = areas[STEPS] * powers[STEPS]
    outflow[...] = rate * emitted
    write_flow = pltpu.make_async_copy(outflow, outflow_h, out_sem.at[0])
    write_flow.start()
    loads["cotangent"].wait()
    g_area = cotangent[...] * rate * (5.0 / 3.0) * powers[STEPS]
    g_rate = cotangent[...] * emitted
    for t in reversed(range(STEPS)):
        index = 2 * STEPS - 1 - t
        inner = g_area * shrinks[t]
        g_inflow = inner * beta
        grad_lateral[t] = g_inflow
        send(index, pick(g_inflow, take_recv), -1)
        g_flow = jnp.zeros((events, reaches), f32)
        for d in range(1, 9):
            g_flow = g_flow + masks[d - 1] * pltpu.roll(g_inflow, reaches - d, 1)
        drop = g_inflow * areas[t + 1] * powers[t]
        g_rate = g_rate - drop
        g_area = inner - (2.0 / 3.0) * rate * drop / areas[t]
        if t == STEPS - 1:
            for block in range(STEPS, n_event):
                network(lax.rem(ev + block, n_event))
        g_flow = g_flow + scatter(receive(index, -1), take_send)
        g_rate = g_rate + g_flow * areas[t] * powers[t]
        g_area = g_area + (5.0 / 3.0) * rate * powers[t] * g_flow
    write_lateral = pltpu.make_async_copy(grad_lateral, grad_lateral_h, out_sem.at[1])
    write_lateral.start()
    rate_out[...] = jnp.sum(g_rate, axis=0, keepdims=True)

    def rate_copy(i):
        return pltpu.make_async_remote_copy(
            src_ref=rate_out,
            dst_ref=rate_in.at[i],
            send_sem=r_send.at[i],
            recv_sem=r_recv.at[i],
            device_id={"event": lax.rem(ev + 1 + i, n_event)},
            device_id_type=MESH,
        )

    for i in range(n_event - 1):
        rate_copy(i).start()
    for i in range(n_event - 1):
        rate_copy(i).wait_recv()
    terms = [rate_out[...]] + [rate_in[i] for i in range(n_event - 1)]
    g_sum = jnp.zeros((1, reaches), f32)
    for e in range(n_event):
        term = terms[0]
        for i in range(n_event - 1):
            term = jnp.where(lax.rem(e + 1 + i, n_event) == ev, terms[i + 1], term)
        g_sum = g_sum + term
    g_logit = (
        g_sum * (-rate / rough) * (scale * 0.08) * squash * (1.0 - squash)
    ).astype(bf16)
    g_logit32 = g_logit.astype(f32)

    scaled = (h_one[mine, :].astype(f32) * g_logit32).astype(bf16)
    large = lax.dot_general(scaled, d_two[...], NT, preferred_element_type=f32)
    tiles = hid // 128
    for d in range(owners):
        for r in range(chunk // 8):
            for c in range(tiles):
                top = d * chunk + 8 * r
                slab[d, r * tiles + c] = large[top : top + 8, 128 * c : 128 * c + 128]

    g_pre = (lower[...] * g_logit32).astype(bf16)
    place = lax.broadcasted_iota(jnp.int32, (PLACES, reaches), 0)
    row_two = jnp.where(place == feat + 1, g_logit32, 0.0).astype(bf16)
    row_out = jnp.where(place == feat + 2, g_logit32, 0.0).astype(bf16)
    g_two = d_two[mine, :]
    second = h_two[mine, :]

    def narrow(low):
        high = low + 128
        return (
            lax.dot_general(attrs[...], g_pre[low:high], NT, preferred_element_type=f32)
            + lax.dot_general(row_two, g_two[low:high], NT, preferred_element_type=f32)
            + lax.dot_general(row_out, second[low:high], NT, preferred_element_type=f32)
        )

    left = narrow(0)
    right = narrow(part - 128)
    first_half = lax.broadcasted_iota(jnp.int32, (8, 128), 1) < 64
    last = slab.shape[1] - 1
    for k in range(5):
        slab[k, last] = left[8 * k : 8 * k + 8]
    for k in range(3):
        even = pltpu.roll(right[16 * k : 16 * k + 8], 64, 1)
        slab[5 + k, last] = jnp.where(first_half, even, right[16 * k + 8 : 16 * k + 16])
    for d in range(8, owners):
        slab[d, last] = jnp.zeros((8, 128), f32)

    def when_owner(index, work):
        if owners == n:
            work()
        else:
            pl.when(index < owners)(work)

    line = n // 2
    low = lax.rem(me, 2)
    spot = me // 2
    pair = me + 1 - 2 * low
    half = lax.rem(ev + n_event // 2, n_event)
    twin = ev + 1 - 2 * lax.rem(ev, 2)
    twin_half = lax.rem(twin + n_event // 2, n_event)
    span = slab.shape[1]
    cut = (span + 1) // 2

    def each(first, last, work):
        if last - first <= 4:
            for j in range(first, last):
                work(j)
        else:
            pl.loop(first, last)(work)

    def near(j):
        if line != 4:
            return lax.rem(spot + j, line)
        if isinstance(j, int) and j == 0:
            return spot
        orders = ((1, 2, 3), (2, 0, 3), (1, 3, 0), (2, 1, 0))
        code = sum(orders[s][j - 1] * 4 ** s for s in range(4))
        power_of = (1 + 3 * lax.rem(spot, 2)) * (1 + 15 * (spot // 2))
        return lax.rem(code // power_of, 4)

    def device(z, parity):
        return 2 * z + parity

    def pair_sum(z, parity):
        return pltpu.make_async_remote_copy(
            src_ref=slab.at[device(z, parity)], dst_ref=rs_pair.at[z],
            send_sem=px_send.at[z], recv_sem=px_recv.at[z],
            device_id={"basin": pair}, device_id_type=MESH,
        )

    def line_sum(z, sender):
        return pltpu.make_async_remote_copy(
            src_ref=rs_pair.at[z], dst_ref=rs_line.at[sender],
            send_sem=pz_send.at[z], recv_sem=pz_recv.at[sender],
            device_id={"basin": device(z, low)}, device_id_type=MESH,
        )

    def far(j):
        return near(line - 1 - j)

    def start_pair(j):
        z = far(j)
        when_owner(device(z, 1 - low), lambda: pair_sum(z, 1 - low).start())

    each(0, line, start_pair)

    for i in range(n_event - 1):
        squash_copy(i).wait_send()
    for index in range(HALO + 1):
        for k in range(LINKS):
            message(index, k, 1).wait_send()
    for i in range(n_event - 1):
        rate_copy(i).wait_send()
    write_flow.wait()
    write_lateral.wait()

    def add_pair(j):
        z = far(j)

        def go():
            pair_sum(z, 1 - low).wait_recv()
            rs_pair[z] = rs_pair[z] + slab[device(z, low)]

            @pl.when(z != spot)
            def _():
                line_sum(z, spot).start()

        when_owner(device(z, low), go)

    each(0, line, add_pair)

    whole = pl.ds(0, span)
    upper = pl.ds(0, cut)
    under = pl.ds(cut, span - cut)

    def move(event, at, rows, sems, slot, target):
        ref = full.at[event, at, rows]
        return pltpu.make_async_remote_copy(
            src_ref=ref, dst_ref=ref, send_sem=sems[0].at[slot], recv_sem=sems[1].at[slot],
            device_id=target, device_id_type=MESH,
        )

    def to_line(source, peer):
        ref = full.at[ev, device(source, low)]
        return pltpu.make_async_remote_copy(
            src_ref=ref, dst_ref=ref, send_sem=az_send.at[peer], recv_sem=az_recv.at[source],
            device_id={"basin": device(peer, low)}, device_id_type=MESH,
        )

    def to_pair(z, parity):
        return move(ev, device(z, parity), whole, (ax_send, ax_recv), z, {"basin": pair})

    def to_half(event, z):
        return move(event, device(z, low), whole, (ay_send, ay_recv), z, {"event": half})

    def on_half(event, z):
        return move(event, device(z, 1 - low), upper, (fa_send, fa_recv), z, {"event": half})

    def on_pair(z, parity):
        return move(half, device(z, parity), under, (fb_send, fb_recv), z, {"basin": pair})

    def to_twin(side, event, z):
        ref = full.at[event, pl.ds(2 * z, 2)]
        return pltpu.make_async_remote_copy(
            src_ref=ref, dst_ref=ref, send_sem=tw_send.at[side, z], recv_sem=tw_recv.at[side, z],
            device_id={"event": twin}, device_id_type=MESH,
        )

    def own():
        def add(i, total):
            sender = lax.rem(spot + line - i, line)
            line_sum(spot, sender).wait_recv()
            return total + rs_line[sender]

        full[ev, me] = lax.fori_loop(1, line, add, rs_pair[spot])
        each(1, line, lambda j: to_line(spot, near(j)).start())
        to_pair(spot, low).start()
        to_half(ev, spot).start()

    when_owner(me, own)

    def from_line(j):
        z = near(j)

        def go():
            to_line(z, spot).wait_recv()
            to_pair(z, low).start()
            to_half(ev, z).start()

        when_owner(device(z, low), go)

    def second_hop(j):
        z = near(j)

        def go():
            to_pair(z, 1 - low).wait_recv()
            on_half(ev, z).start()
            to_twin(0, ev, z).start()
            to_half(half, z).wait_recv()
            on_pair(z, low).start()

        when_owner(2 * z, go)

    def corner(j):
        z = near(j)

        def go():
            on_half(half, z).wait_recv()
            on_pair(z, 1 - low).wait_recv()
            to_twin(1, half, z).start()

        when_owner(2 * z, go)

    if line <= 4:
        for j in range(1, line):
            from_line(j)
            second_hop(j - 1)
            if j >= 2:
                corner(j - 2)
        second_hop(line - 1)
        corner(line - 2)
        corner(line - 1)
    else:
        pl.loop(1, line)(from_line)
        pl.loop(0, line)(second_hop)
        pl.loop(0, line)(corner)

    def drain(z):
        when_owner(device(z, 1 - low), lambda: pair_sum(z, 1 - low).wait_send())

        @pl.when(z != spot)
        def _():
            when_owner(device(z, low), lambda: line_sum(z, spot).wait_send())
            when_owner(me, lambda: to_line(spot, z).wait_send())

        def go():
            to_pair(z, low).wait_send()
            to_half(ev, z).wait_send()
            on_half(ev, z).wait_send()
            on_pair(z, low).wait_send()
            to_twin(0, ev, z).wait_send()
            to_twin(1, half, z).wait_send()

        when_owner(2 * z, go)

    each(0, line, drain)

    def write_full(z):
        where = pl.ds(2 * z, 2)
        return pltpu.make_async_copy(full.at[:, where], full_h.at[:, where], write_sem.at[z])

    def arrive(j):
        z = near(j)

        def go():
            to_twin(0, twin, z).wait_recv()
            to_twin(1, twin_half, z).wait_recv()
            write_full(z).start()

        when_owner(2 * z, go)

    each(0, line, arrive)
    each(0, line, lambda j: when_owner(2 * near(j), lambda: write_full(near(j)).wait()))


def finish(
    feat, full_in, flow_in, lateral_in,
    large, flow_out, lateral_out, w_first, b_first, b_second, w_out,
    full, flow, lateral, sems,
):
    last = full.shape[2] - 1
    middle = full.shape[0] // 2
    steps = []
    for side in range(2):
        where = pl.ds(side * middle, middle)
        steps.append((full_in.at[where], full.at[where], full.at[where, :, pl.ds(0, last)], large.at[where]))
    steps.append((lateral_in, lateral, lateral, lateral_out))
    steps.append((flow_in, flow, flow, flow_out))
    reads = [pltpu.make_async_copy(x[0], x[1], sems.at[0, i]) for i, x in enumerate(steps)]
    copies = [pltpu.make_async_copy(x[2], x[3], sems.at[1, i]) for i, x in enumerate(steps)]
    for read in reads:
        read.start()
    for read, copy in zip(reads, copies):
        read.wait()
        copy.start()
    n_event = full.shape[0]
    first_half = lax.broadcasted_iota(jnp.int32, (8, 128), 1) < 64
    for k in range(5):
        columns = []
        for e in range(0, n_event, 2):
            tails = []
            for s in range(2):
                tail = full[e + s, 5 + k // 2, last]
                tails.append(pltpu.roll(tail, 64, 1) if k % 2 != s else tail)
            turned = pltpu.roll(full[e + 1, k, last], 64, 1)
            columns += [
                full[e, k, last],
                jnp.where(first_half, tails[0], turned),
                jnp.where(first_half, turned, tails[1]),
            ]
        rows = jnp.concatenate(columns, axis=1)
        if k < 4:
            w_first[8 * k : 8 * k + 8, :] = rows
        else:
            b_first[...] = rows[0:1].reshape(rows.shape[1])
            b_second[...] = rows[1:2].reshape(rows.shape[1])
            w_out[...] = rows[2:3].reshape(rows.shape[1])
    for copy in copies:
        copy.wait()


def body(
    n,
    n_event,
    reach_attrs,
    w_first,
    b_first,
    w_second,
    b_second,
    w_out,
    section_factor,
    bed_slope,
    seg_count,
    section_class,
    down_local,
    send_list,
    recv_list,
    area_start,
    lateral,
    cotangent,
):
    f32, bf16 = jnp.float32, jnp.bfloat16
    events, reaches = area_start.shape
    feat, hid = w_first.shape
    part = hid // n_event
    owners = n if part % (8 * n) == 0 else part // 8
    chunk = part // owners
    span = (chunk // 8) * (hid // 128) + 1
    line = n // 2
    scale = 32.0 / math.sqrt(events * n_event * reaches * n)
    vmem = pl.BlockSpec(memory_space=pltpu.VMEM)
    hbm = pl.BlockSpec(memory_space=pltpu.HBM)
    smem = pl.BlockSpec(memory_space=pltpu.SMEM)
    dma = pltpu.SemaphoreType.DMA
    held = lambda x: pltpu.VMEM(x.shape, x.dtype)
    outflow, grad_lateral, full = pl.pallas_call(
        functools.partial(kernel, n, n_event, owners, chunk, scale),
        out_shape=(
            jax.ShapeDtypeStruct((events, reaches), f32),
            jax.ShapeDtypeStruct((STEPS, events, reaches), f32),
            jax.ShapeDtypeStruct((n_event, owners, span, 8, 128), f32),
        ),
        in_specs=[hbm] * 6 + [smem] + [hbm] * 9,
        out_specs=(hbm,) * 3,
        scratch_shapes=[
            pltpu.VMEM((events, reaches), f32),
            pltpu.VMEM((STEPS, events, reaches), f32),
            pltpu.VMEM((n_event, owners, span, 8, 128), f32),
            dma((2,)),
            pltpu.VMEM((PLACES, reaches), bf16),
            held(w_first), held(b_first), held(w_second), held(b_second), held(w_out),
            held(bed_slope), held(seg_count), held(section_class), held(down_local),
            held(send_list), held(recv_list), held(area_start), held(lateral), held(cotangent),
            dma((15,)),
            pltpu.VMEM((hid, feat), bf16),
            pltpu.VMEM((hid, hid), bf16),
            pltpu.VMEM((hid, 8), f32),
            pltpu.VMEM((hid, reaches), f32),
            pltpu.VMEM((hid, reaches), bf16),
            pltpu.VMEM((hid, reaches), bf16),
            pltpu.VMEM((hid, reaches), bf16),
            pltpu.VMEM((part, reaches), f32),
            pltpu.VMEM((n_event, 1, reaches // n_event), f32),
            pltpu.VMEM((LINKS * GROUP, reaches), bf16),
            pltpu.VMEM((LINKS * GROUP, reaches), bf16),
            pltpu.VMEM((HALO + 1, LINKS, 8, 128), f32),
            pltpu.VMEM((HALO + 1, LINKS, 8, 128), f32),
            pltpu.VMEM((1, reaches), f32),
            pltpu.VMEM((n_event - 1, 1, reaches), f32),
            pltpu.VMEM((owners, span, 8, 128), f32),
            pltpu.VMEM((line, span, 8, 128), f32),
            pltpu.VMEM((line, span, 8, 128), f32),
            dma((n_event - 1,)), dma((n_event - 1,)),
            dma((HALO + 1, LINKS)), dma((HALO + 1, LINKS)),
            dma((n_event - 1,)), dma((n_event - 1,)),
            dma((line,)), dma((line,)), dma((line,)), dma((line,)),
            dma((line,)), dma((line,)), dma((line,)), dma((line,)), dma((line,)), dma((line,)),
            dma((line,)), dma((line,)), dma((line,)), dma((line,)), dma((2, line)), dma((2, line)), dma((line,)),
        ],
        compiler_params=pltpu.CompilerParams(
            collective_id=0, has_side_effects=True, vmem_limit_bytes=63 * 1024 * 1024
        ),
    )(
        reach_attrs.T, w_first, b_first, w_second, b_second, w_out, section_factor,
        bed_slope, seg_count, section_class, down_local, send_list, recv_list,
        area_start, lateral, cotangent,
    )
    vector = jax.ShapeDtypeStruct((hid,), f32)
    large, outflow, grad_lateral, g_first, g_b_first, g_b_second, g_out = pl.pallas_call(
        functools.partial(finish, feat),
        out_shape=(
            jax.ShapeDtypeStruct((n_event, owners, span - 1, 8, 128), f32),
            jax.ShapeDtypeStruct((events, reaches), f32),
            jax.ShapeDtypeStruct((STEPS, events, reaches), f32),
            jax.ShapeDtypeStruct((feat, hid), f32),
            vector,
            vector,
            vector,
        ),
        in_specs=[hbm] * 3,
        out_specs=(hbm, hbm, hbm, vmem, vmem, vmem, vmem),
        scratch_shapes=[held(full), held(outflow), held(grad_lateral), dma((2, 4))],
    )(full, outflow, grad_lateral)
    g_second = large.reshape(hid // 8, hid // 128, 8, 128).transpose(0, 2, 1, 3).reshape(hid, hid)
    return outflow, grad_lateral, g_first, g_b_first, g_second, g_b_second, g_out


def solution(mesh):
    return jax.shard_map(
        functools.partial(body, mesh.shape["basin"], mesh.shape["event"]),
        mesh=mesh,
        in_specs=(
            P("basin", None),
            P(),
            P(),
            P(),
            P(),
            P(),
            P(),
            P("basin"),
            P("basin"),
            P("basin"),
            P("basin"),
            P("basin", None, None),
            P("basin", None, None),
            P("event", "basin"),
            P(None, "event", "basin"),
            P("event", "basin"),
        ),
        out_specs=(P("event", "basin"), P(None, "event", "basin"), P(), P(), P(), P(), P()),
        check_vma=False,
    )
```

```python
import functools
import math

import jax
import jax.numpy as jnp
from jax import lax
from jax.experimental import pallas as pl
from jax.experimental.pallas import tpu as pltpu
from jax.sharding import PartitionSpec as P

STEPS = 3
HALO = 2 * STEPS
LINKS = 4
GROUP = 32
PLACES = 48
MESH = pl.DeviceIdType.MESH
NT = (((1,), (1,)), ((), ()))


def split_two(x):
    high = x.astype(jnp.bfloat16)
    low = (x - high.astype(jnp.float32)).astype(jnp.bfloat16)
    return jnp.concatenate([high, low], axis=0)


def kernel(
    n, n_event, owners, chunk, scale,
    attrs_h, w_first_h, b_first_h, w_second_h, b_second_h, w_out_h, section_factor,
    bed_slope_h, seg_count_h, section_class_h, down_local_h, send_list_h, recv_list_h,
    area_start_h, lateral_h, cotangent_h,
    outflow_h, grad_lateral_h, full_h,
    outflow, grad_lateral, full, out_sem,
    attrs, w_first, b_first, w_second, b_second, w_out,
    bed_slope, seg_count, section_class, down_local, send_list, recv_list,
    area_start, lateral, cotangent, load_sem,
    w_firstT, w_secondT, cols,
    t_one, h_one, d_two, h_two, lower, squash_all, take_send, take_recv,
    out_msg, in_msg, rate_out, rate_in, slab, rs_pair, rs_line,
    s_send, s_recv,
    x_send, x_recv, r_send, r_recv, px_send, px_recv, pz_send, pz_recv,
    az_send, az_recv, ax_send, ax_recv, ay_send, ay_recv,
    fa_send, fa_recv, fb_send, fb_recv, tw_send, tw_recv, write_sem,
):
    f32, bf16 = jnp.float32, jnp.bfloat16
    me = lax.axis_index("basin")
    ev = lax.axis_index("event")
    events, reaches = area_start.shape
    hid = w_second.shape[0]
    feat = w_first.shape[0]
    part = hid // n_event
    offsets = (1, 2, n // 2, n - 1)
    base = pl.multiple_of(ev * part, 64)
    mine = pl.ds(base, part)
    width = reaches // n_event

    loads = {}
    for name, source, target in (
        ("w_first", w_first_h, w_first),
        ("attrs", attrs_h, attrs.at[pl.ds(0, feat)]),
        ("b_first", b_first_h, b_first),
        ("b_second", b_second_h, b_second),
        ("w_out", w_out_h, w_out),
        ("w_second", w_second_h, w_second),
        ("send_list", send_list_h, send_list),
        ("recv_list", recv_list_h, recv_list),
        ("bed_slope", bed_slope_h, bed_slope),
        ("section_class", section_class_h, section_class),
        ("seg_count", seg_count_h, seg_count),
        ("down_local", down_local_h, down_local),
        ("area_start", area_start_h, area_start),
        ("lateral", lateral_h, lateral),
        ("cotangent", cotangent_h, cotangent),
    ):
        loads[name] = pltpu.make_async_copy(source, target, load_sem.at[len(loads)])
        loads[name].start()

    barrier = pltpu.get_barrier_semaphore()

    @pl.loop(1, n)
    def _(i):
        pl.semaphore_signal(barrier, inc=1, device_id={"basin": lax.rem(me + i, n)}, device_id_type=MESH)

    for i in range(1, n_event):
        pl.semaphore_signal(
            barrier, inc=1, device_id={"event": lax.rem(ev + i, n_event)}, device_id_type=MESH
        )

    for name in ("send_list", "attrs", "area_start", "bed_slope", "section_class"):
        loads[name].wait()

    extra = attrs.shape[0] - feat
    attrs[feat:, :] = jnp.where(
        lax.broadcasted_iota(jnp.int32, (extra, reaches), 0) == 0, 1.0, 0.0
    ).astype(bf16)
    slot_row = lax.broadcasted_iota(jnp.int32, (LINKS * GROUP, 1), 0)
    slot = slot_row % GROUP
    cap = send_list.shape[2]
    spread = (
        slot == lax.broadcasted_iota(jnp.int32, (LINKS * GROUP, cap), 1)
    ).astype(f32)
    lane_reach = lax.broadcasted_iota(jnp.int32, (LINKS * GROUP, reaches), 1).astype(f32)
    lane_basin = lax.broadcasted_iota(jnp.int32, (LINKS * GROUP, n), 1)

    def one_hot_of(lists, sign):
        table = lax.dot_general(
            spread, lists[0].astype(f32), NT, precision=lax.Precision.HIGHEST,
            preferred_element_type=f32,
        )
        peer = jnp.zeros((LINKS * GROUP, 1), jnp.int32)
        for k, off in enumerate(offsets):
            peer = jnp.where(slot_row // GROUP == k, lax.rem(me + sign * off + n, n), peer)
        column = jnp.sum(jnp.where(lane_basin == peer, table, 0.0), axis=1, keepdims=True)
        column = jnp.where(slot < cap, column, float(reaches))
        return (jnp.abs(lane_reach - column) < 0.5).astype(bf16)


    take_send[...] = one_hot_of(send_list, 1)

    kind = section_class[...].reshape(1, reaches)
    conveyance = jnp.zeros((1, reaches), f32)
    for c in range(section_factor.shape[0]):
        conveyance = jnp.where(kind == c, section_factor[c], conveyance)
    k_base = jnp.sqrt(bed_slope[...].reshape(1, reaches)) * conveyance
    lane_group = lax.broadcasted_iota(jnp.int32, (8, 128), 1) // GROUP
    blocks = events // 8

    def message(index, k, sign):
        return pltpu.make_async_remote_copy(
            src_ref=out_msg.at[index, k],
            dst_ref=in_msg.at[index, k],
            send_sem=x_send.at[index, k],
            recv_sem=x_recv.at[index, k],
            device_id={"basin": lax.rem(me + sign * offsets[k] + n, n)},
            device_id_type=MESH,
        )

    def pick(field, matrix):
        both = lax.dot_general(split_two(field), matrix[...], NT, preferred_element_type=f32)
        return both[:events] + both[events:]

    def send(index, picked, sign):
        for k in range(LINKS):
            packed = jnp.zeros((8, 128), f32)
            for q in range(blocks):
                piece = picked[8 * q : 8 * q + 8]
                shift = ((q - k) * GROUP) % 128
                if shift:
                    piece = pltpu.roll(piece, shift, 1)
                packed = jnp.where(lane_group == q, piece, packed)
            out_msg[index, k] = packed
            message(index, k, sign).start()

    def receive(index, sign):
        for k in range(LINKS):
            message(index, k, sign).wait_recv()
        pieces = []
        for q in range(blocks):
            got = jnp.zeros((8, 128), f32)
            for k in range(LINKS):
                piece = in_msg[index, k]
                shift = ((k - q) * GROUP) % 128
                if shift:
                    piece = pltpu.roll(piece, shift, 1)
                got = jnp.where(lane_group == k, piece, got)
            pieces.append(got)
        return jnp.concatenate(pieces, axis=0)

    def scatter(got, matrix):
        both = jnp.dot(split_two(got), matrix[...], preferred_element_type=f32)
        return both[:events] + both[events:]

    def power(area):
        return jnp.exp((2.0 / 3.0) * jnp.log(area))


    areas = [area_start[...]]
    powers = [power(areas[0])]
    plain = areas[0] * powers[0]
    outer = pick(k_base * plain, take_send)
    inputs = lax.dot_general(attrs[0:feat, :], take_send[...], NT, preferred_element_type=f32)

    pl.semaphore_wait(barrier, n - 1 + n_event - 1)
    send(HALO, inputs, 1)
    send(0, outer, 1)

    for name in ("w_first", "b_first", "b_second", "w_out", "w_second"):
        loads[name].wait()

    w_firstT[...] = jnp.transpose(w_first[...])
    w_secondT[...] = jnp.transpose(w_second[...])
    w_out_row = w_out[...].astype(f32).reshape(1, hid)
    cols[...] = jnp.transpose(jnp.concatenate(
        [b_first[...].reshape(1, hid), b_second[...].reshape(1, hid), w_out_row,
         jnp.zeros((5, hid), f32)], axis=0
    ))
    w_out_rows = jnp.broadcast_to(w_out_row, (16, hid)).astype(bf16)

    def network(block):
        where = pl.ds(pl.multiple_of(block * width, 128), width)
        one = jnp.tanh(
            jnp.dot(w_firstT[...], attrs[0:feat, where], preferred_element_type=f32) + cols[:, 0:1]
        )
        t_one[:, where] = one
        hidden = one.astype(bf16)
        h_one[:, where] = hidden
        two = jnp.tanh(
            jnp.dot(w_secondT[...], hidden, preferred_element_type=f32) + cols[:, 1:2]
        )
        rounded = two.astype(bf16)
        h_two[:, where] = rounded
        factor = (cols[:, 2:3] * (1.0 - two * two)).astype(bf16)
        d_two[:, where] = factor
        first = t_one[mine, where]
        lower[:, where] = (
            jnp.dot(w_second[mine, :], factor, preferred_element_type=f32) * (1.0 - first * first)
        )
        return rounded

    logit = jnp.dot(w_out_rows, network(ev), preferred_element_type=f32)[0:1]
    squash_all[ev] = 1.0 / (1.0 + jnp.exp(-logit))

    def squash_copy(i):
        return pltpu.make_async_remote_copy(
            src_ref=squash_all.at[ev],
            dst_ref=squash_all.at[ev],
            send_sem=s_send.at[i],
            recv_sem=s_recv.at[i],
            device_id={"event": lax.rem(ev + 1 + i, n_event)},
            device_id_type=MESH,
        )

    for i in range(n_event - 1):
        squash_copy(i).start()

    for name in ("recv_list", "seg_count", "down_local", "lateral"):
        loads[name].wait()
    take_recv[...] = one_hot_of(recv_list, -1)
    beta = 1.0 / seg_count[...].reshape(1, reaches).astype(f32)
    down = down_local[...].reshape(1, reaches)
    hop = jnp.where(down < reaches, down - lax.broadcasted_iota(jnp.int32, (1, reaches), 1), 0)
    masks = [(hop == d).astype(f32) for d in range(1, 9)]


    def hidden_of(weight, x, column):
        return jnp.tanh(
            jnp.dot(weight[...], x, preferred_element_type=f32) + cols[:, column : column + 1]
        ).astype(bf16)

    around = receive(HALO, 1).astype(bf16)
    around = hidden_of(w_secondT, hidden_of(w_firstT, around, 0), 1)
    around = jnp.dot(w_out_rows, around, preferred_element_type=f32)[0:1]
    flow_in = receive(0, 1) / (0.02 + 0.08 * (1.0 / (1.0 + jnp.exp(-around))))
    flow_in = scatter(flow_in, take_recv)

    for i in range(n_event - 1):
        squash_copy(i).wait_recv()
    squash = jnp.concatenate([squash_all[e] for e in range(n_event)], axis=1)
    rough = 0.02 + 0.08 * squash
    rate = k_base / rough
    shrinks = []
    for t in range(STEPS):
        area, p = areas[t], powers[t]
        flow = rate * area * p
        if t > 0:
            send(t, pick(flow, take_send), 1)
        inflow = lateral[t]
        for d in range(1, 9):
            inflow = inflow + pltpu.roll(flow * masks[d - 1], d, 1)
        shrink = 1.0 / (1.0 + beta * rate * p)
        shrinks.append(shrink)
        if t > 0:
            if t < n_event:
                network(lax.rem(ev + t, n_event))
            flow_in = scatter(receive(t, 1), take_recv)
        inflow = inflow + flow_in
        areas.append((area + beta * inflow) * shrink)
        powers.append(power(areas[t + 1]))
    emitted = areas[STEPS] * powers[STEPS]
    outflow[...] = rate * emitted
    write_flow = pltpu.make_async_copy(outflow, outflow_h, out_sem.at[0])
    write_flow.start()
    loads["cotangent"].wait()
    g_area = cotangent[...] * rate * (5.0 / 3.0) * powers[STEPS]
    g_rate = cotangent[...] * emitted
    for t in reversed(range(STEPS)):
        index = 2 * STEPS - 1 - t
        inner = g_area * shrinks[t]
        g_inflow = inner * beta
        grad_lateral[t] = g_inflow
        send(index, pick(g_inflow, take_recv), -1)
        g_flow = jnp.zeros((events, reaches), f32)
        for d in range(1, 9):
            g_flow = g_flow + masks[d - 1] * pltpu.roll(g_inflow, reaches - d, 1)
        drop = g_inflow * areas[t + 1] * powers[t]
        g_rate = g_rate - drop
        g_area = inner - (2.0 / 3.0) * rate * drop / areas[t]
        if t == STEPS - 1:
            for block in range(STEPS, n_event):
                network(lax.rem(ev + block, n_event))
        g_flow = g_flow + scatter(receive(index, -1), take_send)
        g_rate = g_rate + g_flow * areas[t] * powers[t]
        g_area = g_area + (5.0 / 3.0) * rate * powers[t] * g_flow
    write_lateral = pltpu.make_async_copy(grad_lateral, grad_lateral_h, out_sem.at[1])
    write_lateral.start()
    rate_out[...] = jnp.sum(g_rate, axis=0, keepdims=True)

    def rate_copy(i):
        return pltpu.make_async_remote_copy(
            src_ref=rate_out,
            dst_ref=rate_in.at[i],
            send_sem=r_send.at[i],
            recv_sem=r_recv.at[i],
            device_id={"event": lax.rem(ev + 1 + i, n_event)},
            device_id_type=MESH,
        )

    for i in range(n_event - 1):
        rate_copy(i).start()
    for i in range(n_event - 1):
        rate_copy(i).wait_recv()
    terms = [rate_out[...]] + [rate_in[i] for i in range(n_event - 1)]
    g_sum = jnp.zeros((1, reaches), f32)
    for e in range(n_event):
        term = terms[0]
        for i in range(n_event - 1):
            term = jnp.where(lax.rem(e + 1 + i, n_event) == ev, terms[i + 1], term)
        g_sum = g_sum + term
    g_logit = (
        g_sum * (-rate / rough) * (scale * 0.08) * squash * (1.0 - squash)
    ).astype(bf16)
    g_logit32 = g_logit.astype(f32)

    scaled = (h_one[mine, :].astype(f32) * g_logit32).astype(bf16)
    large = lax.dot_general(scaled, d_two[...], NT, preferred_element_type=f32)
    tiles = hid // 128
    for d in range(owners):
        for r in range(chunk // 8):
            for c in range(tiles):
                top = d * chunk + 8 * r
                slab[d, r * tiles + c] = large[top : top + 8, 128 * c : 128 * c + 128]

    g_pre = (lower[...] * g_logit32).astype(bf16)
    place = lax.broadcasted_iota(jnp.int32, (PLACES, reaches), 0)
    row_two = jnp.where(place == feat + 1, g_logit32, 0.0).astype(bf16)
    row_out = jnp.where(place == feat + 2, g_logit32, 0.0).astype(bf16)
    g_two = d_two[mine, :]
    second = h_two[mine, :]

    def narrow(low):
        high = low + 128
        return (
            lax.dot_general(attrs[...], g_pre[low:high], NT, preferred_element_type=f32)
            + lax.dot_general(row_two, g_two[low:high], NT, preferred_element_type=f32)
            + lax.dot_general(row_out, second[low:high], NT, preferred_element_type=f32)
        )

    left = narrow(0)
    right = narrow(part - 128)
    first_half = lax.broadcasted_iota(jnp.int32, (8, 128), 1) < 64
    last = slab.shape[1] - 1
    for k in range(5):
        slab[k, last] = left[8 * k : 8 * k + 8]
    for k in range(3):
        even = pltpu.roll(right[16 * k : 16 * k + 8], 64, 1)
        slab[5 + k, last] = jnp.where(first_half, even, right[16 * k + 8 : 16 * k + 16])
    for d in range(8, owners):
        slab[d, last] = jnp.zeros((8, 128), f32)

    def when_owner(index, work):
        if owners == n:
            work()
        else:
            pl.when(index < owners)(work)

    line = n // 2
    low = lax.rem(me, 2)
    spot = me // 2
    pair = me + 1 - 2 * low
    half = lax.rem(ev + n_event // 2, n_event)
    twin = ev + 1 - 2 * lax.rem(ev, 2)
    twin_half = lax.rem(twin + n_event // 2, n_event)
    span = slab.shape[1]
    cut = (span + 1) // 2
    halves = (pl.ds(0, cut), pl.ds(cut, span - cut))

    def each(first, last, work):
        if last - first <= 4:
            for j in range(first, last):
                work(j)
        else:
            pl.loop(first, last)(work)

    def near(j):
        if line != 4:
            return lax.rem(spot + j, line)
        if isinstance(j, int) and j == 0:
            return spot
        orders = ((1, 2, 3), (2, 0, 3), (1, 3, 0), (2, 1, 0))
        code = sum(orders[s][j - 1] * 4 ** s for s in range(4))
        power_of = (1 + 3 * lax.rem(spot, 2)) * (1 + 15 * (spot // 2))
        return lax.rem(code // power_of, 4)

    def device(z, parity):
        return 2 * z + parity

    def pair_sum(h, z, parity):
        return pltpu.make_async_remote_copy(
            src_ref=slab.at[device(z, parity), halves[h]], dst_ref=rs_pair.at[z, halves[h]],
            send_sem=px_send.at[h, z], recv_sem=px_recv.at[h, z],
            device_id={"basin": pair}, device_id_type=MESH,
        )

    def line_sum(h, z, sender):
        return pltpu.make_async_remote_copy(
            src_ref=rs_pair.at[z, halves[h]], dst_ref=rs_line.at[sender, halves[h]],
            send_sem=pz_send.at[h, z], recv_sem=pz_recv.at[h, sender],
            device_id={"basin": device(z, low)}, device_id_type=MESH,
        )

    def far(j):
        return near(line - 1 - j)

    def start_pair(h, j):
        z = far(j)
        when_owner(device(z, 1 - low), lambda: pair_sum(h, z, 1 - low).start())

    for h in range(2):
        each(0, line, functools.partial(start_pair, h))

    for i in range(n_event - 1):
        squash_copy(i).wait_send()
    for index in range(HALO + 1):
        for k in range(LINKS):
            message(index, k, 1).wait_send()
    for i in range(n_event - 1):
        rate_copy(i).wait_send()
    write_flow.wait()
    write_lateral.wait()

    def add_pair(h, j):
        z = far(j)

        def go():
            pair_sum(h, z, 1 - low).wait_recv()
            rs_pair[z, halves[h]] = rs_pair[z, halves[h]] + slab[device(z, low), halves[h]]

            @pl.when(z != spot)
            def _():
                line_sum(h, z, spot).start()

        when_owner(device(z, low), go)

    def move(event, at, h, sems, slot, target):
        ref = full.at[event, at, halves[h]]
        return pltpu.make_async_remote_copy(
            src_ref=ref, dst_ref=ref, send_sem=sems[0].at[slot], recv_sem=sems[1].at[slot],
            device_id=target, device_id_type=MESH,
        )

    def to_line(h, source, peer):
        ref = full.at[ev, device(source, low), halves[h]]
        return pltpu.make_async_remote_copy(
            src_ref=ref, dst_ref=ref, send_sem=az_send.at[h, peer], recv_sem=az_recv.at[h, source],
            device_id={"basin": device(peer, low)}, device_id_type=MESH,
        )

    def to_pair(h, z, parity):
        return move(ev, device(z, parity), h, (ax_send.at[h], ax_recv.at[h]), z, {"basin": pair})

    def to_half(h, event, z):
        return move(event, device(z, low), h, (ay_send.at[h], ay_recv.at[h]), z, {"event": half})

    def on_half(event, z):
        return move(event, device(z, 1 - low), 0, (fa_send, fa_recv), z, {"event": half})

    def on_pair(z, parity):
        return move(half, device(z, parity), 1, (fb_send, fb_recv), z, {"basin": pair})

    def to_twin(side, event, z):
        ref = full.at[event, pl.ds(2 * z, 2)]
        return pltpu.make_async_remote_copy(
            src_ref=ref, dst_ref=ref, send_sem=tw_send.at[side, z], recv_sem=tw_recv.at[side, z],
            device_id={"event": twin}, device_id_type=MESH,
        )

    def own(h):
        def go():
            total = rs_pair[spot, halves[h]]
            if line <= 4:
                for j in range(1, line):
                    sender = near(j)
                    line_sum(h, spot, sender).wait_recv()
                    total = total + rs_line[sender, halves[h]]
            else:

                def add(i, total):
                    sender = lax.rem(spot + line - i, line)
                    line_sum(h, spot, sender).wait_recv()
                    return total + rs_line[sender, halves[h]]

                total = lax.fori_loop(1, line, add, total)
            full[ev, me, halves[h]] = total
            each(1, line, lambda j: to_line(h, spot, near(j)).start())
            to_pair(h, spot, low).start()
            to_half(h, ev, spot).start()

        when_owner(me, go)

    def from_line(h, j):
        z = near(j)

        def go():
            to_line(h, z, spot).wait_recv()
            to_pair(h, z, low).start()
            to_half(h, ev, z).start()

        when_owner(device(z, low), go)

    def hop(h, j):
        z = near(j)

        def go():
            if h == 0:
                to_pair(0, z, 1 - low).wait_recv()
                on_half(ev, z).start()
            else:
                to_half(1, half, z).wait_recv()
                on_pair(z, low).start()

        when_owner(2 * z, go)

    def corner(j):
        z = near(j)

        def go():
            to_pair(1, z, 1 - low).wait_recv()
            to_twin(0, ev, z).start()
            to_half(0, half, z).wait_recv()
            on_half(half, z).wait_recv()
            on_pair(z, 1 - low).wait_recv()
            to_twin(1, half, z).start()

        when_owner(2 * z, go)

    if line == 4:
        for j in range(line):
            add_pair(0, j)
        add_pair(1, 0)
        add_pair(1, 1)
        own(0)
        add_pair(1, 2)
        add_pair(1, 3)
        hop(0, 0)
        from_line(0, 1)
        own(1)
        for work, h, j in (
            (from_line, 0, 2), (from_line, 0, 3), (hop, 0, 1), (hop, 1, 0), (from_line, 1, 1),
            (hop, 0, 2), (from_line, 1, 2), (hop, 0, 3), (from_line, 1, 3), (hop, 1, 1),
            (hop, 1, 2), (hop, 1, 3),
        ):
            work(h, j)
    else:
        for h in range(2):
            each(0, line, functools.partial(add_pair, h))
        for h in range(2):
            own(h)
        for h in range(2):
            each(1, line, functools.partial(from_line, h))
        for h in range(2):
            each(0, line, functools.partial(hop, h))
    each(0, line, corner)

    def drain(z):
        for h in range(2):
            when_owner(device(z, 1 - low), lambda: pair_sum(h, z, 1 - low).wait_send())

            @pl.when(z != spot)
            def _():
                when_owner(device(z, low), lambda: line_sum(h, z, spot).wait_send())
                when_owner(me, lambda: to_line(h, spot, z).wait_send())

        def go():
            for h in range(2):
                to_pair(h, z, low).wait_send()
                to_half(h, ev, z).wait_send()
            on_half(ev, z).wait_send()
            on_pair(z, low).wait_send()
            to_twin(0, ev, z).wait_send()
            to_twin(1, half, z).wait_send()

        when_owner(2 * z, go)

    each(0, line, drain)

    def write_full(z):
        where = pl.ds(2 * z, 2)
        return pltpu.make_async_copy(full.at[:, where], full_h.at[:, where], write_sem.at[z])

    def arrive(j):
        z = near(j)

        def go():
            to_twin(0, twin, z).wait_recv()
            to_twin(1, twin_half, z).wait_recv()
            write_full(z).start()

        when_owner(2 * z, go)

    each(0, line, arrive)
    each(0, line, lambda j: when_owner(2 * near(j), lambda: write_full(near(j)).wait()))


def finish(
    feat, full_in, flow_in, lateral_in,
    large, flow_out, lateral_out, w_first, b_first, b_second, w_out,
    full, flow, lateral, sems,
):
    last = full.shape[2] - 1
    middle = full.shape[0] // 2
    steps = []
    for side in range(2):
        where = pl.ds(side * middle, middle)
        steps.append((full_in.at[where], full.at[where], full.at[where, :, pl.ds(0, last)], large.at[where]))
    steps.append((lateral_in, lateral, lateral, lateral_out))
    steps.append((flow_in, flow, flow, flow_out))
    reads = [pltpu.make_async_copy(x[0], x[1], sems.at[0, i]) for i, x in enumerate(steps)]
    copies = [pltpu.make_async_copy(x[2], x[3], sems.at[1, i]) for i, x in enumerate(steps)]
    for read in reads:
        read.start()
    for read, copy in zip(reads, copies):
        read.wait()
        copy.start()
    n_event = full.shape[0]
    first_half = lax.broadcasted_iota(jnp.int32, (8, 128), 1) < 64
    for k in range(5):
        columns = []
        for e in range(0, n_event, 2):
            tails = []
            for s in range(2):
                tail = full[e + s, 5 + k // 2, last]
                tails.append(pltpu.roll(tail, 64, 1) if k % 2 != s else tail)
            turned = pltpu.roll(full[e + 1, k, last], 64, 1)
            columns += [
                full[e, k, last],
                jnp.where(first_half, tails[0], turned),
                jnp.where(first_half, turned, tails[1]),
            ]
        rows = jnp.concatenate(columns, axis=1)
        if k < 4:
            w_first[8 * k : 8 * k + 8, :] = rows
        else:
            b_first[...] = rows[0:1].reshape(rows.shape[1])
            b_second[...] = rows[1:2].reshape(rows.shape[1])
            w_out[...] = rows[2:3].reshape(rows.shape[1])
    for copy in copies:
        copy.wait()


def body(
    n,
    n_event,
    reach_attrs,
    w_first,
    b_first,
    w_second,
    b_second,
    w_out,
    section_factor,
    bed_slope,
    seg_count,
    section_class,
    down_local,
    send_list,
    recv_list,
    area_start,
    lateral,
    cotangent,
):
    f32, bf16 = jnp.float32, jnp.bfloat16
    events, reaches = area_start.shape
    feat, hid = w_first.shape
    part = hid // n_event
    owners = n if part % (8 * n) == 0 else part // 8
    chunk = part // owners
    span = (chunk // 8) * (hid // 128) + 1
    line = n // 2
    scale = 32.0 / math.sqrt(events * n_event * reaches * n)
    vmem = pl.BlockSpec(memory_space=pltpu.VMEM)
    hbm = pl.BlockSpec(memory_space=pltpu.HBM)
    smem = pl.BlockSpec(memory_space=pltpu.SMEM)
    dma = pltpu.SemaphoreType.DMA
    held = lambda x: pltpu.VMEM(x.shape, x.dtype)
    outflow, grad_lateral, full = pl.pallas_call(
        functools.partial(kernel, n, n_event, owners, chunk, scale),
        out_shape=(
            jax.ShapeDtypeStruct((events, reaches), f32),
            jax.ShapeDtypeStruct((STEPS, events, reaches), f32),
            jax.ShapeDtypeStruct((n_event, owners, span, 8, 128), f32),
        ),
        in_specs=[hbm] * 6 + [smem] + [hbm] * 9,
        out_specs=(hbm,) * 3,
        scratch_shapes=[
            pltpu.VMEM((events, reaches), f32),
            pltpu.VMEM((STEPS, events, reaches), f32),
            pltpu.VMEM((n_event, owners, span, 8, 128), f32),
            dma((2,)),
            pltpu.VMEM((PLACES, reaches), bf16),
            held(w_first), held(b_first), held(w_second), held(b_second), held(w_out),
            held(bed_slope), held(seg_count), held(section_class), held(down_local),
            held(send_list), held(recv_list), held(area_start), held(lateral), held(cotangent),
            dma((15,)),
            pltpu.VMEM((hid, feat), bf16),
            pltpu.VMEM((hid, hid), bf16),
            pltpu.VMEM((hid, 8), f32),
            pltpu.VMEM((hid, reaches), f32),
            pltpu.VMEM((hid, reaches), bf16),
            pltpu.VMEM((hid, reaches), bf16),
            pltpu.VMEM((hid, reaches), bf16),
            pltpu.VMEM((part, reaches), f32),
            pltpu.VMEM((n_event, 1, reaches // n_event), f32),
            pltpu.VMEM((LINKS * GROUP, reaches), bf16),
            pltpu.VMEM((LINKS * GROUP, reaches), bf16),
            pltpu.VMEM((HALO + 1, LINKS, 8, 128), f32),
            pltpu.VMEM((HALO + 1, LINKS, 8, 128), f32),
            pltpu.VMEM((1, reaches), f32),
            pltpu.VMEM((n_event - 1, 1, reaches), f32),
            pltpu.VMEM((owners, span, 8, 128), f32),
            pltpu.VMEM((line, span, 8, 128), f32),
            pltpu.VMEM((line, span, 8, 128), f32),
            dma((n_event - 1,)), dma((n_event - 1,)),
            dma((HALO + 1, LINKS)), dma((HALO + 1, LINKS)),
            dma((n_event - 1,)), dma((n_event - 1,)),
            dma((2, line)), dma((2, line)), dma((2, line)), dma((2, line)),
            dma((2, line)), dma((2, line)), dma((2, line)), dma((2, line)),
            dma((2, line)), dma((2, line)),
            dma((line,)), dma((line,)), dma((line,)), dma((line,)), dma((2, line)), dma((2, line)),
            dma((line,)),
        ],
        compiler_params=pltpu.CompilerParams(
            collective_id=0, has_side_effects=True, vmem_limit_bytes=63 * 1024 * 1024
        ),
    )(
        reach_attrs.T, w_first, b_first, w_second, b_second, w_out, section_factor,
        bed_slope, seg_count, section_class, down_local, send_list, recv_list,
        area_start, lateral, cotangent,
    )
    vector = jax.ShapeDtypeStruct((hid,), f32)
    large, outflow, grad_lateral, g_first, g_b_first, g_b_second, g_out = pl.pallas_call(
        functools.partial(finish, feat),
        out_shape=(
            jax.ShapeDtypeStruct((n_event, owners, span - 1, 8, 128), f32),
            jax.ShapeDtypeStruct((events, reaches), f32),
            jax.ShapeDtypeStruct((STEPS, events, reaches), f32),
            jax.ShapeDtypeStruct((feat, hid), f32),
            vector,
            vector,
            vector,
        ),
        in_specs=[hbm] * 3,
        out_specs=(hbm, hbm, hbm, vmem, vmem, vmem, vmem),
        scratch_shapes=[held(full), held(outflow), held(grad_lateral), dma((2, 4))],
    )(full, outflow, grad_lateral)
    g_second = large.reshape(hid // 8, hid // 128, 8, 128).transpose(0, 2, 1, 3).reshape(hid, hid)
    return outflow, grad_lateral, g_first, g_b_first, g_second, g_b_second, g_out


def solution(mesh):
    return jax.shard_map(
        functools.partial(body, mesh.shape["basin"], mesh.shape["event"]),
        mesh=mesh,
        in_specs=(
            P("basin", None),
            P(),
            P(),
            P(),
            P(),
            P(),
            P(),
            P("basin"),
            P("basin"),
            P("basin"),
            P("basin"),
            P("basin", None, None),
            P("basin", None, None),
            P("event", "basin"),
            P(None, "event", "basin"),
            P("event", "basin"),
        ),
        out_specs=(P("event", "basin"), P(None, "event", "basin"), P(), P(), P(), P(), P()),
        check_vma=False,
    )
```

```python
import functools
import math

import jax
import jax.numpy as jnp
from jax import lax
from jax.experimental import pallas as pl
from jax.experimental.pallas import tpu as pltpu
from jax.sharding import PartitionSpec as P

STEPS = 3
TINY = 1e-30
HALO = 2 * STEPS
LINKS = 4
GROUP = 32
PLACES = 48
MESH = pl.DeviceIdType.MESH
NT = (((1,), (1,)), ((), ()))
NN = (((1,), (0,)), ((), ()))


def split_two(x):
    high = x.astype(jnp.bfloat16)
    low = (x - high.astype(jnp.float32)).astype(jnp.bfloat16)
    return jnp.concatenate([high, low], axis=0)


def kernel(
    n, n_event, owners, chunk, scale,
    attrs_h, w_first_h, b_first_h, w_second_h, b_second_h, w_out_h, section_factor,
    bed_slope_h, seg_count_h, section_class_h, down_local_h, send_list_h, recv_list_h,
    area_start_h, lateral_h, cotangent_h,
    outflow_h, grad_lateral_h, full_h,
    outflow, grad_lateral, full, out_sem,
    attrs, w_first, b_first, w_second, b_second, w_out,
    bed_slope, seg_count, section_class, down_local, send_list, recv_list,
    area_start, lateral, cotangent, load_sem,
    w_firstT, w_secondT, cols,
    t_one, h_one, d_two, h_two, lower, squash_all, take_send, take_recv, overlap,
    out_msg, in_msg, rate_out, rate_in, slab, rs_pair, rs_line,
    s_send, s_recv,
    x_send, x_recv, r_send, r_recv, px_send, px_recv, pz_send, pz_recv,
    az_send, az_recv, ax_send, ax_recv, ay_send, ay_recv,
    fa_send, fa_recv, fb_send, fb_recv, tw_send, tw_recv, write_sem,
):
    f32, bf16 = jnp.float32, jnp.bfloat16
    me = lax.axis_index("basin")
    ev = lax.axis_index("event")
    events, reaches = area_start.shape
    hid = w_second.shape[0]
    feat = w_first.shape[0]
    part = hid // n_event
    offsets = (1, 2, n // 2, n - 1)
    base = pl.multiple_of(ev * part, 64)
    mine = pl.ds(base, part)
    width = reaches // n_event

    barrier = pltpu.get_barrier_semaphore()

    @pl.loop(1, n)
    def _(i):
        pl.semaphore_signal(barrier, inc=1, device_id={"basin": lax.rem(me + i, n)}, device_id_type=MESH)

    for i in range(1, n_event):
        pl.semaphore_signal(
            barrier, inc=1, device_id={"event": lax.rem(ev + i, n_event)}, device_id_type=MESH
        )

    loads = {}
    for name, source, target in (
        ("send_list", send_list_h, send_list),
        ("attrs", attrs_h, attrs.at[pl.ds(0, feat)]),
        ("area_start", area_start_h, area_start),
        ("bed_slope", bed_slope_h, bed_slope),
        ("section_class", section_class_h, section_class),
        ("w_second", w_second_h, w_second),
        ("w_first", w_first_h, w_first),
        ("b_first", b_first_h, b_first),
        ("b_second", b_second_h, b_second),
        ("w_out", w_out_h, w_out),
        ("recv_list", recv_list_h, recv_list),
        ("seg_count", seg_count_h, seg_count),
        ("down_local", down_local_h, down_local),
        ("lateral", lateral_h, lateral),
        ("cotangent", cotangent_h, cotangent),
    ):
        loads[name] = pltpu.make_async_copy(source, target, load_sem.at[len(loads)])
        loads[name].start()

    for name in ("send_list", "attrs", "area_start", "bed_slope", "section_class"):
        loads[name].wait()

    extra = attrs.shape[0] - feat
    attrs[feat:, :] = jnp.where(
        lax.broadcasted_iota(jnp.int32, (extra, reaches), 0) == 0, 1.0, 0.0
    ).astype(bf16)
    slot_row = lax.broadcasted_iota(jnp.int32, (LINKS * GROUP, 1), 0)
    slot = slot_row % GROUP
    cap = send_list.shape[2]
    spread = (
        slot == lax.broadcasted_iota(jnp.int32, (LINKS * GROUP, cap), 1)
    ).astype(f32)
    lane_reach = lax.broadcasted_iota(jnp.int32, (LINKS * GROUP, reaches), 1).astype(f32)
    lane_basin = lax.broadcasted_iota(jnp.int32, (LINKS * GROUP, n), 1)

    def one_hot_of(lists, sign):
        table = lax.dot_general(
            spread, lists[0].astype(f32), NT, precision=lax.Precision.HIGHEST,
            preferred_element_type=f32,
        )
        peer = jnp.zeros((LINKS * GROUP, 1), jnp.int32)
        for k, off in enumerate(offsets):
            peer = jnp.where(slot_row // GROUP == k, lax.rem(me + sign * off + n, n), peer)
        column = jnp.sum(jnp.where(lane_basin == peer, table, 0.0), axis=1, keepdims=True)
        column = jnp.where(slot < cap, column, float(reaches))
        return (jnp.abs(lane_reach - column) < 0.5).astype(bf16)


    take_send[...] = one_hot_of(send_list, 1)

    kind = section_class[...].reshape(1, reaches)
    conveyance = jnp.zeros((1, reaches), f32)
    for c in range(section_factor.shape[0]):
        conveyance = jnp.where(kind == c, section_factor[c], conveyance)
    k_base = jnp.sqrt(bed_slope[...].reshape(1, reaches)) * conveyance
    lane_group = lax.broadcasted_iota(jnp.int32, (8, 128), 1) // GROUP
    blocks = events // 8

    def message(index, k, sign):
        return pltpu.make_async_remote_copy(
            src_ref=out_msg.at[index, k],
            dst_ref=in_msg.at[index, k],
            send_sem=x_send.at[index, k],
            recv_sem=x_recv.at[index, k],
            device_id={"basin": lax.rem(me + sign * offsets[k] + n, n)},
            device_id_type=MESH,
        )

    def pick(fields, matrix):
        rows = fields[0].shape[0]
        both = lax.dot_general(
            jnp.concatenate([split_two(field) for field in fields], axis=0), matrix[...], NT,
            preferred_element_type=f32,
        )
        return [
            both[2 * rows * i : 2 * rows * i + rows] + both[2 * rows * i + rows : 2 * rows * (i + 1)]
            for i in range(len(fields))
        ]

    def send(index, picked, sign):
        for k in range(LINKS):
            packed = jnp.zeros((8, 128), f32)
            for q in range(blocks):
                piece = picked[8 * q : 8 * q + 8]
                shift = ((q - k) * GROUP) % 128
                if shift:
                    piece = pltpu.roll(piece, shift, 1)
                packed = jnp.where(lane_group == q, piece, packed)
            out_msg[index, k] = packed
            message(index, k, sign).start()

    def receive(index, sign):
        for k in range(LINKS):
            message(index, k, sign).wait_recv()
        pieces = []
        for q in range(blocks):
            got = jnp.zeros((8, 128), f32)
            for k in range(LINKS):
                piece = in_msg[index, k]
                shift = ((k - q) * GROUP) % 128
                if shift:
                    piece = pltpu.roll(piece, shift, 1)
                got = jnp.where(lane_group == k, piece, got)
            pieces.append(got)
        return jnp.concatenate(pieces, axis=0)

    def scatter(got, matrix):
        both = jnp.dot(split_two(got), matrix[...], preferred_element_type=f32)
        rows = got.shape[0]
        return both[:rows] + both[rows:]

    def cross(got, dims):
        both = lax.dot_general(split_two(got), overlap[...], dims, preferred_element_type=f32)
        return both[:events] + both[events:]

    def power(area):
        return jnp.exp((2.0 / 3.0) * jnp.log(area))

    def slot_power(area):
        return power(jnp.maximum(area, TINY))


    areas = [area_start[...]]
    powers = [power(areas[0])]
    plain = areas[0] * powers[0]
    outer, slot_plain = pick([k_base * plain, plain], take_send)
    inputs = lax.dot_general(attrs[0:feat, :], take_send[...], NT, preferred_element_type=f32)

    pl.semaphore_wait(barrier, n - 1 + n_event - 1)
    send(HALO, inputs, 1)
    send(0, outer, 1)

    for name in ("w_first", "b_first", "b_second", "w_out", "w_second"):
        loads[name].wait()

    w_firstT[...] = jnp.transpose(w_first[...])
    w_secondT[...] = jnp.transpose(w_second[...])
    w_out_row = w_out[...].astype(f32).reshape(1, hid)
    cols[...] = jnp.transpose(jnp.concatenate(
        [b_first[...].reshape(1, hid), b_second[...].reshape(1, hid), w_out_row,
         jnp.zeros((5, hid), f32)], axis=0
    ))
    w_out_rows = jnp.broadcast_to(w_out_row, (16, hid)).astype(bf16)

    def network(start, length):
        where = pl.ds(pl.multiple_of(start * 128, 128), length)
        one = jnp.tanh(
            jnp.dot(w_firstT[...], attrs[0:feat, where], preferred_element_type=f32) + cols[:, 0:1]
        )
        t_one[:, where] = one
        hidden = one.astype(bf16)
        h_one[:, where] = hidden
        two = jnp.tanh(
            jnp.dot(w_secondT[...], hidden, preferred_element_type=f32) + cols[:, 1:2]
        )
        rounded = two.astype(bf16)
        h_two[:, where] = rounded
        factor = (cols[:, 2:3] * (1.0 - two * two)).astype(bf16)
        d_two[:, where] = factor
        first = t_one[mine, where]
        lower[:, where] = (
            jnp.dot(w_second[mine, :], factor, preferred_element_type=f32) * (1.0 - first * first)
        )
        return rounded

    logit = jnp.dot(w_out_rows, network(ev * (width // 128), width), preferred_element_type=f32)[0:1]
    squash_all[ev] = 1.0 / (1.0 + jnp.exp(-logit))

    def squash_copy(i):
        return pltpu.make_async_remote_copy(
            src_ref=squash_all.at[ev],
            dst_ref=squash_all.at[ev],
            send_sem=s_send.at[i],
            recv_sem=s_recv.at[i],
            device_id={"event": lax.rem(ev + 1 + i, n_event)},
            device_id_type=MESH,
        )

    for i in range(n_event - 1):
        squash_copy(i).start()

    for name in ("recv_list", "seg_count", "down_local", "lateral"):
        loads[name].wait()
    take_recv[...] = one_hot_of(recv_list, -1)
    overlap[...] = lax.dot_general(
        take_send[...], take_recv[...], NT, preferred_element_type=f32
    ).astype(bf16)
    beta = 1.0 / seg_count[...].reshape(1, reaches).astype(f32)
    down = down_local[...].reshape(1, reaches)
    hop = jnp.where(down < reaches, down - lax.broadcasted_iota(jnp.int32, (1, reaches), 1), 0)
    masks = [(hop == d).astype(f32) for d in range(1, 9)]


    def hidden_of(weight, x, column):
        return jnp.tanh(
            jnp.dot(weight[...], x, preferred_element_type=f32) + cols[:, column : column + 1]
        ).astype(bf16)

    around = receive(HALO, 1).astype(bf16)
    around = hidden_of(w_secondT, hidden_of(w_firstT, around, 0), 1)
    around = jnp.dot(w_out_rows, around, preferred_element_type=f32)[0:1]
    got = receive(0, 1) / (0.02 + 0.08 * (1.0 / (1.0 + jnp.exp(-around))))

    units = reaches // 128
    begin = (ev + 1) * (width // 128)
    odd = lax.rem(begin, 2)
    pieces_left = [(lax.rem(begin + odd + 2 * i, units), 256) for i in range(4)]
    pieces_left.append((lax.rem(begin + 8 * (1 - odd), units), 128))

    for i in range(n_event - 1):
        squash_copy(i).wait_recv()
    squash = jnp.concatenate([squash_all[e] for e in range(n_event)], axis=1)
    rough = 0.02 + 0.08 * squash
    rate = k_base / rough
    slot_rate = pick([jnp.broadcast_to(rate, (16, reaches))], take_send)[0][0:1]
    shrinks = []
    for t in range(STEPS):
        area, p = areas[t], powers[t]
        flow = rate * area * p
        inflow = lateral[t]
        for d in range(1, 9):
            inflow = inflow + pltpu.roll(flow * masks[d - 1], d, 1)
        shrink = 1.0 / (1.0 + beta * rate * p)
        shrinks.append(shrink)
        kept = (area + beta * inflow) * shrink
        gain = beta * shrink
        if t < STEPS - 1:
            slots = pick([kept, gain], take_send)
        else:
            loads["cotangent"].wait()
            weight = cotangent[...] * rate * (5.0 / 3.0) * gain
            slots = pick([kept, gain, weight], take_recv)
        if t > 0:
            network(*pieces_left.pop(0))
            got = receive(t, 1)
        if t < STEPS - 1:
            slot_area = slots[0] + slots[1] * cross(got, NT)
            send(t + 1, slot_rate * slot_area * slot_power(slot_area), 1)
        else:
            slot_area = slots[0] + slots[1] * got
            send(STEPS, slots[2] * slot_power(slot_area), -1)
        areas.append(kept + gain * scatter(got, take_recv))
        powers.append(power(areas[t + 1]))
    emitted = areas[STEPS] * powers[STEPS]
    outflow[...] = rate * emitted
    write_flow = pltpu.make_async_copy(outflow, outflow_h, out_sem.at[0])
    write_flow.start()
    g_area = cotangent[...] * rate * (5.0 / 3.0) * powers[STEPS]
    g_rate = cotangent[...] * emitted
    for t in reversed(range(STEPS)):
        index = 2 * STEPS - 1 - t
        inner = g_area * shrinks[t]
        g_inflow = inner * beta
        grad_lateral[t] = g_inflow
        g_flow = jnp.zeros((events, reaches), f32)
        for d in range(1, 9):
            g_flow = g_flow + masks[d - 1] * pltpu.roll(g_inflow, reaches - d, 1)
        drop = g_inflow * areas[t + 1] * powers[t]
        g_rate = g_rate - drop + g_flow * areas[t] * powers[t]
        if t > 0:
            lean = (5.0 / 3.0) * rate * powers[t]
            onward = inner - (2.0 / 3.0) * rate * drop / areas[t] + lean * g_flow
            gain = beta * shrinks[t - 1]
            slots = pick([onward * gain, lean * gain], take_recv)
            network(*pieces_left.pop(0))
            got = receive(index, -1)
            send(index + 1, slots[0] + slots[1] * cross(got, NN), -1)
            back = scatter(got, take_send)
            g_rate = g_rate + back * areas[t] * powers[t]
            g_area = onward + lean * back
    write_lateral = pltpu.make_async_copy(grad_lateral, grad_lateral_h, out_sem.at[1])
    write_lateral.start()
    g_row = jnp.sum(g_rate, axis=0, keepdims=True)
    network(*pieces_left.pop(0))
    got = jnp.sum(receive(2 * STEPS - 1, -1) * slot_plain, axis=0, keepdims=True)
    rate_out[...] = g_row + scatter(jnp.broadcast_to(got, (16, LINKS * GROUP)), take_send)[0:1]

    def rate_copy(i):
        return pltpu.make_async_remote_copy(
            src_ref=rate_out,
            dst_ref=rate_in.at[i],
            send_sem=r_send.at[i],
            recv_sem=r_recv.at[i],
            device_id={"event": lax.rem(ev + 1 + i, n_event)},
            device_id_type=MESH,
        )

    for i in range(n_event - 1):
        rate_copy(i).start()
    for i in range(n_event - 1):
        rate_copy(i).wait_recv()
    terms = [rate_out[...]] + [rate_in[i] for i in range(n_event - 1)]
    g_sum = jnp.zeros((1, reaches), f32)
    for e in range(n_event):
        term = terms[0]
        for i in range(n_event - 1):
            term = jnp.where(lax.rem(e + 1 + i, n_event) == ev, terms[i + 1], term)
        g_sum = g_sum + term
    g_logit = (
        g_sum * (-rate / rough) * (scale * 0.08) * squash * (1.0 - squash)
    ).astype(bf16)
    g_logit32 = g_logit.astype(f32)

    scaled = (h_one[mine, :].astype(f32) * g_logit32).astype(bf16)
    large = lax.dot_general(scaled, d_two[...], NT, preferred_element_type=f32)
    tiles = hid // 128
    for d in range(owners):
        for r in range(chunk // 8):
            for c in range(tiles):
                top = d * chunk + 8 * r
                slab[d, r * tiles + c] = large[top : top + 8, 128 * c : 128 * c + 128]

    def when_owner(index, work):
        if owners == n:
            work()
        else:
            pl.when(index < owners)(work)

    line = n // 2
    low = lax.rem(me, 2)
    spot = me // 2
    pair = me + 1 - 2 * low
    half = lax.rem(ev + n_event // 2, n_event)
    twin = ev + 1 - 2 * lax.rem(ev, 2)
    twin_half = lax.rem(twin + n_event // 2, n_event)
    span = slab.shape[1]
    cut = (span + 1) // 2
    halves = (pl.ds(0, cut), pl.ds(cut, span - cut))

    def each(first, last, work):
        if last - first <= 4:
            for j in range(first, last):
                work(j)
        else:
            pl.loop(first, last)(work)

    def near(j):
        if line != 4:
            return lax.rem(spot + j, line)
        if isinstance(j, int) and j == 0:
            return spot
        orders = ((1, 2, 3), (2, 0, 3), (1, 3, 0), (2, 1, 0))
        code = sum(orders[s][j - 1] * 4 ** s for s in range(4))
        power_of = (1 + 3 * lax.rem(spot, 2)) * (1 + 15 * (spot // 2))
        return lax.rem(code // power_of, 4)

    def device(z, parity):
        return 2 * z + parity

    def pair_sum(h, z, parity):
        return pltpu.make_async_remote_copy(
            src_ref=slab.at[device(z, parity), halves[h]], dst_ref=rs_pair.at[z, halves[h]],
            send_sem=px_send.at[h, z], recv_sem=px_recv.at[h, z],
            device_id={"basin": pair}, device_id_type=MESH,
        )

    def line_sum(h, z, sender):
        return pltpu.make_async_remote_copy(
            src_ref=rs_pair.at[z, halves[h]], dst_ref=rs_line.at[sender, halves[h]],
            send_sem=pz_send.at[h, z], recv_sem=pz_recv.at[h, sender],
            device_id={"basin": device(z, low)}, device_id_type=MESH,
        )

    def far(j):
        return near(line - 1 - j)

    def start_pair(h, j):
        z = far(j)
        when_owner(device(z, 1 - low), lambda: pair_sum(h, z, 1 - low).start())

    each(0, line, functools.partial(start_pair, 0))

    g_pre = (lower[...] * g_logit32).astype(bf16)
    place = lax.broadcasted_iota(jnp.int32, (PLACES, reaches), 0)
    row_two = jnp.where(place == feat + 1, g_logit32, 0.0).astype(bf16)
    row_out = jnp.where(place == feat + 2, g_logit32, 0.0).astype(bf16)
    g_two = d_two[mine, :]
    second = h_two[mine, :]

    def narrow(first):
        end = first + 128
        return (
            lax.dot_general(attrs[...], g_pre[first:end], NT, preferred_element_type=f32)
            + lax.dot_general(row_two, g_two[first:end], NT, preferred_element_type=f32)
            + lax.dot_general(row_out, second[first:end], NT, preferred_element_type=f32)
        )

    left = narrow(0)
    right = narrow(part - 128)
    first_half = lax.broadcasted_iota(jnp.int32, (8, 128), 1) < 64
    last = slab.shape[1] - 1
    for k in range(5):
        slab[k, last] = left[8 * k : 8 * k + 8]
    for k in range(3):
        even = pltpu.roll(right[16 * k : 16 * k + 8], 64, 1)
        slab[5 + k, last] = jnp.where(first_half, even, right[16 * k + 8 : 16 * k + 16])
    for d in range(8, owners):
        slab[d, last] = jnp.zeros((8, 128), f32)

    each(0, line, functools.partial(start_pair, 1))

    for i in range(n_event - 1):
        squash_copy(i).wait_send()
    for index in range(HALO + 1):
        for k in range(LINKS):
            message(index, k, 1).wait_send()
    for i in range(n_event - 1):
        rate_copy(i).wait_send()
    write_flow.wait()
    write_lateral.wait()

    def add_pair(h, j):
        z = far(j)

        def go():
            pair_sum(h, z, 1 - low).wait_recv()
            rs_pair[z, halves[h]] = rs_pair[z, halves[h]] + slab[device(z, low), halves[h]]

            @pl.when(z != spot)
            def _():
                line_sum(h, z, spot).start()

        when_owner(device(z, low), go)

    def move(event, at, h, sems, slot, target):
        ref = full.at[event, at, halves[h]]
        return pltpu.make_async_remote_copy(
            src_ref=ref, dst_ref=ref, send_sem=sems[0].at[slot], recv_sem=sems[1].at[slot],
            device_id=target, device_id_type=MESH,
        )

    def to_line(h, source, peer):
        ref = full.at[ev, device(source, low), halves[h]]
        return pltpu.make_async_remote_copy(
            src_ref=ref, dst_ref=ref, send_sem=az_send.at[h, peer], recv_sem=az_recv.at[h, source],
            device_id={"basin": device(peer, low)}, device_id_type=MESH,
        )

    def to_pair(h, z, parity):
        return move(ev, device(z, parity), h, (ax_send.at[h], ax_recv.at[h]), z, {"basin": pair})

    def to_half(h, event, z):
        return move(event, device(z, low), h, (ay_send.at[h], ay_recv.at[h]), z, {"event": half})

    def on_half(event, z):
        return move(event, device(z, 1 - low), 0, (fa_send, fa_recv), z, {"event": half})

    def on_pair(z, parity):
        return move(half, device(z, parity), 1, (fb_send, fb_recv), z, {"basin": pair})

    def to_twin(side, event, z):
        ref = full.at[event, pl.ds(2 * z, 2)]
        return pltpu.make_async_remote_copy(
            src_ref=ref, dst_ref=ref, send_sem=tw_send.at[side, z], recv_sem=tw_recv.at[side, z],
            device_id={"event": twin}, device_id_type=MESH,
        )

    def own(h):
        def go():
            total = rs_pair[spot, halves[h]]
            if line <= 4:
                for j in range(1, line):
                    sender = near(j)
                    line_sum(h, spot, sender).wait_recv()
                    total = total + rs_line[sender, halves[h]]
            else:

                def add(i, total):
                    sender = lax.rem(spot + line - i, line)
                    line_sum(h, spot, sender).wait_recv()
                    return total + rs_line[sender, halves[h]]

                total = lax.fori_loop(1, line, add, total)
            full[ev, me, halves[h]] = total
            each(1, line, lambda j: to_line(h, spot, near(j)).start())
            to_pair(h, spot, low).start()
            to_half(h, ev, spot).start()

        when_owner(me, go)

    def from_line(h, j):
        z = near(j)

        def go():
            to_line(h, z, spot).wait_recv()
            to_pair(h, z, low).start()
            to_half(h, ev, z).start()

        when_owner(device(z, low), go)

    def hop(h, j):
        z = near(j)

        def go():
            if h == 0:
                to_pair(0, z, 1 - low).wait_recv()
                on_half(ev, z).start()
            else:
                to_half(1, half, z).wait_recv()
                on_pair(z, low).start()

        when_owner(2 * z, go)

    def corner(j):
        z = near(j)

        def go():
            to_pair(1, z, 1 - low).wait_recv()
            to_twin(0, ev, z).start()
            to_half(0, half, z).wait_recv()
            on_half(half, z).wait_recv()
            on_pair(z, 1 - low).wait_recv()
            to_twin(1, half, z).start()

        when_owner(2 * z, go)

    if line == 4:
        for j in range(line):
            add_pair(0, j)
        add_pair(1, 0)
        add_pair(1, 1)
        own(0)
        add_pair(1, 2)
        add_pair(1, 3)
        hop(0, 0)
        from_line(0, 1)
        own(1)
        for work, h, j in (
            (from_line, 0, 2), (from_line, 0, 3), (hop, 0, 1), (hop, 1, 0), (from_line, 1, 1),
            (hop, 0, 2), (from_line, 1, 2), (hop, 0, 3), (from_line, 1, 3), (hop, 1, 1),
            (hop, 1, 2), (hop, 1, 3),
        ):
            work(h, j)
    else:
        for h in range(2):
            each(0, line, functools.partial(add_pair, h))
        for h in range(2):
            own(h)
        for h in range(2):
            each(1, line, functools.partial(from_line, h))
        for h in range(2):
            each(0, line, functools.partial(hop, h))
    each(0, line, corner)

    def drain(z):
        for h in range(2):
            when_owner(device(z, 1 - low), lambda: pair_sum(h, z, 1 - low).wait_send())

            @pl.when(z != spot)
            def _():
                when_owner(device(z, low), lambda: line_sum(h, z, spot).wait_send())
                when_owner(me, lambda: to_line(h, spot, z).wait_send())

        def go():
            for h in range(2):
                to_pair(h, z, low).wait_send()
                to_half(h, ev, z).wait_send()
            on_half(ev, z).wait_send()
            on_pair(z, low).wait_send()
            to_twin(0, ev, z).wait_send()
            to_twin(1, half, z).wait_send()

        when_owner(2 * z, go)

    each(0, line, drain)

    def write_full(z):
        where = pl.ds(2 * z, 2)
        return pltpu.make_async_copy(full.at[:, where], full_h.at[:, where], write_sem.at[z])

    def arrive(j):
        z = near(j)

        def go():
            to_twin(0, twin, z).wait_recv()
            to_twin(1, twin_half, z).wait_recv()
            write_full(z).start()

        when_owner(2 * z, go)

    each(0, line, arrive)
    each(0, line, lambda j: when_owner(2 * near(j), lambda: write_full(near(j)).wait()))


def finish(
    feat, full_in, flow_in, lateral_in,
    large, flow_out, lateral_out, w_first, b_first, b_second, w_out,
    full, flow, lateral, small, vectors, sems, small_sems,
):
    last = full.shape[2] - 1
    middle = full.shape[0] // 2
    steps = []
    for side in range(2):
        where = pl.ds(side * middle, middle)
        steps.append((full_in.at[where], full.at[where], full.at[where, :, pl.ds(0, last)], large.at[where]))
    steps.append((lateral_in, lateral, lateral, lateral_out))
    steps.append((flow_in, flow, flow, flow_out))
    reads = [pltpu.make_async_copy(x[0], x[1], sems.at[0, i]) for i, x in enumerate(steps)]
    copies = [pltpu.make_async_copy(x[2], x[3], sems.at[1, i]) for i, x in enumerate(steps)]
    for read in reads:
        read.start()
    for read, copy in zip(reads, copies):
        read.wait()
        copy.start()
    n_event = full.shape[0]
    first_half = lax.broadcasted_iota(jnp.int32, (8, 128), 1) < 64
    for k in range(5):
        columns = []
        for e in range(0, n_event, 2):
            tails = []
            for s in range(2):
                tail = full[e + s, 5 + k // 2, last]
                tails.append(pltpu.roll(tail, 64, 1) if k % 2 != s else tail)
            turned = pltpu.roll(full[e + 1, k, last], 64, 1)
            columns += [
                full[e, k, last],
                jnp.where(first_half, tails[0], turned),
                jnp.where(first_half, turned, tails[1]),
            ]
        rows = jnp.concatenate(columns, axis=1)
        if k < 4:
            small[8 * k : 8 * k + 8, :] = rows
        else:
            for i, held in enumerate(vectors):
                held[...] = rows[i : i + 1].reshape(rows.shape[1])
    pairs = [(small, w_first)] + list(zip(vectors, (b_first, b_second, w_out)))
    for i, (held, target) in enumerate(pairs):
        copies.append(pltpu.make_async_copy(held, target, small_sems.at[i]))
        copies[-1].start()
    for copy in copies:
        copy.wait()


def body(
    n,
    n_event,
    reach_attrs,
    w_first,
    b_first,
    w_second,
    b_second,
    w_out,
    section_factor,
    bed_slope,
    seg_count,
    section_class,
    down_local,
    send_list,
    recv_list,
    area_start,
    lateral,
    cotangent,
):
    f32, bf16 = jnp.float32, jnp.bfloat16
    events, reaches = area_start.shape
    feat, hid = w_first.shape
    part = hid // n_event
    owners = n if part % (8 * n) == 0 else part // 8
    chunk = part // owners
    span = (chunk // 8) * (hid // 128) + 1
    line = n // 2
    scale = 32.0 / math.sqrt(events * n_event * reaches * n)
    vmem = pl.BlockSpec(memory_space=pltpu.VMEM)
    hbm = pl.BlockSpec(memory_space=pltpu.HBM)
    smem = pl.BlockSpec(memory_space=pltpu.SMEM)
    dma = pltpu.SemaphoreType.DMA
    held = lambda x: pltpu.VMEM(x.shape, x.dtype)
    outflow, grad_lateral, full = pl.pallas_call(
        functools.partial(kernel, n, n_event, owners, chunk, scale),
        out_shape=(
            jax.ShapeDtypeStruct((events, reaches), f32),
            jax.ShapeDtypeStruct((STEPS, events, reaches), f32),
            jax.ShapeDtypeStruct((n_event, owners, span, 8, 128), f32),
        ),
        in_specs=[hbm] * 6 + [smem] + [hbm] * 9,
        out_specs=(hbm,) * 3,
        scratch_shapes=[
            pltpu.VMEM((events, reaches), f32),
            pltpu.VMEM((STEPS, events, reaches), f32),
            pltpu.VMEM((n_event, owners, span, 8, 128), f32),
            dma((2,)),
            pltpu.VMEM((PLACES, reaches), bf16),
            held(w_first), held(b_first), held(w_second), held(b_second), held(w_out),
            held(bed_slope), held(seg_count), held(section_class), held(down_local),
            held(send_list), held(recv_list), held(area_start), held(lateral), held(cotangent),
            dma((15,)),
            pltpu.VMEM((hid, feat), bf16),
            pltpu.VMEM((hid, hid), bf16),
            pltpu.VMEM((hid, 8), f32),
            pltpu.VMEM((hid, reaches), f32),
            pltpu.VMEM((hid, reaches), bf16),
            pltpu.VMEM((hid, reaches), bf16),
            pltpu.VMEM((hid, reaches), bf16),
            pltpu.VMEM((part, reaches), f32),
            pltpu.VMEM((n_event, 1, reaches // n_event), f32),
            pltpu.VMEM((LINKS * GROUP, reaches), bf16),
            pltpu.VMEM((LINKS * GROUP, reaches), bf16),
            pltpu.VMEM((LINKS * GROUP, LINKS * GROUP), bf16),
            pltpu.VMEM((HALO + 1, LINKS, 8, 128), f32),
            pltpu.VMEM((HALO + 1, LINKS, 8, 128), f32),
            pltpu.VMEM((1, reaches), f32),
            pltpu.VMEM((n_event - 1, 1, reaches), f32),
            pltpu.VMEM((owners, span, 8, 128), f32),
            pltpu.VMEM((line, span, 8, 128), f32),
            pltpu.VMEM((line, span, 8, 128), f32),
            dma((n_event - 1,)), dma((n_event - 1,)),
            dma((HALO + 1, LINKS)), dma((HALO + 1, LINKS)),
            dma((n_event - 1,)), dma((n_event - 1,)),
            dma((2, line)), dma((2, line)), dma((2, line)), dma((2, line)),
            dma((2, line)), dma((2, line)), dma((2, line)), dma((2, line)),
            dma((2, line)), dma((2, line)),
            dma((line,)), dma((line,)), dma((line,)), dma((line,)), dma((2, line)), dma((2, line)),
            dma((line,)),
        ],
        compiler_params=pltpu.CompilerParams(
            collective_id=0, has_side_effects=True, vmem_limit_bytes=63 * 1024 * 1024
        ),
    )(
        reach_attrs.T, w_first, b_first, w_second, b_second, w_out, section_factor,
        bed_slope, seg_count, section_class, down_local, send_list, recv_list,
        area_start, lateral, cotangent,
    )
    vector = jax.ShapeDtypeStruct((hid,), f32)
    w_first_f32 = jax.ShapeDtypeStruct((feat, hid), f32)
    large, outflow, grad_lateral, g_first, g_b_first, g_b_second, g_out = pl.pallas_call(
        functools.partial(finish, feat),
        out_shape=(
            jax.ShapeDtypeStruct((n_event, owners, span - 1, 8, 128), f32),
            jax.ShapeDtypeStruct((events, reaches), f32),
            jax.ShapeDtypeStruct((STEPS, events, reaches), f32),
            w_first_f32,
            vector,
            vector,
            vector,
        ),
        in_specs=[hbm] * 3,
        out_specs=(hbm,) * 7,
        scratch_shapes=[
            held(full), held(outflow), held(grad_lateral),
            held(w_first_f32), [held(vector)] * 3, dma((2, 4)), dma((4,)),
        ],
    )(full, outflow, grad_lateral)
    g_second = large.reshape(hid // 8, hid // 128, 8, 128).transpose(0, 2, 1, 3).reshape(hid, hid)
    return outflow, grad_lateral, g_first, g_b_first, g_second, g_b_second, g_out


def solution(mesh):
    return jax.shard_map(
        functools.partial(body, mesh.shape["basin"], mesh.shape["event"]),
        mesh=mesh,
        in_specs=(
            P("basin", None),
            P(),
            P(),
            P(),
            P(),
            P(),
            P(),
            P("basin"),
            P("basin"),
            P("basin"),
            P("basin"),
            P("basin", None, None),
            P("basin", None, None),
            P("event", "basin"),
            P(None, "event", "basin"),
            P("event", "basin"),
        ),
        out_specs=(P("event", "basin"), P(None, "event", "basin"), P(), P(), P(), P(), P()),
        check_vma=False,
    )
```

```python
import functools
import math

import jax
import jax.numpy as jnp
from jax import lax
from jax.experimental import pallas as pl
from jax.experimental.pallas import tpu as pltpu
from jax.sharding import PartitionSpec as P

STEPS = 3
TINY = 1e-30
HALO = 2 * STEPS
LINKS = 4
GROUP = 32
PLACES = 48
MESH = pl.DeviceIdType.MESH
NT = (((1,), (1,)), ((), ()))
NN = (((1,), (0,)), ((), ()))


def split_two(x):
    high = x.astype(jnp.bfloat16)
    low = (x - high.astype(jnp.float32)).astype(jnp.bfloat16)
    return jnp.concatenate([high, low], axis=0)


def kernel(
    n, n_event, owners, chunk, scale,
    attrs_h, w_first_h, b_first_h, w_second_h, b_second_h, w_out_h, section_factor,
    bed_slope_h, seg_count_h, section_class_h, down_local_h, send_list_h, recv_list_h,
    area_start_h, lateral_h, cotangent_h,
    outflow_h, grad_lateral_h, full_h,
    outflow, grad_lateral, full, out_sem,
    attrs, w_first, b_first, w_second, b_second, w_out,
    bed_slope, seg_count, section_class, down_local, send_list, recv_list,
    area_start, lateral, cotangent, load_sem,
    w_firstT, w_secondT, cols,
    t_one, h_one, d_two, h_two, lower, squash_all, take_send, take_recv, overlap,
    out_msg, in_msg, share_out, share_in, share_send, share_recv, rate_out, rate_in, slab, rs_pair, rs_line,
    s_send, s_recv,
    x_send, x_recv, r_send, r_recv, px_send, px_recv, pz_send, pz_recv,
    az_send, az_recv, ax_send, ax_recv, ay_send, ay_recv,
    fa_send, fa_recv, fb_send, fb_recv, tw_send, tw_recv, write_sem,
):
    f32, bf16 = jnp.float32, jnp.bfloat16
    me = lax.axis_index("basin")
    ev = lax.axis_index("event")
    events, reaches = area_start.shape
    hid = w_second.shape[0]
    feat = w_first.shape[0]
    part = hid // n_event
    offsets = (1, 2, n // 2, n - 1)
    base = pl.multiple_of(ev * part, 64)
    mine = pl.ds(base, part)
    width = reaches // n_event

    barrier = pltpu.get_barrier_semaphore()

    def greet(offset):
        pl.semaphore_signal(
            barrier, inc=1, device_id={"basin": lax.rem(me + offset, n)}, device_id_type=MESH
        )

    greet(1)
    greet(n - 1)
    if n <= 8:
        for i in range(1, n // 2):
            greet(2 * i)
    else:
        pl.loop(1, n // 2)(lambda i: greet(2 * i))

    for i in range(1, n_event):
        pl.semaphore_signal(
            barrier, inc=1, device_id={"event": lax.rem(ev + i, n_event)}, device_id_type=MESH
        )

    loads = {}
    for name, source, target in (
        ("send_list", send_list_h, send_list),
        ("attrs", attrs_h, attrs.at[pl.ds(0, feat)]),
        ("area_start", area_start_h, area_start),
        ("bed_slope", bed_slope_h, bed_slope),
        ("section_class", section_class_h, section_class),
        ("w_second", w_second_h, w_second),
        ("w_first", w_first_h, w_first),
        ("b_first", b_first_h, b_first),
        ("b_second", b_second_h, b_second),
        ("w_out", w_out_h, w_out),
        ("recv_list", recv_list_h, recv_list),
        ("seg_count", seg_count_h, seg_count),
        ("down_local", down_local_h, down_local),
        ("lateral", lateral_h, lateral),
        ("cotangent", cotangent_h, cotangent),
    ):
        loads[name] = pltpu.make_async_copy(source, target, load_sem.at[len(loads)])
        loads[name].start()

    for name in ("send_list", "attrs", "area_start", "bed_slope", "section_class"):
        loads[name].wait()

    extra = attrs.shape[0] - feat
    attrs[feat:, :] = jnp.where(
        lax.broadcasted_iota(jnp.int32, (extra, reaches), 0) == 0, 1.0, 0.0
    ).astype(bf16)
    slot_row = lax.broadcasted_iota(jnp.int32, (LINKS * GROUP, 1), 0)
    slot = slot_row % GROUP
    cap = send_list.shape[2]
    spread = (
        slot == lax.broadcasted_iota(jnp.int32, (LINKS * GROUP, cap), 1)
    ).astype(f32)
    lane_reach = lax.broadcasted_iota(jnp.int32, (LINKS * GROUP, reaches), 1).astype(f32)
    lane_basin = lax.broadcasted_iota(jnp.int32, (LINKS * GROUP, n), 1)

    def one_hot_of(lists, sign):
        table = lax.dot_general(
            spread, lists[0].astype(f32), NT, precision=lax.Precision.HIGHEST,
            preferred_element_type=f32,
        )
        peer = jnp.zeros((LINKS * GROUP, 1), jnp.int32)
        for k, off in enumerate(offsets):
            peer = jnp.where(slot_row // GROUP == k, lax.rem(me + sign * off + n, n), peer)
        column = jnp.sum(jnp.where(lane_basin == peer, table, 0.0), axis=1, keepdims=True)
        column = jnp.where(slot < cap, column, float(reaches))
        return (jnp.abs(lane_reach - column) < 0.5).astype(bf16)


    take_send[...] = one_hot_of(send_list, 1)

    kind = section_class[...].reshape(1, reaches)
    conveyance = jnp.zeros((1, reaches), f32)
    for c in range(section_factor.shape[0]):
        conveyance = jnp.where(kind == c, section_factor[c], conveyance)
    k_base = jnp.sqrt(bed_slope[...].reshape(1, reaches)) * conveyance
    lane_group = lax.broadcasted_iota(jnp.int32, (8, 128), 1) // GROUP
    blocks = events // 8

    def message(index, k, sign):
        return pltpu.make_async_remote_copy(
            src_ref=out_msg.at[index, k],
            dst_ref=in_msg.at[index, k],
            send_sem=x_send.at[index, k],
            recv_sem=x_recv.at[index, k],
            device_id={"basin": lax.rem(me + sign * offsets[k] + n, n)},
            device_id_type=MESH,
        )

    def pick(fields, matrix):
        rows = fields[0].shape[0]
        both = lax.dot_general(
            jnp.concatenate([split_two(field) for field in fields], axis=0), matrix[...], NT,
            preferred_element_type=f32,
        )
        return [
            both[2 * rows * i : 2 * rows * i + rows] + both[2 * rows * i + rows : 2 * rows * (i + 1)]
            for i in range(len(fields))
        ]

    def send(index, picked, sign):
        for k in range(LINKS):
            packed = jnp.zeros((8, 128), f32)
            for q in range(blocks):
                piece = picked[8 * q : 8 * q + 8]
                shift = ((q - k) * GROUP) % 128
                if shift:
                    piece = pltpu.roll(piece, shift, 1)
                packed = jnp.where(lane_group == q, piece, packed)
            out_msg[index, k] = packed
            message(index, k, sign).start()

    def receive(index, sign):
        for k in range(LINKS):
            message(index, k, sign).wait_recv()
        pieces = []
        for q in range(blocks):
            got = jnp.zeros((8, 128), f32)
            for k in range(LINKS):
                piece = in_msg[index, k]
                shift = ((k - q) * GROUP) % 128
                if shift:
                    piece = pltpu.roll(piece, shift, 1)
                got = jnp.where(lane_group == k, piece, got)
            pieces.append(got)
        return jnp.concatenate(pieces, axis=0)

    def scatter(got, matrix):
        both = jnp.dot(split_two(got), matrix[...], preferred_element_type=f32)
        rows = got.shape[0]
        return both[:rows] + both[rows:]

    def cross(got, dims):
        both = lax.dot_general(split_two(got), overlap[...], dims, preferred_element_type=f32)
        return both[:events] + both[events:]

    def power(area):
        return jnp.exp((2.0 / 3.0) * jnp.log(area))

    def slot_power(area):
        return power(jnp.maximum(area, TINY))


    areas = [area_start[...]]
    powers = [power(areas[0])]
    plain = areas[0] * powers[0]
    outer = pick([k_base * plain], take_send)[0]
    inputs = lax.dot_general(attrs[0:feat, :], take_send[...], NT, preferred_element_type=f32)

    pl.semaphore_wait(barrier, n // 2 + 1 + n_event - 1)
    send(HALO, inputs, 1)
    send(0, outer, 1)

    for name in ("w_first", "b_first", "b_second", "w_out", "w_second"):
        loads[name].wait()

    w_firstT[...] = jnp.transpose(w_first[...])
    w_secondT[...] = jnp.transpose(w_second[...])
    w_out_row = w_out[...].astype(f32).reshape(1, hid)
    cols[...] = jnp.transpose(jnp.concatenate(
        [b_first[...].reshape(1, hid), b_second[...].reshape(1, hid), w_out_row,
         jnp.zeros((5, hid), f32)], axis=0
    ))
    w_out_rows = jnp.broadcast_to(w_out_row, (16, hid)).astype(bf16)

    def network(start, length):
        where = pl.ds(pl.multiple_of(start * 128, 128), length)
        one = jnp.tanh(
            jnp.dot(w_firstT[...], attrs[0:feat, where], preferred_element_type=f32) + cols[:, 0:1]
        )
        t_one[:, where] = one
        hidden = one.astype(bf16)
        h_one[:, where] = hidden
        two = jnp.tanh(
            jnp.dot(w_secondT[...], hidden, preferred_element_type=f32) + cols[:, 1:2]
        )
        rounded = two.astype(bf16)
        h_two[:, where] = rounded
        factor = (cols[:, 2:3] * (1.0 - two * two)).astype(bf16)
        d_two[:, where] = factor
        first = t_one[mine, where]
        lower[:, where] = (
            jnp.dot(w_second[mine, :], factor, preferred_element_type=f32) * (1.0 - first * first)
        )
        return rounded

    logit = jnp.dot(w_out_rows, network(ev * (width // 128), width), preferred_element_type=f32)[0:1]
    squash_all[ev] = 1.0 / (1.0 + jnp.exp(-logit))

    def squash_copy(i):
        return pltpu.make_async_remote_copy(
            src_ref=squash_all.at[ev],
            dst_ref=squash_all.at[ev],
            send_sem=s_send.at[i],
            recv_sem=s_recv.at[i],
            device_id={"event": lax.rem(ev + 1 + i, n_event)},
            device_id_type=MESH,
        )

    for i in range(n_event - 1):
        squash_copy(i).start()

    for name in ("recv_list", "seg_count", "down_local", "lateral"):
        loads[name].wait()
    take_recv[...] = one_hot_of(recv_list, -1)
    overlap[...] = lax.dot_general(
        take_send[...], take_recv[...], NT, preferred_element_type=f32
    ).astype(bf16)
    beta = 1.0 / seg_count[...].reshape(1, reaches).astype(f32)
    down = down_local[...].reshape(1, reaches)
    hop = jnp.where(down < reaches, down - lax.broadcasted_iota(jnp.int32, (1, reaches), 1), 0)
    masks = [(hop == d).astype(f32) for d in range(1, 9)]


    def hidden_of(weight, x, column):
        return jnp.tanh(
            jnp.dot(weight[...], x, preferred_element_type=f32) + cols[:, column : column + 1]
        ).astype(bf16)

    around = receive(HALO, 1).astype(bf16)
    around = hidden_of(w_secondT, hidden_of(w_firstT, around, 0), 1)
    around = jnp.dot(w_out_rows, around, preferred_element_type=f32)[0:1]
    got = receive(0, 1) / (0.02 + 0.08 * (1.0 / (1.0 + jnp.exp(-around))))

    units = reaches // 128
    begin = (ev + 1) * (width // 128)
    odd = lax.rem(begin, 2)
    pieces_left = [(lax.rem(begin + odd + 2 * i, units), 256) for i in range(4)]
    pieces_left.append((lax.rem(begin + 8 * (1 - odd), units), 128))

    for i in range(n_event - 1):
        squash_copy(i).wait_recv()
    squash = jnp.concatenate([squash_all[e] for e in range(n_event)], axis=1)
    rough = 0.02 + 0.08 * squash
    rate = k_base / rough
    slot_rate = pick([jnp.broadcast_to(rate, (16, reaches))], take_send)[0][0:1]
    first_got = got

    def share(k, e):
        return pltpu.make_async_remote_copy(
            src_ref=share_out,
            dst_ref=share_in.at[k, ev],
            send_sem=share_send.at[k, e],
            recv_sem=share_recv.at[k, ev],
            device_id={"basin": lax.rem(me + n - offsets[k], n), "event": e},
            device_id_type=MESH,
        )

    def shared_from(k, e):
        return pltpu.make_async_remote_copy(
            src_ref=share_out,
            dst_ref=share_in.at[k, e],
            send_sem=share_send.at[k, e],
            recv_sem=share_recv.at[k, e],
            device_id={"basin": lax.rem(me + n - offsets[k], n), "event": e},
            device_id_type=MESH,
        )

    shrinks = []
    for t in range(STEPS):
        area, p = areas[t], powers[t]
        flow = rate * area * p
        inflow = lateral[t]
        for d in range(1, 9):
            inflow = inflow + pltpu.roll(flow * masks[d - 1], d, 1)
        shrink = 1.0 / (1.0 + beta * rate * p)
        shrinks.append(shrink)
        kept = (area + beta * inflow) * shrink
        gain = beta * shrink
        if t < STEPS - 1:
            slots = pick([kept, gain], take_send)
        else:
            loads["cotangent"].wait()
            weight = cotangent[...] * rate * (5.0 / 3.0) * gain
            slots = pick([kept, gain, weight], take_recv)
        if t > 0:
            network(*pieces_left.pop(0))
            got = receive(t, 1)
        if t < STEPS - 1:
            slot_area = slots[0] + slots[1] * cross(got, NT)
            send(t + 1, slot_rate * slot_area * slot_power(slot_area), 1)
        else:
            slot_area = slots[0] + slots[1] * got
            send(STEPS, slots[2] * slot_power(slot_area), -1)
        areas.append(kept + gain * scatter(got, take_recv))
        powers.append(power(areas[t + 1]))
    emitted = areas[STEPS] * powers[STEPS]
    outflow[...] = rate * emitted
    write_flow = pltpu.make_async_copy(outflow, outflow_h, out_sem.at[0])
    write_flow.start()
    g_area = cotangent[...] * rate * (5.0 / 3.0) * powers[STEPS]
    g_rate = cotangent[...] * emitted
    for t in reversed(range(STEPS)):
        index = 2 * STEPS - 1 - t
        inner = g_area * shrinks[t]
        g_inflow = inner * beta
        grad_lateral[t] = g_inflow
        g_flow = jnp.zeros((events, reaches), f32)
        for d in range(1, 9):
            g_flow = g_flow + masks[d - 1] * pltpu.roll(g_inflow, reaches - d, 1)
        drop = g_inflow * areas[t + 1] * powers[t]
        g_rate = g_rate - drop + g_flow * areas[t] * powers[t]
        if t > 0:
            lean = (5.0 / 3.0) * rate * powers[t]
            onward = inner - (2.0 / 3.0) * rate * drop / areas[t] + lean * g_flow
            gain = beta * shrinks[t - 1]
            slots = pick([onward * gain, lean * gain], take_recv)
            network(*pieces_left.pop(0))
            got = receive(index, -1)
            onto = slots[0] + slots[1] * cross(got, NN)
            if t > 1:
                send(index + 1, onto, -1)
            else:
                share_out[...] = jnp.sum(onto * first_got, axis=0, keepdims=True)
                for k in range(LINKS):
                    for e in range(n_event):
                        share(k, e).start()
            back = scatter(got, take_send)
            g_rate = g_rate + back * areas[t] * powers[t]
            g_area = onward + lean * back
    write_lateral = pltpu.make_async_copy(grad_lateral, grad_lateral_h, out_sem.at[1])
    write_lateral.start()
    rate_out[...] = jnp.sum(g_rate, axis=0, keepdims=True)

    def rate_copy(i):
        return pltpu.make_async_remote_copy(
            src_ref=rate_out,
            dst_ref=rate_in.at[i],
            send_sem=r_send.at[i],
            recv_sem=r_recv.at[i],
            device_id={"event": lax.rem(ev + 1 + i, n_event)},
            device_id_type=MESH,
        )

    for i in range(n_event - 1):
        rate_copy(i).start()
    network(*pieces_left.pop(0))
    for i in range(n_event - 1):
        rate_copy(i).wait_recv()
    slot_group = lax.broadcasted_iota(jnp.int32, (1, LINKS * GROUP), 1) // GROUP
    shares = jnp.zeros((1, LINKS * GROUP), f32)
    for k in range(LINKS):
        for e in range(n_event):
            shared_from(k, e).wait_recv()
        total = share_in[k, 0]
        for e in range(1, n_event):
            total = total + share_in[k, e]
        shares = jnp.where(slot_group == k, total, shares)
    shared = scatter(jnp.broadcast_to(shares, (16, LINKS * GROUP)), take_send)[0:1] / rate
    terms = [rate_out[...]] + [rate_in[i] for i in range(n_event - 1)]
    g_sum = jnp.zeros((1, reaches), f32)
    for e in range(n_event):
        term = terms[0]
        for i in range(n_event - 1):
            term = jnp.where(lax.rem(e + 1 + i, n_event) == ev, terms[i + 1], term)
        g_sum = g_sum + term
    g_sum = g_sum + shared
    g_logit = (
        g_sum * (-rate / rough) * (scale * 0.08) * squash * (1.0 - squash)
    ).astype(bf16)
    g_logit32 = g_logit.astype(f32)

    scaled = (h_one[mine, :].astype(f32) * g_logit32).astype(bf16)
    large = lax.dot_general(scaled, d_two[...], NT, preferred_element_type=f32)
    tiles = hid // 128
    for d in range(owners):
        for r in range(chunk // 8):
            for c in range(tiles):
                top = d * chunk + 8 * r
                slab[d, r * tiles + c] = large[top : top + 8, 128 * c : 128 * c + 128]

    def when_owner(index, work):
        if owners == n:
            work()
        else:
            pl.when(index < owners)(work)

    line = n // 2
    low = lax.rem(me, 2)
    spot = me // 2
    pair = me + 1 - 2 * low
    half = lax.rem(ev + n_event // 2, n_event)
    twin = ev + 1 - 2 * lax.rem(ev, 2)
    twin_half = lax.rem(twin + n_event // 2, n_event)
    span = slab.shape[1]
    cut = (span + 1) // 2
    halves = (pl.ds(0, cut), pl.ds(cut, span - cut))

    def each(first, last, work):
        if last - first <= 4:
            for j in range(first, last):
                work(j)
        else:
            pl.loop(first, last)(work)

    def near(j):
        if line != 4:
            return lax.rem(spot + j, line)
        if isinstance(j, int) and j == 0:
            return spot
        orders = ((1, 2, 3), (2, 0, 3), (1, 3, 0), (2, 1, 0))
        code = sum(orders[s][j - 1] * 4 ** s for s in range(4))
        power_of = (1 + 3 * lax.rem(spot, 2)) * (1 + 15 * (spot // 2))
        return lax.rem(code // power_of, 4)

    def device(z, parity):
        return 2 * z + parity

    def pair_sum(h, z, parity):
        return pltpu.make_async_remote_copy(
            src_ref=slab.at[device(z, parity), halves[h]], dst_ref=rs_pair.at[z, halves[h]],
            send_sem=px_send.at[h, z], recv_sem=px_recv.at[h, z],
            device_id={"basin": pair}, device_id_type=MESH,
        )

    def line_sum(h, z, sender):
        return pltpu.make_async_remote_copy(
            src_ref=rs_pair.at[z, halves[h]], dst_ref=rs_line.at[sender, halves[h]],
            send_sem=pz_send.at[h, z], recv_sem=pz_recv.at[h, sender],
            device_id={"basin": device(z, low)}, device_id_type=MESH,
        )

    def far(j):
        return near(line - 1 - j)

    def start_pair(h, j):
        z = far(j)
        when_owner(device(z, 1 - low), lambda: pair_sum(h, z, 1 - low).start())

    each(0, line, functools.partial(start_pair, 0))

    g_pre = (lower[...] * g_logit32).astype(bf16)
    place = lax.broadcasted_iota(jnp.int32, (PLACES, reaches), 0)
    row_two = jnp.where(place == feat + 1, g_logit32, 0.0).astype(bf16)
    row_out = jnp.where(place == feat + 2, g_logit32, 0.0).astype(bf16)
    g_two = d_two[mine, :]
    second = h_two[mine, :]

    def narrow(first):
        end = first + 128
        return (
            lax.dot_general(attrs[...], g_pre[first:end], NT, preferred_element_type=f32)
            + lax.dot_general(row_two, g_two[first:end], NT, preferred_element_type=f32)
            + lax.dot_general(row_out, second[first:end], NT, preferred_element_type=f32)
        )

    left = narrow(0)
    right = narrow(part - 128)
    first_half = lax.broadcasted_iota(jnp.int32, (8, 128), 1) < 64
    last = slab.shape[1] - 1
    for k in range(5):
        slab[k, last] = left[8 * k : 8 * k + 8]
    for k in range(3):
        even = pltpu.roll(right[16 * k : 16 * k + 8], 64, 1)
        slab[5 + k, last] = jnp.where(first_half, even, right[16 * k + 8 : 16 * k + 16])
    for d in range(8, owners):
        slab[d, last] = jnp.zeros((8, 128), f32)

    each(0, line, functools.partial(start_pair, 1))

    for i in range(n_event - 1):
        squash_copy(i).wait_send()
    for index in range(HALO + 1):
        for k in range(LINKS):
            if index != 2 * STEPS - 1:
                message(index, k, 1).wait_send()
    for k in range(LINKS):
        for e in range(n_event):
            share(k, e).wait_send()
    for i in range(n_event - 1):
        rate_copy(i).wait_send()
    write_flow.wait()
    write_lateral.wait()

    def add_pair(h, j):
        z = far(j)

        def go():
            pair_sum(h, z, 1 - low).wait_recv()
            rs_pair[z, halves[h]] = rs_pair[z, halves[h]] + slab[device(z, low), halves[h]]

            @pl.when(z != spot)
            def _():
                line_sum(h, z, spot).start()

        when_owner(device(z, low), go)

    def move(event, at, h, sems, slot, target):
        ref = full.at[event, at, halves[h]]
        return pltpu.make_async_remote_copy(
            src_ref=ref, dst_ref=ref, send_sem=sems[0].at[slot], recv_sem=sems[1].at[slot],
            device_id=target, device_id_type=MESH,
        )

    def to_line(h, source, peer):
        ref = full.at[ev, device(source, low), halves[h]]
        return pltpu.make_async_remote_copy(
            src_ref=ref, dst_ref=ref, send_sem=az_send.at[h, peer], recv_sem=az_recv.at[h, source],
            device_id={"basin": device(peer, low)}, device_id_type=MESH,
        )

    def to_pair(h, z, parity):
        return move(ev, device(z, parity), h, (ax_send.at[h], ax_recv.at[h]), z, {"basin": pair})

    def to_half(h, event, z):
        return move(event, device(z, low), h, (ay_send.at[h], ay_recv.at[h]), z, {"event": half})

    def on_half(event, z):
        return move(event, device(z, 1 - low), 0, (fa_send, fa_recv), z, {"event": half})

    def on_pair(z, parity):
        return move(half, device(z, parity), 1, (fb_send, fb_recv), z, {"basin": pair})

    def to_twin(side, event, z):
        ref = full.at[event, pl.ds(2 * z, 2)]
        return pltpu.make_async_remote_copy(
            src_ref=ref, dst_ref=ref, send_sem=tw_send.at[side, z], recv_sem=tw_recv.at[side, z],
            device_id={"event": twin}, device_id_type=MESH,
        )

    def own(h):
        def go():
            total = rs_pair[spot, halves[h]]
            if line <= 4:
                for j in range(1, line):
                    sender = near(j)
                    line_sum(h, spot, sender).wait_recv()
                    total = total + rs_line[sender, halves[h]]
            else:

                def add(i, total):
                    sender = lax.rem(spot + line - i, line)
                    line_sum(h, spot, sender).wait_recv()
                    return total + rs_line[sender, halves[h]]

                total = lax.fori_loop(1, line, add, total)
            full[ev, me, halves[h]] = total
            each(1, line, lambda j: to_line(h, spot, near(j)).start())
            to_pair(h, spot, low).start()
            to_half(h, ev, spot).start()

        when_owner(me, go)

    def from_line(h, j):
        z = near(j)

        def go():
            to_line(h, z, spot).wait_recv()
            to_pair(h, z, low).start()
            to_half(h, ev, z).start()

        when_owner(device(z, low), go)

    def hop(h, j):
        z = near(j)

        def go():
            if h == 0:
                to_pair(0, z, 1 - low).wait_recv()
                on_half(ev, z).start()
            else:
                to_half(1, half, z).wait_recv()
                on_pair(z, low).start()

        when_owner(2 * z, go)

    def corner(j):
        z = near(j)

        def go():
            to_pair(1, z, 1 - low).wait_recv()
            to_twin(0, ev, z).start()
            to_half(0, half, z).wait_recv()
            on_half(half, z).wait_recv()
            on_pair(z, 1 - low).wait_recv()
            to_twin(1, half, z).start()

        when_owner(2 * z, go)

    if line == 4:
        for j in range(line):
            add_pair(0, j)
        add_pair(1, 0)
        add_pair(1, 1)
        own(0)
        add_pair(1, 2)
        add_pair(1, 3)
        hop(0, 0)
        from_line(0, 1)
        own(1)
        for work, h, j in (
            (from_line, 0, 2), (from_line, 0, 3), (hop, 0, 1), (hop, 1, 0), (from_line, 1, 1),
            (hop, 0, 2), (from_line, 1, 2), (hop, 0, 3), (from_line, 1, 3), (hop, 1, 1),
            (hop, 1, 2), (hop, 1, 3),
        ):
            work(h, j)
    else:
        for h in range(2):
            each(0, line, functools.partial(add_pair, h))
        for h in range(2):
            own(h)
        for h in range(2):
            each(1, line, functools.partial(from_line, h))
        for h in range(2):
            each(0, line, functools.partial(hop, h))
    each(0, line, corner)

    def drain(z):
        for h in range(2):
            when_owner(device(z, 1 - low), lambda: pair_sum(h, z, 1 - low).wait_send())

            @pl.when(z != spot)
            def _():
                when_owner(device(z, low), lambda: line_sum(h, z, spot).wait_send())
                when_owner(me, lambda: to_line(h, spot, z).wait_send())

        def go():
            for h in range(2):
                to_pair(h, z, low).wait_send()
                to_half(h, ev, z).wait_send()
            on_half(ev, z).wait_send()
            on_pair(z, low).wait_send()
            to_twin(0, ev, z).wait_send()
            to_twin(1, half, z).wait_send()

        when_owner(2 * z, go)

    def write_full(z):
        where = pl.ds(2 * z, 2)
        return pltpu.make_async_copy(full.at[:, where], full_h.at[:, where], write_sem.at[z])

    def arrive(j):
        z = near(j)

        def go():
            to_twin(0, twin, z).wait_recv()
            to_twin(1, twin_half, z).wait_recv()
            write_full(z).start()

        when_owner(2 * z, go)

    each(0, line, arrive)
    each(0, line, drain)
    each(0, line, lambda j: when_owner(2 * near(j), lambda: write_full(near(j)).wait()))


def finish(
    feat, full_in, flow_in, lateral_in,
    large, flow_out, lateral_out, w_first, b_first, b_second, w_out,
    full, flow, lateral, small, vectors, sems, small_sems,
):
    last = full.shape[2] - 1
    middle = full.shape[0] // 2
    steps = []
    for side in range(2):
        where = pl.ds(side * middle, middle)
        steps.append((full_in.at[where], full.at[where], full.at[where, :, pl.ds(0, last)], large.at[where]))
    steps.append((lateral_in, lateral, lateral, lateral_out))
    steps.append((flow_in, flow, flow, flow_out))
    reads = [pltpu.make_async_copy(x[0], x[1], sems.at[0, i]) for i, x in enumerate(steps)]
    copies = [pltpu.make_async_copy(x[2], x[3], sems.at[1, i]) for i, x in enumerate(steps)]
    for read in reads:
        read.start()
    for read, copy in zip(reads, copies):
        read.wait()
        copy.start()
    n_event = full.shape[0]
    first_half = lax.broadcasted_iota(jnp.int32, (8, 128), 1) < 64
    for k in range(5):
        columns = []
        for e in range(0, n_event, 2):
            tails = []
            for s in range(2):
                tail = full[e + s, 5 + k // 2, last]
                tails.append(pltpu.roll(tail, 64, 1) if k % 2 != s else tail)
            turned = pltpu.roll(full[e + 1, k, last], 64, 1)
            columns += [
                full[e, k, last],
                jnp.where(first_half, tails[0], turned),
                jnp.where(first_half, turned, tails[1]),
            ]
        rows = jnp.concatenate(columns, axis=1)
        if k < 4:
            small[8 * k : 8 * k + 8, :] = rows
        else:
            for i, held in enumerate(vectors):
                held[...] = rows[i : i + 1].reshape(rows.shape[1])
    pairs = [(small, w_first)] + list(zip(vectors, (b_first, b_second, w_out)))
    for i, (held, target) in enumerate(pairs):
        copies.append(pltpu.make_async_copy(held, target, small_sems.at[i]))
        copies[-1].start()
    for copy in copies:
        copy.wait()


def body(
    n,
    n_event,
    reach_attrs,
    w_first,
    b_first,
    w_second,
    b_second,
    w_out,
    section_factor,
    bed_slope,
    seg_count,
    section_class,
    down_local,
    send_list,
    recv_list,
    area_start,
    lateral,
    cotangent,
):
    f32, bf16 = jnp.float32, jnp.bfloat16
    events, reaches = area_start.shape
    feat, hid = w_first.shape
    part = hid // n_event
    owners = n if part % (8 * n) == 0 else part // 8
    chunk = part // owners
    span = (chunk // 8) * (hid // 128) + 1
    line = n // 2
    scale = 32.0 / math.sqrt(events * n_event * reaches * n)
    vmem = pl.BlockSpec(memory_space=pltpu.VMEM)
    hbm = pl.BlockSpec(memory_space=pltpu.HBM)
    smem = pl.BlockSpec(memory_space=pltpu.SMEM)
    dma = pltpu.SemaphoreType.DMA
    held = lambda x: pltpu.VMEM(x.shape, x.dtype)
    outflow, grad_lateral, full = pl.pallas_call(
        functools.partial(kernel, n, n_event, owners, chunk, scale),
        out_shape=(
            jax.ShapeDtypeStruct((events, reaches), f32),
            jax.ShapeDtypeStruct((STEPS, events, reaches), f32),
            jax.ShapeDtypeStruct((n_event, owners, span, 8, 128), f32),
        ),
        in_specs=[hbm] * 6 + [smem] + [hbm] * 9,
        out_specs=(hbm,) * 3,
        scratch_shapes=[
            pltpu.VMEM((events, reaches), f32),
            pltpu.VMEM((STEPS, events, reaches), f32),
            pltpu.VMEM((n_event, owners, span, 8, 128), f32),
            dma((2,)),
            pltpu.VMEM((PLACES, reaches), bf16),
            held(w_first), held(b_first), held(w_second), held(b_second), held(w_out),
            held(bed_slope), held(seg_count), held(section_class), held(down_local),
            held(send_list), held(recv_list), held(area_start), held(lateral), held(cotangent),
            dma((15,)),
            pltpu.VMEM((hid, feat), bf16),
            pltpu.VMEM((hid, hid), bf16),
            pltpu.VMEM((hid, 8), f32),
            pltpu.VMEM((hid, reaches), f32),
            pltpu.VMEM((hid, reaches), bf16),
            pltpu.VMEM((hid, reaches), bf16),
            pltpu.VMEM((hid, reaches), bf16),
            pltpu.VMEM((part, reaches), f32),
            pltpu.VMEM((n_event, 1, reaches // n_event), f32),
            pltpu.VMEM((LINKS * GROUP, reaches), bf16),
            pltpu.VMEM((LINKS * GROUP, reaches), bf16),
            pltpu.VMEM((LINKS * GROUP, LINKS * GROUP), bf16),
            pltpu.VMEM((HALO + 1, LINKS, 8, 128), f32),
            pltpu.VMEM((HALO + 1, LINKS, 8, 128), f32),
            pltpu.VMEM((1, LINKS * GROUP), f32),
            pltpu.VMEM((LINKS, n_event, 1, LINKS * GROUP), f32),
            dma((LINKS, n_event)),
            dma((LINKS, n_event)),
            pltpu.VMEM((1, reaches), f32),
            pltpu.VMEM((n_event - 1, 1, reaches), f32),
            pltpu.VMEM((owners, span, 8, 128), f32),
            pltpu.VMEM((line, span, 8, 128), f32),
            pltpu.VMEM((line, span, 8, 128), f32),
            dma((n_event - 1,)), dma((n_event - 1,)),
            dma((HALO + 1, LINKS)), dma((HALO + 1, LINKS)),
            dma((n_event - 1,)), dma((n_event - 1,)),
            dma((2, line)), dma((2, line)), dma((2, line)), dma((2, line)),
            dma((2, line)), dma((2, line)), dma((2, line)), dma((2, line)),
            dma((2, line)), dma((2, line)),
            dma((line,)), dma((line,)), dma((line,)), dma((line,)), dma((2, line)), dma((2, line)),
            dma((line,)),
        ],
        compiler_params=pltpu.CompilerParams(
            collective_id=0, has_side_effects=True, vmem_limit_bytes=63 * 1024 * 1024
        ),
    )(
        reach_attrs.T, w_first, b_first, w_second, b_second, w_out, section_factor,
        bed_slope, seg_count, section_class, down_local, send_list, recv_list,
        area_start, lateral, cotangent,
    )
    vector = jax.ShapeDtypeStruct((hid,), f32)
    w_first_f32 = jax.ShapeDtypeStruct((feat, hid), f32)
    large, outflow, grad_lateral, g_first, g_b_first, g_b_second, g_out = pl.pallas_call(
        functools.partial(finish, feat),
        out_shape=(
            jax.ShapeDtypeStruct((n_event, owners, span - 1, 8, 128), f32),
            jax.ShapeDtypeStruct((events, reaches), f32),
            jax.ShapeDtypeStruct((STEPS, events, reaches), f32),
            w_first_f32,
            vector,
            vector,
            vector,
        ),
        in_specs=[hbm] * 3,
        out_specs=(hbm,) * 7,
        scratch_shapes=[
            held(full), held(outflow), held(grad_lateral),
            held(w_first_f32), [held(vector)] * 3, dma((2, 4)), dma((4,)),
        ],
    )(full, outflow, grad_lateral)
    g_second = large.reshape(hid // 8, hid // 128, 8, 128).transpose(0, 2, 1, 3).reshape(hid, hid)
    return outflow, grad_lateral, g_first, g_b_first, g_second, g_b_second, g_out


def solution(mesh):
    return jax.shard_map(
        functools.partial(body, mesh.shape["basin"], mesh.shape["event"]),
        mesh=mesh,
        in_specs=(
            P("basin", None),
            P(),
            P(),
            P(),
            P(),
            P(),
            P(),
            P("basin"),
            P("basin"),
            P("basin"),
            P("basin"),
            P("basin", None, None),
            P("basin", None, None),
            P("event", "basin"),
            P(None, "event", "basin"),
            P("event", "basin"),
        ),
        out_specs=(P("event", "basin"), P(None, "event", "basin"), P(), P(), P(), P(), P()),
        check_vma=False,
    )
```

```python
import functools
import math

import jax
import jax.numpy as jnp
from jax import lax
from jax.experimental import pallas as pl
from jax.experimental.pallas import tpu as pltpu
from jax.sharding import PartitionSpec as P

STEPS = 3
TINY = 1e-30
HALO = 2 * STEPS
LINKS = 4
GROUP = 32
PLACES = 48
MESH = pl.DeviceIdType.MESH
NT = (((1,), (1,)), ((), ()))
NN = (((1,), (0,)), ((), ()))


def split_two(x):
    high = x.astype(jnp.bfloat16)
    low = (x - high.astype(jnp.float32)).astype(jnp.bfloat16)
    return jnp.concatenate([high, low], axis=0)


def kernel(
    n, n_event, owners, chunk, scale,
    attrs_h, w_first_h, b_first_h, w_second_h, b_second_h, w_out_h, section_factor,
    bed_slope_h, seg_count_h, section_class_h, down_local_h, send_list_h, recv_list_h,
    area_start_h, lateral_h, cotangent_h,
    outflow_h, grad_lateral_h, full_h,
    outflow, grad_lateral, full, out_sem,
    attrs, w_first, b_first, w_second, b_second, w_out,
    bed_slope, seg_count, section_class, down_local, send_list, recv_list,
    area_start, lateral, cotangent, load_sem,
    w_firstT, w_secondT, cols,
    t_one, h_one, d_two, h_two, lower, squash_all, take_send, take_recv, overlap,
    out_msg, in_msg, share_out, share_in, share_send, share_recv, rate_out, rate_in, slab, rs_pair, rs_line,
    s_send, s_recv,
    x_send, x_recv, r_send, r_recv, px_send, px_recv, pz_send, pz_recv,
    az_send, az_recv, ax_send, ax_recv, ay_send, ay_recv,
    fa_send, fa_recv, fb_send, fb_recv, tw_send, tw_recv, write_sem,
):
    f32, bf16 = jnp.float32, jnp.bfloat16
    me = lax.axis_index("basin")
    ev = lax.axis_index("event")
    events, reaches = area_start.shape
    hid = w_second.shape[0]
    feat = w_first.shape[0]
    part = hid // n_event
    offsets = (1, 2, n // 2, n - 1)
    base = pl.multiple_of(ev * part, 64)
    mine = pl.ds(base, part)
    width = reaches // n_event

    barrier = pltpu.get_barrier_semaphore()

    def greet(offset):
        pl.semaphore_signal(
            barrier, inc=1, device_id={"basin": lax.rem(me + offset, n)}, device_id_type=MESH
        )

    greet(1)
    greet(n - 1)
    if n <= 8:
        for i in range(1, n // 2):
            greet(2 * i)
    else:
        pl.loop(1, n // 2)(lambda i: greet(2 * i))

    for i in range(1, n_event):
        pl.semaphore_signal(
            barrier, inc=1, device_id={"event": lax.rem(ev + i, n_event)}, device_id_type=MESH
        )

    loads = {}
    for name, source, target in (
        ("send_list", send_list_h, send_list),
        ("attrs", attrs_h, attrs.at[pl.ds(0, feat)]),
        ("area_start", area_start_h, area_start),
        ("bed_slope", bed_slope_h, bed_slope),
        ("section_class", section_class_h, section_class),
        ("w_second", w_second_h, w_second),
        ("w_first", w_first_h, w_first),
        ("b_first", b_first_h, b_first),
        ("b_second", b_second_h, b_second),
        ("w_out", w_out_h, w_out),
    ):
        loads[name] = pltpu.make_async_copy(source, target, load_sem.at[len(loads)])
        loads[name].start()

    for name in ("send_list", "attrs", "area_start", "bed_slope", "section_class"):
        loads[name].wait()

    extra = attrs.shape[0] - feat
    attrs[feat:, :] = jnp.where(
        lax.broadcasted_iota(jnp.int32, (extra, reaches), 0) == 0, 1.0, 0.0
    ).astype(bf16)
    slot_row = lax.broadcasted_iota(jnp.int32, (LINKS * GROUP, 1), 0)
    slot = slot_row % GROUP
    cap = send_list.shape[2]
    spread = (
        slot == lax.broadcasted_iota(jnp.int32, (LINKS * GROUP, cap), 1)
    ).astype(f32)
    lane_reach = lax.broadcasted_iota(jnp.int32, (LINKS * GROUP, reaches), 1).astype(f32)
    lane_basin = lax.broadcasted_iota(jnp.int32, (LINKS * GROUP, n), 1)

    def one_hot_of(lists, sign):
        table = lax.dot_general(
            spread, lists[0].astype(f32), NT, precision=lax.Precision.HIGHEST,
            preferred_element_type=f32,
        )
        peer = jnp.zeros((LINKS * GROUP, 1), jnp.int32)
        for k, off in enumerate(offsets):
            peer = jnp.where(slot_row // GROUP == k, lax.rem(me + sign * off + n, n), peer)
        column = jnp.sum(jnp.where(lane_basin == peer, table, 0.0), axis=1, keepdims=True)
        column = jnp.where(slot < cap, column, float(reaches))
        return (jnp.abs(lane_reach - column) < 0.5).astype(bf16)


    take_send[...] = one_hot_of(send_list, 1)

    kind = section_class[...].reshape(1, reaches)
    conveyance = jnp.zeros((1, reaches), f32)
    for c in range(section_factor.shape[0]):
        conveyance = jnp.where(kind == c, section_factor[c], conveyance)
    k_base = jnp.sqrt(bed_slope[...].reshape(1, reaches)) * conveyance
    lane_group = lax.broadcasted_iota(jnp.int32, (8, 128), 1) // GROUP
    blocks = events // 8

    def message(index, k, sign):
        return pltpu.make_async_remote_copy(
            src_ref=out_msg.at[index, k],
            dst_ref=in_msg.at[index, k],
            send_sem=x_send.at[index, k],
            recv_sem=x_recv.at[index, k],
            device_id={"basin": lax.rem(me + sign * offsets[k] + n, n)},
            device_id_type=MESH,
        )

    def pick(fields, matrix):
        rows = fields[0].shape[0]
        both = lax.dot_general(
            jnp.concatenate([split_two(field) for field in fields], axis=0), matrix[...], NT,
            preferred_element_type=f32,
        )
        return [
            both[2 * rows * i : 2 * rows * i + rows] + both[2 * rows * i + rows : 2 * rows * (i + 1)]
            for i in range(len(fields))
        ]

    def send(index, picked, sign):
        for k in range(LINKS):
            packed = jnp.zeros((8, 128), f32)
            for q in range(blocks):
                piece = picked[8 * q : 8 * q + 8]
                shift = ((q - k) * GROUP) % 128
                if shift:
                    piece = pltpu.roll(piece, shift, 1)
                packed = jnp.where(lane_group == q, piece, packed)
            out_msg[index, k] = packed
            message(index, k, sign).start()

    def receive(index, sign):
        for k in range(LINKS):
            message(index, k, sign).wait_recv()
        pieces = []
        for q in range(blocks):
            got = jnp.zeros((8, 128), f32)
            for k in range(LINKS):
                piece = in_msg[index, k]
                shift = ((k - q) * GROUP) % 128
                if shift:
                    piece = pltpu.roll(piece, shift, 1)
                got = jnp.where(lane_group == k, piece, got)
            pieces.append(got)
        return jnp.concatenate(pieces, axis=0)

    def scatter(got, matrix):
        both = jnp.dot(split_two(got), matrix[...], preferred_element_type=f32)
        rows = got.shape[0]
        return both[:rows] + both[rows:]

    def cross(got, dims):
        both = lax.dot_general(split_two(got), overlap[...], dims, preferred_element_type=f32)
        return both[:events] + both[events:]

    def power(area):
        return jnp.exp((2.0 / 3.0) * jnp.log(area))

    def slot_power(area):
        return power(jnp.maximum(area, TINY))


    areas = [area_start[...]]
    powers = [power(areas[0])]
    plain = areas[0] * powers[0]
    outer = pick([k_base * plain], take_send)[0]
    inputs = lax.dot_general(attrs[0:feat, :], take_send[...], NT, preferred_element_type=f32)

    pl.semaphore_wait(barrier, n // 2 + 1 + n_event - 1)
    send(HALO, inputs, 1)
    send(0, outer, 1)
    for name, source, target in (
        ("recv_list", recv_list_h, recv_list),
        ("seg_count", seg_count_h, seg_count),
        ("down_local", down_local_h, down_local),
        ("lateral", lateral_h, lateral),
        ("cotangent", cotangent_h, cotangent),
    ):
        loads[name] = pltpu.make_async_copy(source, target, load_sem.at[len(loads)])
        loads[name].start()

    for name in ("w_first", "b_first", "b_second", "w_out", "w_second"):
        loads[name].wait()

    w_firstT[...] = jnp.transpose(w_first[...])
    w_secondT[...] = jnp.transpose(w_second[...])
    w_out_row = w_out[...].astype(f32).reshape(1, hid)
    cols[...] = jnp.transpose(jnp.concatenate(
        [b_first[...].reshape(1, hid), b_second[...].reshape(1, hid), w_out_row,
         jnp.zeros((5, hid), f32)], axis=0
    ))
    w_out_rows = jnp.broadcast_to(w_out_row, (16, hid)).astype(bf16)

    def network(start, length):
        where = pl.ds(pl.multiple_of(start * 128, 128), length)
        one = jnp.tanh(
            jnp.dot(w_firstT[...], attrs[0:feat, where], preferred_element_type=f32) + cols[:, 0:1]
        )
        t_one[:, where] = one
        hidden = one.astype(bf16)
        h_one[:, where] = hidden
        two = jnp.tanh(
            jnp.dot(w_secondT[...], hidden, preferred_element_type=f32) + cols[:, 1:2]
        )
        rounded = two.astype(bf16)
        h_two[:, where] = rounded
        factor = (cols[:, 2:3] * (1.0 - two * two)).astype(bf16)
        d_two[:, where] = factor
        first = t_one[mine, where]
        lower[:, where] = (
            jnp.dot(w_second[mine, :], factor, preferred_element_type=f32) * (1.0 - first * first)
        )
        return rounded

    logit = jnp.dot(w_out_rows, network(ev * (width // 128), width), preferred_element_type=f32)[0:1]
    squash_all[ev] = 1.0 / (1.0 + jnp.exp(-logit))

    def squash_copy(i):
        return pltpu.make_async_remote_copy(
            src_ref=squash_all.at[ev],
            dst_ref=squash_all.at[ev],
            send_sem=s_send.at[i],
            recv_sem=s_recv.at[i],
            device_id={"event": lax.rem(ev + 1 + i, n_event)},
            device_id_type=MESH,
        )

    for i in range(n_event - 1):
        squash_copy(i).start()

    for name in ("recv_list", "seg_count", "down_local", "lateral"):
        loads[name].wait()
    take_recv[...] = one_hot_of(recv_list, -1)
    overlap[...] = lax.dot_general(
        take_send[...], take_recv[...], NT, preferred_element_type=f32
    ).astype(bf16)
    beta = 1.0 / seg_count[...].reshape(1, reaches).astype(f32)
    down = down_local[...].reshape(1, reaches)
    hop = jnp.where(down < reaches, down - lax.broadcasted_iota(jnp.int32, (1, reaches), 1), 0)
    masks = [(hop == d).astype(f32) for d in range(1, 9)]


    def hidden_of(weight, x, column):
        return jnp.tanh(
            jnp.dot(weight[...], x, preferred_element_type=f32) + cols[:, column : column + 1]
        ).astype(bf16)

    around = receive(HALO, 1).astype(bf16)
    around = hidden_of(w_secondT, hidden_of(w_firstT, around, 0), 1)
    around = jnp.dot(w_out_rows, around, preferred_element_type=f32)[0:1]
    got = receive(0, 1) / (0.02 + 0.08 * (1.0 / (1.0 + jnp.exp(-around))))

    units = reaches // 128
    begin = (ev + 1) * (width // 128)
    odd = lax.rem(begin, 2)
    pieces_left = [(lax.rem(begin + odd + 2 * i, units), 256) for i in range(4)]
    pieces_left.append((lax.rem(begin + 8 * (1 - odd), units), 128))

    for i in range(n_event - 1):
        squash_copy(i).wait_recv()
    squash = jnp.concatenate([squash_all[e] for e in range(n_event)], axis=1)
    rough = 0.02 + 0.08 * squash
    rate = k_base / rough
    slot_rate = pick([jnp.broadcast_to(rate, (16, reaches))], take_send)[0][0:1]
    first_got = got

    def share(k, e):
        return pltpu.make_async_remote_copy(
            src_ref=share_out,
            dst_ref=share_in.at[k, ev],
            send_sem=share_send.at[k, e],
            recv_sem=share_recv.at[k, ev],
            device_id={"basin": lax.rem(me + n - offsets[k], n), "event": e},
            device_id_type=MESH,
        )

    def shared_from(k, e):
        return pltpu.make_async_remote_copy(
            src_ref=share_out,
            dst_ref=share_in.at[k, e],
            send_sem=share_send.at[k, e],
            recv_sem=share_recv.at[k, e],
            device_id={"basin": lax.rem(me + n - offsets[k], n), "event": e},
            device_id_type=MESH,
        )

    shrinks = []
    for t in range(STEPS):
        area, p = areas[t], powers[t]
        flow = rate * area * p
        inflow = lateral[t]
        for d in range(1, 9):
            inflow = inflow + pltpu.roll(flow * masks[d - 1], d, 1)
        shrink = 1.0 / (1.0 + beta * rate * p)
        shrinks.append(shrink)
        kept = (area + beta * inflow) * shrink
        gain = beta * shrink
        if t < STEPS - 1:
            slots = pick([kept, gain], take_send)
        else:
            loads["cotangent"].wait()
            weight = cotangent[...] * rate * (5.0 / 3.0) * gain
            slots = pick([kept, gain, weight], take_recv)
        if t > 0:
            network(*pieces_left.pop(0))
            got = receive(t, 1)
        if t < STEPS - 1:
            slot_area = slots[0] + slots[1] * cross(got, NT)
            send(t + 1, slot_rate * slot_area * slot_power(slot_area), 1)
        else:
            slot_area = slots[0] + slots[1] * got
            send(STEPS, slots[2] * slot_power(slot_area), -1)
        areas.append(kept + gain * scatter(got, take_recv))
        powers.append(power(areas[t + 1]))
    emitted = areas[STEPS] * powers[STEPS]
    outflow[...] = rate * emitted
    write_flow = pltpu.make_async_copy(outflow, outflow_h, out_sem.at[0])
    write_flow.start()
    g_area = cotangent[...] * rate * (5.0 / 3.0) * powers[STEPS]
    g_rate = cotangent[...] * emitted
    for t in reversed(range(STEPS)):
        index = 2 * STEPS - 1 - t
        inner = g_area * shrinks[t]
        g_inflow = inner * beta
        grad_lateral[t] = g_inflow
        g_flow = jnp.zeros((events, reaches), f32)
        for d in range(1, 9):
            g_flow = g_flow + masks[d - 1] * pltpu.roll(g_inflow, reaches - d, 1)
        drop = g_inflow * areas[t + 1] * powers[t]
        g_rate = g_rate - drop + g_flow * areas[t] * powers[t]
        if t > 0:
            lean = (5.0 / 3.0) * rate * powers[t]
            onward = inner - (2.0 / 3.0) * rate * drop / areas[t] + lean * g_flow
            gain = beta * shrinks[t - 1]
            slots = pick([onward * gain, lean * gain], take_recv)
            network(*pieces_left.pop(0))
            got = receive(index, -1)
            onto = slots[0] + slots[1] * cross(got, NN)
            if t > 1:
                send(index + 1, onto, -1)
            else:
                share_out[...] = jnp.sum(onto * first_got, axis=0, keepdims=True)
                for k in range(LINKS):
                    for e in range(n_event):
                        share(k, e).start()
            back = scatter(got, take_send)
            g_rate = g_rate + back * areas[t] * powers[t]
            g_area = onward + lean * back
    write_lateral = pltpu.make_async_copy(grad_lateral, grad_lateral_h, out_sem.at[1])
    write_lateral.start()
    rate_out[...] = jnp.sum(g_rate, axis=0, keepdims=True)

    def rate_copy(i):
        return pltpu.make_async_remote_copy(
            src_ref=rate_out,
            dst_ref=rate_in.at[i],
            send_sem=r_send.at[i],
            recv_sem=r_recv.at[i],
            device_id={"event": lax.rem(ev + 1 + i, n_event)},
            device_id_type=MESH,
        )

    for i in range(n_event - 1):
        rate_copy(i).start()
    network(*pieces_left.pop(0))
    for i in range(n_event - 1):
        rate_copy(i).wait_recv()
    slot_group = lax.broadcasted_iota(jnp.int32, (1, LINKS * GROUP), 1) // GROUP
    shares = jnp.zeros((1, LINKS * GROUP), f32)
    for k in range(LINKS):
        for e in range(n_event):
            shared_from(k, e).wait_recv()
        total = share_in[k, 0]
        for e in range(1, n_event):
            total = total + share_in[k, e]
        shares = jnp.where(slot_group == k, total, shares)
    shared = scatter(jnp.broadcast_to(shares, (16, LINKS * GROUP)), take_send)[0:1] / rate
    terms = [rate_out[...]] + [rate_in[i] for i in range(n_event - 1)]
    g_sum = jnp.zeros((1, reaches), f32)
    for e in range(n_event):
        term = terms[0]
        for i in range(n_event - 1):
            term = jnp.where(lax.rem(e + 1 + i, n_event) == ev, terms[i + 1], term)
        g_sum = g_sum + term
    g_sum = g_sum + shared
    g_logit = (
        g_sum * (-rate / rough) * (scale * 0.08) * squash * (1.0 - squash)
    ).astype(bf16)
    g_logit32 = g_logit.astype(f32)

    scaled = (h_one[mine, :].astype(f32) * g_logit32).astype(bf16)
    large = lax.dot_general(scaled, d_two[...], NT, preferred_element_type=f32)
    tiles = hid // 128
    for d in range(owners):
        for r in range(chunk // 8):
            for c in range(tiles):
                top = d * chunk + 8 * r
                slab[d, r * tiles + c] = large[top : top + 8, 128 * c : 128 * c + 128]

    def when_owner(index, work):
        if owners == n:
            work()
        else:
            pl.when(index < owners)(work)

    line = n // 2
    low = lax.rem(me, 2)
    spot = me // 2
    pair = me + 1 - 2 * low
    half = lax.rem(ev + n_event // 2, n_event)
    twin = ev + 1 - 2 * lax.rem(ev, 2)
    twin_half = lax.rem(twin + n_event // 2, n_event)
    span = slab.shape[1]
    cut = (span + 1) // 2
    halves = (pl.ds(0, cut), pl.ds(cut, span - cut))

    def each(first, last, work):
        if last - first <= 4:
            for j in range(first, last):
                work(j)
        else:
            pl.loop(first, last)(work)

    def near(j):
        if line != 4:
            return lax.rem(spot + j, line)
        if isinstance(j, int) and j == 0:
            return spot
        orders = ((1, 2, 3), (2, 0, 3), (1, 3, 0), (2, 1, 0))
        code = sum(orders[s][j - 1] * 4 ** s for s in range(4))
        power_of = (1 + 3 * lax.rem(spot, 2)) * (1 + 15 * (spot // 2))
        return lax.rem(code // power_of, 4)

    def device(z, parity):
        return 2 * z + parity

    def pair_sum(h, z, parity):
        return pltpu.make_async_remote_copy(
            src_ref=slab.at[device(z, parity), halves[h]], dst_ref=rs_pair.at[z, halves[h]],
            send_sem=px_send.at[h, z], recv_sem=px_recv.at[h, z],
            device_id={"basin": pair}, device_id_type=MESH,
        )

    def line_sum(h, z, sender):
        return pltpu.make_async_remote_copy(
            src_ref=rs_pair.at[z, halves[h]], dst_ref=rs_line.at[sender, halves[h]],
            send_sem=pz_send.at[h, z], recv_sem=pz_recv.at[h, sender],
            device_id={"basin": device(z, low)}, device_id_type=MESH,
        )

    def far(j):
        return near(line - 1 - j)

    def start_pair(h, j):
        z = far(j)
        when_owner(device(z, 1 - low), lambda: pair_sum(h, z, 1 - low).start())

    each(0, line, functools.partial(start_pair, 0))

    g_pre = (lower[...] * g_logit32).astype(bf16)
    place = lax.broadcasted_iota(jnp.int32, (PLACES, reaches), 0)
    row_two = jnp.where(place == feat + 1, g_logit32, 0.0).astype(bf16)
    row_out = jnp.where(place == feat + 2, g_logit32, 0.0).astype(bf16)
    g_two = d_two[mine, :]
    second = h_two[mine, :]

    def narrow(first):
        end = first + 128
        return (
            lax.dot_general(attrs[...], g_pre[first:end], NT, preferred_element_type=f32)
            + lax.dot_general(row_two, g_two[first:end], NT, preferred_element_type=f32)
            + lax.dot_general(row_out, second[first:end], NT, preferred_element_type=f32)
        )

    left = narrow(0)
    right = narrow(part - 128)
    first_half = lax.broadcasted_iota(jnp.int32, (8, 128), 1) < 64
    last = slab.shape[1] - 1
    for k in range(5):
        slab[k, last] = left[8 * k : 8 * k + 8]
    for k in range(3):
        even = pltpu.roll(right[16 * k : 16 * k + 8], 64, 1)
        slab[5 + k, last] = jnp.where(first_half, even, right[16 * k + 8 : 16 * k + 16])
    for d in range(8, owners):
        slab[d, last] = jnp.zeros((8, 128), f32)

    each(0, line, functools.partial(start_pair, 1))

    for i in range(n_event - 1):
        squash_copy(i).wait_send()
    for index in range(HALO + 1):
        for k in range(LINKS):
            if index != 2 * STEPS - 1:
                message(index, k, 1).wait_send()
    for k in range(LINKS):
        for e in range(n_event):
            share(k, e).wait_send()
    for i in range(n_event - 1):
        rate_copy(i).wait_send()
    write_flow.wait()
    write_lateral.wait()

    def add_pair(h, j):
        z = far(j)

        def go():
            pair_sum(h, z, 1 - low).wait_recv()
            rs_pair[z, halves[h]] = rs_pair[z, halves[h]] + slab[device(z, low), halves[h]]

            @pl.when(z != spot)
            def _():
                line_sum(h, z, spot).start()

        when_owner(device(z, low), go)

    def move(event, at, h, sems, slot, target):
        ref = full.at[event, at, halves[h]]
        return pltpu.make_async_remote_copy(
            src_ref=ref, dst_ref=ref, send_sem=sems[0].at[slot], recv_sem=sems[1].at[slot],
            device_id=target, device_id_type=MESH,
        )

    def to_line(h, source, peer):
        ref = full.at[ev, device(source, low), halves[h]]
        return pltpu.make_async_remote_copy(
            src_ref=ref, dst_ref=ref, send_sem=az_send.at[h, peer], recv_sem=az_recv.at[h, source],
            device_id={"basin": device(peer, low)}, device_id_type=MESH,
        )

    def to_pair(h, z, parity):
        return move(ev, device(z, parity), h, (ax_send.at[h], ax_recv.at[h]), z, {"basin": pair})

    def to_half(h, event, z):
        return move(event, device(z, low), h, (ay_send.at[h], ay_recv.at[h]), z, {"event": half})

    def on_half(event, z):
        return move(event, device(z, 1 - low), 0, (fa_send, fa_recv), z, {"event": half})

    def on_half_two(event, z):
        return move(event, device(z, 1 - low), 1, (fb_send, fb_recv), z, {"event": half})

    def to_twin(side, event, z):
        ref = full.at[event, pl.ds(2 * z, 2)]
        return pltpu.make_async_remote_copy(
            src_ref=ref, dst_ref=ref, send_sem=tw_send.at[side, z], recv_sem=tw_recv.at[side, z],
            device_id={"event": twin}, device_id_type=MESH,
        )

    def own(h):
        def go():
            total = rs_pair[spot, halves[h]]
            if line <= 4:
                for j in range(1, line):
                    sender = near(j)
                    line_sum(h, spot, sender).wait_recv()
                    total = total + rs_line[sender, halves[h]]
            else:

                def add(i, total):
                    sender = lax.rem(spot + line - i, line)
                    line_sum(h, spot, sender).wait_recv()
                    return total + rs_line[sender, halves[h]]

                total = lax.fori_loop(1, line, add, total)
            full[ev, me, halves[h]] = total
            each(1, line, lambda j: to_line(h, spot, near(j)).start())
            to_pair(h, spot, low).start()
            to_half(h, ev, spot).start()

        when_owner(me, go)

    def from_line(h, j):
        z = near(j)

        def go():
            to_line(h, z, spot).wait_recv()
            to_pair(h, z, low).start()
            to_half(h, ev, z).start()

        when_owner(device(z, low), go)

    def hop(h, j):
        z = near(j)

        def go():
            if h == 0:
                to_pair(0, z, 1 - low).wait_recv()
                on_half(ev, z).start()
            else:
                to_pair(1, z, 1 - low).wait_recv()
                on_half_two(ev, z).start()

        when_owner(2 * z, go)

    def corner(j):
        z = near(j)

        def go():
            to_twin(0, ev, z).start()
            to_half(0, half, z).wait_recv()
            to_half(1, half, z).wait_recv()
            on_half(half, z).wait_recv()
            on_half_two(half, z).wait_recv()
            to_twin(1, half, z).start()

        when_owner(2 * z, go)

    if line == 4:
        for j in range(line):
            add_pair(0, j)
        add_pair(1, 0)
        add_pair(1, 1)
        own(0)
        add_pair(1, 2)
        add_pair(1, 3)
        hop(0, 0)
        from_line(0, 1)
        own(1)
        for work, h, j in (
            (from_line, 0, 2), (from_line, 0, 3), (hop, 0, 1), (hop, 1, 0), (from_line, 1, 1),
            (hop, 0, 2), (from_line, 1, 2), (hop, 0, 3), (from_line, 1, 3), (hop, 1, 1),
            (hop, 1, 2), (hop, 1, 3),
        ):
            work(h, j)
    else:
        for h in range(2):
            each(0, line, functools.partial(add_pair, h))
        for h in range(2):
            own(h)
        for h in range(2):
            each(1, line, functools.partial(from_line, h))
        for h in range(2):
            each(0, line, functools.partial(hop, h))
    def settle(z):
        for h in range(2):
            when_owner(device(z, 1 - low), lambda: pair_sum(h, z, 1 - low).wait_send())

            @pl.when(z != spot)
            def _():
                when_owner(device(z, low), lambda: line_sum(h, z, spot).wait_send())
                when_owner(me, lambda: to_line(h, spot, z).wait_send())

        def go():
            for h in range(2):
                to_pair(h, z, low).wait_send()
                to_half(h, ev, z).wait_send()

        when_owner(2 * z, go)

    def drain(z):
        def go():
            on_half(ev, z).wait_send()
            on_half_two(ev, z).wait_send()
            to_twin(0, ev, z).wait_send()
            to_twin(1, half, z).wait_send()

        when_owner(2 * z, go)

    each(0, line - 1, corner)
    each(0, line, settle)
    corner(line - 1)

    def write_full(z):
        where = pl.ds(2 * z, 2)
        return pltpu.make_async_copy(full.at[:, where], full_h.at[:, where], write_sem.at[z])

    def arrive(j):
        z = near(j)

        def go():
            to_twin(0, twin, z).wait_recv()
            to_twin(1, twin_half, z).wait_recv()
            write_full(z).start()

        when_owner(2 * z, go)

    each(0, line, arrive)
    each(0, line, drain)
    each(0, line, lambda j: when_owner(2 * near(j), lambda: write_full(near(j)).wait()))


def finish(
    feat, full_in, flow_in, lateral_in,
    large, flow_out, lateral_out, w_first, b_first, b_second, w_out,
    full, flow, lateral, small, vectors, sems, small_sems,
):
    last = full.shape[2] - 1
    steps = []
    for side in range(full.shape[0]):
        where = pl.ds(side, 1)
        steps.append((full_in.at[where], full.at[where], full.at[where, :, pl.ds(0, last)], large.at[where]))
    steps.append((lateral_in, lateral, lateral, lateral_out))
    steps.append((flow_in, flow, flow, flow_out))
    reads = [pltpu.make_async_copy(x[0], x[1], sems.at[0, i]) for i, x in enumerate(steps)]
    copies = [pltpu.make_async_copy(x[2], x[3], sems.at[1, i]) for i, x in enumerate(steps)]
    for read in reads:
        read.start()
    for read, copy in zip(reads, copies):
        read.wait()
        copy.start()
    n_event = full.shape[0]
    first_half = lax.broadcasted_iota(jnp.int32, (8, 128), 1) < 64
    for k in range(5):
        columns = []
        for e in range(0, n_event, 2):
            tails = []
            for s in range(2):
                tail = full[e + s, 5 + k // 2, last]
                tails.append(pltpu.roll(tail, 64, 1) if k % 2 != s else tail)
            turned = pltpu.roll(full[e + 1, k, last], 64, 1)
            columns += [
                full[e, k, last],
                jnp.where(first_half, tails[0], turned),
                jnp.where(first_half, turned, tails[1]),
            ]
        rows = jnp.concatenate(columns, axis=1)
        if k < 4:
            small[8 * k : 8 * k + 8, :] = rows
        else:
            for i, held in enumerate(vectors):
                held[...] = rows[i : i + 1].reshape(rows.shape[1])
    pairs = [(small, w_first)] + list(zip(vectors, (b_first, b_second, w_out)))
    for i, (held, target) in enumerate(pairs):
        copies.append(pltpu.make_async_copy(held, target, small_sems.at[i]))
        copies[-1].start()
    for copy in copies:
        copy.wait()


def body(
    n,
    n_event,
    reach_attrs,
    w_first,
    b_first,
    w_second,
    b_second,
    w_out,
    section_factor,
    bed_slope,
    seg_count,
    section_class,
    down_local,
    send_list,
    recv_list,
    area_start,
    lateral,
    cotangent,
):
    f32, bf16 = jnp.float32, jnp.bfloat16
    events, reaches = area_start.shape
    feat, hid = w_first.shape
    part = hid // n_event
    owners = n if part % (8 * n) == 0 else part // 8
    chunk = part // owners
    span = (chunk // 8) * (hid // 128) + 1
    line = n // 2
    scale = 32.0 / math.sqrt(events * n_event * reaches * n)
    vmem = pl.BlockSpec(memory_space=pltpu.VMEM)
    hbm = pl.BlockSpec(memory_space=pltpu.HBM)
    smem = pl.BlockSpec(memory_space=pltpu.SMEM)
    dma = pltpu.SemaphoreType.DMA
    held = lambda x: pltpu.VMEM(x.shape, x.dtype)
    outflow, grad_lateral, full = pl.pallas_call(
        functools.partial(kernel, n, n_event, owners, chunk, scale),
        out_shape=(
            jax.ShapeDtypeStruct((events, reaches), f32),
            jax.ShapeDtypeStruct((STEPS, events, reaches), f32),
            jax.ShapeDtypeStruct((n_event, owners, span, 8, 128), f32),
        ),
        in_specs=[hbm] * 6 + [smem] + [hbm] * 9,
        out_specs=(hbm,) * 3,
        scratch_shapes=[
            pltpu.VMEM((events, reaches), f32),
            pltpu.VMEM((STEPS, events, reaches), f32),
            pltpu.VMEM((n_event, owners, span, 8, 128), f32),
            dma((2,)),
            pltpu.VMEM((PLACES, reaches), bf16),
            held(w_first), held(b_first), held(w_second), held(b_second), held(w_out),
            held(bed_slope), held(seg_count), held(section_class), held(down_local),
            held(send_list), held(recv_list), held(area_start), held(lateral), held(cotangent),
            dma((15,)),
            pltpu.VMEM((hid, feat), bf16),
            pltpu.VMEM((hid, hid), bf16),
            pltpu.VMEM((hid, 8), f32),
            pltpu.VMEM((hid, reaches), f32),
            pltpu.VMEM((hid, reaches), bf16),
            pltpu.VMEM((hid, reaches), bf16),
            pltpu.VMEM((hid, reaches), bf16),
            pltpu.VMEM((part, reaches), f32),
            pltpu.VMEM((n_event, 1, reaches // n_event), f32),
            pltpu.VMEM((LINKS * GROUP, reaches), bf16),
            pltpu.VMEM((LINKS * GROUP, reaches), bf16),
            pltpu.VMEM((LINKS * GROUP, LINKS * GROUP), bf16),
            pltpu.VMEM((HALO + 1, LINKS, 8, 128), f32),
            pltpu.VMEM((HALO + 1, LINKS, 8, 128), f32),
            pltpu.VMEM((1, LINKS * GROUP), f32),
            pltpu.VMEM((LINKS, n_event, 1, LINKS * GROUP), f32),
            dma((LINKS, n_event)),
            dma((LINKS, n_event)),
            pltpu.VMEM((1, reaches), f32),
            pltpu.VMEM((n_event - 1, 1, reaches), f32),
            pltpu.VMEM((owners, span, 8, 128), f32),
            pltpu.VMEM((line, span, 8, 128), f32),
            pltpu.VMEM((line, span, 8, 128), f32),
            dma((n_event - 1,)), dma((n_event - 1,)),
            dma((HALO + 1, LINKS)), dma((HALO + 1, LINKS)),
            dma((n_event - 1,)), dma((n_event - 1,)),
            dma((2, line)), dma((2, line)), dma((2, line)), dma((2, line)),
            dma((2, line)), dma((2, line)), dma((2, line)), dma((2, line)),
            dma((2, line)), dma((2, line)),
            dma((line,)), dma((line,)), dma((line,)), dma((line,)), dma((2, line)), dma((2, line)),
            dma((line,)),
        ],
        compiler_params=pltpu.CompilerParams(
            collective_id=0, has_side_effects=True, vmem_limit_bytes=63 * 1024 * 1024
        ),
    )(
        reach_attrs.T, w_first, b_first, w_second, b_second, w_out, section_factor,
        bed_slope, seg_count, section_class, down_local, send_list, recv_list,
        area_start, lateral, cotangent,
    )
    vector = jax.ShapeDtypeStruct((hid,), f32)
    w_first_f32 = jax.ShapeDtypeStruct((feat, hid), f32)
    large, outflow, grad_lateral, g_first, g_b_first, g_b_second, g_out = pl.pallas_call(
        functools.partial(finish, feat),
        out_shape=(
            jax.ShapeDtypeStruct((n_event, owners, span - 1, 8, 128), f32),
            jax.ShapeDtypeStruct((events, reaches), f32),
            jax.ShapeDtypeStruct((STEPS, events, reaches), f32),
            w_first_f32,
            vector,
            vector,
            vector,
        ),
        in_specs=[hbm] * 3,
        out_specs=(hbm,) * 7,
        scratch_shapes=[
            held(full), held(outflow), held(grad_lateral),
            held(w_first_f32), [held(vector)] * 3, dma((2, n_event + 2)), dma((4,)),
        ],
    )(full, outflow, grad_lateral)
    g_second = large.reshape(hid // 8, hid // 128, 8, 128).transpose(0, 2, 1, 3).reshape(hid, hid)
    return outflow, grad_lateral, g_first, g_b_first, g_second, g_b_second, g_out


def solution(mesh):
    return jax.shard_map(
        functools.partial(body, mesh.shape["basin"], mesh.shape["event"]),
        mesh=mesh,
        in_specs=(
            P("basin", None),
            P(),
            P(),
            P(),
            P(),
            P(),
            P(),
            P("basin"),
            P("basin"),
            P("basin"),
            P("basin"),
            P("basin", None, None),
            P("basin", None, None),
            P("event", "basin"),
            P(None, "event", "basin"),
            P("event", "basin"),
        ),
        out_specs=(P("event", "basin"), P(None, "event", "basin"), P(), P(), P(), P(), P()),
        check_vma=False,
    )
```

```python
import functools
import math

import jax
import jax.numpy as jnp
from jax import lax
from jax.experimental import pallas as pl
from jax.experimental.pallas import tpu as pltpu
from jax.sharding import PartitionSpec as P

STEPS = 3
TINY = 1e-30
HALO = 2 * STEPS
LINKS = 4
GROUP = 32
PLACES = 48
MESH = pl.DeviceIdType.MESH
NT = (((1,), (1,)), ((), ()))
NN = (((1,), (0,)), ((), ()))


def split_two(x):
    high = x.astype(jnp.bfloat16)
    low = (x - high.astype(jnp.float32)).astype(jnp.bfloat16)
    return jnp.concatenate([high, low], axis=0)


def kernel(
    n, n_event, owners, chunk, scale,
    attrs_h, w_first_h, b_first_h, w_second_h, b_second_h, w_out_h, section_factor,
    bed_slope_h, seg_count_h, section_class_h, down_local_h, send_list_h, recv_list_h,
    area_start_h, lateral_h, cotangent_h,
    outflow_h, grad_lateral_h, full_h,
    outflow, grad_lateral, full, out_sem,
    attrs, w_first, b_first, w_second, b_second, w_out,
    bed_slope, seg_count, section_class, down_local, send_list, recv_list,
    area_start, lateral, cotangent, load_sem,
    w_firstT, w_secondT, cols,
    t_one, h_one, d_two, h_two, lower, squash_all, take_send, take_recv, overlap,
    out_msg, in_msg, share_out, share_in, share_send, share_recv, rate_out, rate_in, slab, rs_pair, rs_line,
    s_send, s_recv,
    x_send, x_recv, r_send, r_recv, px_send, px_recv, pz_send, pz_recv,
    az_send, az_recv, ax_send, ax_recv, ay_send, ay_recv,
    fa_send, fa_recv, fb_send, fb_recv, tw_send, tw_recv, write_sem,
):
    f32, bf16 = jnp.float32, jnp.bfloat16
    me = lax.axis_index("basin")
    ev = lax.axis_index("event")
    events, reaches = area_start.shape
    hid = w_second.shape[0]
    feat = w_first.shape[0]
    part = hid // n_event
    offsets = (1, 2, n // 2, n - 1)
    base = pl.multiple_of(ev * part, 64)
    mine = pl.ds(base, part)
    width = reaches // n_event

    barrier = pltpu.get_barrier_semaphore()

    def greet(offset):
        pl.semaphore_signal(
            barrier, inc=1, device_id={"basin": lax.rem(me + offset, n)}, device_id_type=MESH
        )

    greet(1)
    greet(n - 1)
    if n <= 8:
        for i in range(1, n // 2):
            greet(2 * i)
    else:
        pl.loop(1, n // 2)(lambda i: greet(2 * i))

    for i in range(1, n_event):
        pl.semaphore_signal(
            barrier, inc=1, device_id={"event": lax.rem(ev + i, n_event)}, device_id_type=MESH
        )

    loads = {}
    for name, source, target in (
        ("send_list", send_list_h, send_list),
        ("attrs", attrs_h, attrs.at[pl.ds(0, feat)]),
        ("area_start", area_start_h, area_start),
        ("bed_slope", bed_slope_h, bed_slope),
        ("section_class", section_class_h, section_class),
        ("w_second", w_second_h, w_second),
        ("w_first", w_first_h, w_first),
        ("b_first", b_first_h, b_first),
        ("b_second", b_second_h, b_second),
        ("w_out", w_out_h, w_out),
    ):
        loads[name] = pltpu.make_async_copy(source, target, load_sem.at[len(loads)])
        loads[name].start()

    for name in ("send_list", "attrs", "area_start", "bed_slope", "section_class"):
        loads[name].wait()

    extra = attrs.shape[0] - feat
    attrs[feat:, :] = jnp.where(
        lax.broadcasted_iota(jnp.int32, (extra, reaches), 0) == 0, 1.0, 0.0
    ).astype(bf16)
    slot_row = lax.broadcasted_iota(jnp.int32, (LINKS * GROUP, 1), 0)
    slot = slot_row % GROUP
    cap = send_list.shape[2]
    spread = (
        slot == lax.broadcasted_iota(jnp.int32, (LINKS * GROUP, cap), 1)
    ).astype(f32)
    lane_reach = lax.broadcasted_iota(jnp.int32, (LINKS * GROUP, reaches), 1).astype(f32)
    lane_basin = lax.broadcasted_iota(jnp.int32, (LINKS * GROUP, n), 1)

    def one_hot_of(lists, sign):
        table = lax.dot_general(
            spread, lists[0].astype(f32), NT, precision=lax.Precision.HIGHEST,
            preferred_element_type=f32,
        )
        peer = jnp.zeros((LINKS * GROUP, 1), jnp.int32)
        for k, off in enumerate(offsets):
            peer = jnp.where(slot_row // GROUP == k, lax.rem(me + sign * off + n, n), peer)
        column = jnp.sum(jnp.where(lane_basin == peer, table, 0.0), axis=1, keepdims=True)
        column = jnp.where(slot < cap, column, float(reaches))
        return (jnp.abs(lane_reach - column) < 0.5).astype(bf16)


    take_send[...] = one_hot_of(send_list, 1)

    kind = section_class[...].reshape(1, reaches)
    conveyance = jnp.zeros((1, reaches), f32)
    for c in range(section_factor.shape[0]):
        conveyance = jnp.where(kind == c, section_factor[c], conveyance)
    k_base = jnp.sqrt(bed_slope[...].reshape(1, reaches)) * conveyance
    lane_group = lax.broadcasted_iota(jnp.int32, (8, 128), 1) // GROUP
    blocks = events // 8

    def message(index, k, sign):
        return pltpu.make_async_remote_copy(
            src_ref=out_msg.at[index, k],
            dst_ref=in_msg.at[index, k],
            send_sem=x_send.at[index, k],
            recv_sem=x_recv.at[index, k],
            device_id={"basin": lax.rem(me + sign * offsets[k] + n, n)},
            device_id_type=MESH,
        )

    def pick(fields, matrix):
        rows = fields[0].shape[0]
        both = lax.dot_general(
            jnp.concatenate([split_two(field) for field in fields], axis=0), matrix[...], NT,
            preferred_element_type=f32,
        )
        return [
            both[2 * rows * i : 2 * rows * i + rows] + both[2 * rows * i + rows : 2 * rows * (i + 1)]
            for i in range(len(fields))
        ]

    def send(index, picked, sign):
        for k in range(LINKS):
            packed = jnp.zeros((8, 128), f32)
            for q in range(blocks):
                piece = picked[8 * q : 8 * q + 8]
                shift = ((q - k) * GROUP) % 128
                if shift:
                    piece = pltpu.roll(piece, shift, 1)
                packed = jnp.where(lane_group == q, piece, packed)
            out_msg[index, k] = packed
            message(index, k, sign).start()

    def receive(index, sign):
        for k in range(LINKS):
            message(index, k, sign).wait_recv()
        pieces = []
        for q in range(blocks):
            got = jnp.zeros((8, 128), f32)
            for k in range(LINKS):
                piece = in_msg[index, k]
                shift = ((k - q) * GROUP) % 128
                if shift:
                    piece = pltpu.roll(piece, shift, 1)
                got = jnp.where(lane_group == k, piece, got)
            pieces.append(got)
        return jnp.concatenate(pieces, axis=0)

    def scatter(got, matrix):
        both = jnp.dot(split_two(got), matrix[...], preferred_element_type=f32)
        rows = got.shape[0]
        return both[:rows] + both[rows:]

    def cross(got, dims):
        both = lax.dot_general(split_two(got), overlap[...], dims, preferred_element_type=f32)
        return both[:events] + both[events:]

    def power(area):
        return jnp.exp((2.0 / 3.0) * jnp.log(area))

    def slot_power(area):
        return power(jnp.maximum(area, TINY))


    areas = [area_start[...]]
    powers = [power(areas[0])]
    plain = areas[0] * powers[0]
    outer = pick([k_base * plain], take_send)[0]
    inputs = lax.dot_general(attrs[0:feat, :], take_send[...], NT, preferred_element_type=f32)

    pl.semaphore_wait(barrier, n // 2 + 1 + n_event - 1)
    send(HALO, inputs, 1)
    send(0, outer, 1)
    for name, source, target in (
        ("recv_list", recv_list_h, recv_list),
        ("seg_count", seg_count_h, seg_count),
        ("down_local", down_local_h, down_local),
        ("lateral", lateral_h, lateral),
        ("cotangent", cotangent_h, cotangent),
    ):
        loads[name] = pltpu.make_async_copy(source, target, load_sem.at[len(loads)])
        loads[name].start()

    for name in ("w_first", "b_first", "b_second", "w_out", "w_second"):
        loads[name].wait()

    w_firstT[...] = jnp.transpose(w_first[...])
    w_secondT[...] = jnp.transpose(w_second[...])
    w_out_row = w_out[...].astype(f32).reshape(1, hid)
    cols[...] = jnp.transpose(jnp.concatenate(
        [b_first[...].reshape(1, hid), b_second[...].reshape(1, hid), w_out_row,
         jnp.zeros((5, hid), f32)], axis=0
    ))
    w_out_rows = jnp.broadcast_to(w_out_row, (16, hid)).astype(bf16)

    def network(start, length):
        where = pl.ds(pl.multiple_of(start * 128, 128), length)
        one = jnp.tanh(
            jnp.dot(w_firstT[...], attrs[0:feat, where], preferred_element_type=f32) + cols[:, 0:1]
        )
        t_one[:, where] = one
        hidden = one.astype(bf16)
        h_one[:, where] = hidden
        two = jnp.tanh(
            jnp.dot(w_secondT[...], hidden, preferred_element_type=f32) + cols[:, 1:2]
        )
        rounded = two.astype(bf16)
        h_two[:, where] = rounded
        factor = (cols[:, 2:3] * (1.0 - two * two)).astype(bf16)
        d_two[:, where] = factor
        first = t_one[mine, where]
        lower[:, where] = (
            jnp.dot(w_second[mine, :], factor, preferred_element_type=f32) * (1.0 - first * first)
        )
        return rounded

    logit = jnp.dot(w_out_rows, network(ev * (width // 128), width), preferred_element_type=f32)[0:1]
    squash_all[ev] = 1.0 / (1.0 + jnp.exp(-logit))

    def squash_copy(i):
        return pltpu.make_async_remote_copy(
            src_ref=squash_all.at[ev],
            dst_ref=squash_all.at[ev],
            send_sem=s_send.at[i],
            recv_sem=s_recv.at[i],
            device_id={"event": lax.rem(ev + 1 + i, n_event)},
            device_id_type=MESH,
        )

    for i in range(n_event - 1):
        squash_copy(i).start()

    for name in ("recv_list", "seg_count", "down_local", "lateral"):
        loads[name].wait()
    take_recv[...] = one_hot_of(recv_list, -1)
    overlap[...] = lax.dot_general(
        take_send[...], take_recv[...], NT, preferred_element_type=f32
    ).astype(bf16)
    beta = 1.0 / seg_count[...].reshape(1, reaches).astype(f32)
    down = down_local[...].reshape(1, reaches)
    hop = jnp.where(down < reaches, down - lax.broadcasted_iota(jnp.int32, (1, reaches), 1), 0)
    masks = [(hop == d).astype(f32) for d in range(1, 9)]


    def hidden_of(weight, x, column):
        return jnp.tanh(
            jnp.dot(weight[...], x, preferred_element_type=f32) + cols[:, column : column + 1]
        ).astype(bf16)

    carried = [pltpu.roll(plain * masks[d - 1], d, 1) for d in range(1, 9)]
    around = receive(HALO, 1).astype(bf16)
    around = hidden_of(w_secondT, hidden_of(w_firstT, around, 0), 1)
    around = jnp.dot(w_out_rows, around, preferred_element_type=f32)[0:1]
    got = receive(0, 1) / (0.02 + 0.08 * (1.0 / (1.0 + jnp.exp(-around))))

    units = reaches // 128
    begin = (ev + 1) * (width // 128)
    odd = lax.rem(begin, 2)
    pieces_left = [(lax.rem(begin + odd + 2 * i, units), 256) for i in range(4)]
    pieces_left.append((lax.rem(begin + 8 * (1 - odd), units), 128))

    for i in range(n_event - 1):
        squash_copy(i).wait_recv()
    squash = jnp.concatenate([squash_all[e] for e in range(n_event)], axis=1)
    rough = 0.02 + 0.08 * squash
    rate = k_base / rough
    slot_rate = pick([jnp.broadcast_to(rate, (16, reaches))], take_send)[0][0:1]
    first_got = got

    def share(k, e):
        return pltpu.make_async_remote_copy(
            src_ref=share_out,
            dst_ref=share_in.at[k, ev],
            send_sem=share_send.at[k, e],
            recv_sem=share_recv.at[k, ev],
            device_id={"basin": lax.rem(me + n - offsets[k], n), "event": e},
            device_id_type=MESH,
        )

    def shared_from(k, e):
        return pltpu.make_async_remote_copy(
            src_ref=share_out,
            dst_ref=share_in.at[k, e],
            send_sem=share_send.at[k, e],
            recv_sem=share_recv.at[k, e],
            device_id={"basin": lax.rem(me + n - offsets[k], n), "event": e},
            device_id_type=MESH,
        )

    shrinks = []
    for t in range(STEPS):
        area, p = areas[t], powers[t]
        flow = rate * area * p
        inflow = lateral[t]
        for d in range(1, 9):
            if t == 0:
                moved = pltpu.roll(jnp.broadcast_to(rate, (8, reaches)), d, 1)[0:1]
                inflow = inflow + carried[d - 1] * moved
            else:
                inflow = inflow + pltpu.roll(flow * masks[d - 1], d, 1)
        shrink = 1.0 / (1.0 + beta * rate * p)
        shrinks.append(shrink)
        kept = (area + beta * inflow) * shrink
        gain = beta * shrink
        if t < STEPS - 1:
            slots = pick([kept, gain], take_send)
        else:
            loads["cotangent"].wait()
            weight = cotangent[...] * rate * (5.0 / 3.0) * gain
            slots = pick([kept, gain, weight], take_recv)
        if t > 0:
            network(*pieces_left.pop(0))
            got = receive(t, 1)
        if t < STEPS - 1:
            slot_area = slots[0] + slots[1] * cross(got, NT)
            send(t + 1, slot_rate * slot_area * slot_power(slot_area), 1)
        else:
            slot_area = slots[0] + slots[1] * got
            send(STEPS, slots[2] * slot_power(slot_area), -1)
        areas.append(kept + gain * scatter(got, take_recv))
        powers.append(power(areas[t + 1]))
    emitted = areas[STEPS] * powers[STEPS]
    outflow[...] = rate * emitted
    write_flow = pltpu.make_async_copy(outflow, outflow_h, out_sem.at[0])
    write_flow.start()
    g_area = cotangent[...] * rate * (5.0 / 3.0) * powers[STEPS]
    g_rate = cotangent[...] * emitted
    for t in reversed(range(STEPS)):
        index = 2 * STEPS - 1 - t
        inner = g_area * shrinks[t]
        g_inflow = inner * beta
        grad_lateral[t] = g_inflow
        g_flow = jnp.zeros((events, reaches), f32)
        for d in range(1, 9):
            g_flow = g_flow + masks[d - 1] * pltpu.roll(g_inflow, reaches - d, 1)
        drop = g_inflow * areas[t + 1] * powers[t]
        g_rate = g_rate - drop + g_flow * areas[t] * powers[t]
        if t > 0:
            lean = (5.0 / 3.0) * rate * powers[t]
            onward = inner - (2.0 / 3.0) * rate * drop / areas[t] + lean * g_flow
            gain = beta * shrinks[t - 1]
            slots = pick([onward * gain, lean * gain], take_recv)
            network(*pieces_left.pop(0))
            got = receive(index, -1)
            onto = slots[0] + slots[1] * cross(got, NN)
            if t > 1:
                send(index + 1, onto, -1)
            else:
                share_out[...] = jnp.sum(onto * first_got, axis=0, keepdims=True)
                for k in range(LINKS):
                    for e in range(n_event):
                        share(k, e).start()
            back = scatter(got, take_send)
            g_rate = g_rate + back * areas[t] * powers[t]
            g_area = onward + lean * back
    write_lateral = pltpu.make_async_copy(grad_lateral, grad_lateral_h, out_sem.at[1])
    write_lateral.start()
    rate_out[...] = jnp.sum(g_rate, axis=0, keepdims=True)

    def rate_copy(i):
        return pltpu.make_async_remote_copy(
            src_ref=rate_out,
            dst_ref=rate_in.at[i],
            send_sem=r_send.at[i],
            recv_sem=r_recv.at[i],
            device_id={"event": lax.rem(ev + 1 + i, n_event)},
            device_id_type=MESH,
        )

    for i in range(n_event - 1):
        rate_copy(i).start()
    network(*pieces_left.pop(0))
    for i in range(n_event - 1):
        rate_copy(i).wait_recv()
    slot_group = lax.broadcasted_iota(jnp.int32, (1, LINKS * GROUP), 1) // GROUP
    shares = jnp.zeros((1, LINKS * GROUP), f32)
    for k in range(LINKS):
        for e in range(n_event):
            shared_from(k, e).wait_recv()
        total = share_in[k, 0]
        for e in range(1, n_event):
            total = total + share_in[k, e]
        shares = jnp.where(slot_group == k, total, shares)
    shared = scatter(jnp.broadcast_to(shares, (16, LINKS * GROUP)), take_send)[0:1] / rate
    terms = [rate_out[...]] + [rate_in[i] for i in range(n_event - 1)]
    g_sum = jnp.zeros((1, reaches), f32)
    for e in range(n_event):
        term = terms[0]
        for i in range(n_event - 1):
            term = jnp.where(lax.rem(e + 1 + i, n_event) == ev, terms[i + 1], term)
        g_sum = g_sum + term
    g_sum = g_sum + shared
    g_logit = (
        g_sum * (-rate / rough) * (scale * 0.08) * squash * (1.0 - squash)
    ).astype(bf16)
    g_logit32 = g_logit.astype(f32)

    scaled = (h_one[mine, :].astype(f32) * g_logit32).astype(bf16)
    large = lax.dot_general(scaled, d_two[...], NT, preferred_element_type=f32)
    tiles = hid // 128
    for d in range(owners):
        for r in range(chunk // 8):
            for c in range(tiles):
                top = d * chunk + 8 * r
                slab[d, r * tiles + c] = large[top : top + 8, 128 * c : 128 * c + 128]

    def when_owner(index, work):
        if owners == n:
            work()
        else:
            pl.when(index < owners)(work)

    line = n // 2
    low = lax.rem(me, 2)
    spot = me // 2
    pair = me + 1 - 2 * low
    half = lax.rem(ev + n_event // 2, n_event)
    twin = ev + 1 - 2 * lax.rem(ev, 2)
    twin_half = lax.rem(twin + n_event // 2, n_event)
    span = slab.shape[1]
    cut = (span + 1) // 2
    halves = (pl.ds(0, cut), pl.ds(cut, span - cut))

    def each(first, last, work):
        if last - first <= 4:
            for j in range(first, last):
                work(j)
        else:
            pl.loop(first, last)(work)

    def near(j):
        if line != 4:
            return lax.rem(spot + j, line)
        if isinstance(j, int) and j == 0:
            return spot
        orders = ((1, 2, 3), (2, 0, 3), (1, 3, 0), (2, 1, 0))
        code = sum(orders[s][j - 1] * 4 ** s for s in range(4))
        power_of = (1 + 3 * lax.rem(spot, 2)) * (1 + 15 * (spot // 2))
        return lax.rem(code // power_of, 4)

    def device(z, parity):
        return 2 * z + parity

    def pair_sum(h, z, parity):
        return pltpu.make_async_remote_copy(
            src_ref=slab.at[device(z, parity), halves[h]], dst_ref=rs_pair.at[z, halves[h]],
            send_sem=px_send.at[h, z], recv_sem=px_recv.at[h, z],
            device_id={"basin": pair}, device_id_type=MESH,
        )

    def line_sum(h, z, sender):
        return pltpu.make_async_remote_copy(
            src_ref=rs_pair.at[z, halves[h]], dst_ref=rs_line.at[sender, halves[h]],
            send_sem=pz_send.at[h, z], recv_sem=pz_recv.at[h, sender],
            device_id={"basin": device(z, low)}, device_id_type=MESH,
        )

    def far(j):
        return near(line - 1 - j)

    def start_pair(h, j):
        z = far(j)
        when_owner(device(z, 1 - low), lambda: pair_sum(h, z, 1 - low).start())

    each(0, line, functools.partial(start_pair, 0))

    g_pre = (lower[...] * g_logit32).astype(bf16)
    place = lax.broadcasted_iota(jnp.int32, (PLACES, reaches), 0)
    row_two = jnp.where(place == feat + 1, g_logit32, 0.0).astype(bf16)
    row_out = jnp.where(place == feat + 2, g_logit32, 0.0).astype(bf16)
    g_two = d_two[mine, :]
    second = h_two[mine, :]

    def narrow(first):
        end = first + 128
        return (
            lax.dot_general(attrs[...], g_pre[first:end], NT, preferred_element_type=f32)
            + lax.dot_general(row_two, g_two[first:end], NT, preferred_element_type=f32)
            + lax.dot_general(row_out, second[first:end], NT, preferred_element_type=f32)
        )

    left = narrow(0)
    right = narrow(part - 128)
    first_half = lax.broadcasted_iota(jnp.int32, (8, 128), 1) < 64
    last = slab.shape[1] - 1
    for k in range(5):
        slab[k, last] = left[8 * k : 8 * k + 8]
    for k in range(3):
        even = pltpu.roll(right[16 * k : 16 * k + 8], 64, 1)
        slab[5 + k, last] = jnp.where(first_half, even, right[16 * k + 8 : 16 * k + 16])
    for d in range(8, owners):
        slab[d, last] = jnp.zeros((8, 128), f32)

    each(0, line, functools.partial(start_pair, 1))

    for i in range(n_event - 1):
        squash_copy(i).wait_send()
    for index in range(HALO + 1):
        for k in range(LINKS):
            if index != 2 * STEPS - 1:
                message(index, k, 1).wait_send()
    for k in range(LINKS):
        for e in range(n_event):
            share(k, e).wait_send()
    for i in range(n_event - 1):
        rate_copy(i).wait_send()
    write_flow.wait()
    write_lateral.wait()

    def add_pair(h, j):
        z = far(j)

        def go():
            pair_sum(h, z, 1 - low).wait_recv()
            rs_pair[z, halves[h]] = rs_pair[z, halves[h]] + slab[device(z, low), halves[h]]

            @pl.when(z != spot)
            def _():
                line_sum(h, z, spot).start()

        when_owner(device(z, low), go)

    def move(event, at, h, sems, slot, target):
        ref = full.at[event, at, halves[h]]
        return pltpu.make_async_remote_copy(
            src_ref=ref, dst_ref=ref, send_sem=sems[0].at[slot], recv_sem=sems[1].at[slot],
            device_id=target, device_id_type=MESH,
        )

    def to_line(h, source, peer):
        ref = full.at[ev, device(source, low), halves[h]]
        return pltpu.make_async_remote_copy(
            src_ref=ref, dst_ref=ref, send_sem=az_send.at[h, peer], recv_sem=az_recv.at[h, source],
            device_id={"basin": device(peer, low)}, device_id_type=MESH,
        )

    def to_pair(h, z, parity):
        return move(ev, device(z, parity), h, (ax_send.at[h], ax_recv.at[h]), z, {"basin": pair})

    def to_half(h, event, z):
        return move(event, device(z, low), h, (ay_send.at[h], ay_recv.at[h]), z, {"event": half})

    def on_half(event, z):
        return move(event, device(z, 1 - low), 0, (fa_send, fa_recv), z, {"event": half})

    def on_half_two(event, z):
        return move(event, device(z, 1 - low), 1, (fb_send, fb_recv), z, {"event": half})

    def to_twin(side, event, z):
        ref = full.at[event, pl.ds(2 * z, 2)]
        return pltpu.make_async_remote_copy(
            src_ref=ref, dst_ref=ref, send_sem=tw_send.at[side, z], recv_sem=tw_recv.at[side, z],
            device_id={"event": twin}, device_id_type=MESH,
        )

    def own(h):
        def go():
            total = rs_pair[spot, halves[h]]
            if line <= 4:
                for j in range(1, line):
                    sender = near(j)
                    line_sum(h, spot, sender).wait_recv()
                    total = total + rs_line[sender, halves[h]]
            else:

                def add(i, total):
                    sender = lax.rem(spot + line - i, line)
                    line_sum(h, spot, sender).wait_recv()
                    return total + rs_line[sender, halves[h]]

                total = lax.fori_loop(1, line, add, total)
            full[ev, me, halves[h]] = total
            each(1, line, lambda j: to_line(h, spot, near(line - j)).start())
            to_pair(h, spot, low).start()
            to_half(h, ev, spot).start()

        when_owner(me, go)

    def from_line(h, j):
        z = near(j)

        def go():
            to_line(h, z, spot).wait_recv()
            to_pair(h, z, low).start()
            to_half(h, ev, z).start()

        when_owner(device(z, low), go)

    def hop(h, j):
        z = near(j)

        def go():
            if h == 0:
                to_pair(0, z, 1 - low).wait_recv()
                on_half(ev, z).start()
            else:
                to_pair(1, z, 1 - low).wait_recv()
                on_half_two(ev, z).start()

        when_owner(2 * z, go)

    def corner(j):
        z = near(j)

        def go():
            to_twin(0, ev, z).start()
            to_half(0, half, z).wait_recv()
            to_half(1, half, z).wait_recv()
            on_half(half, z).wait_recv()
            on_half_two(half, z).wait_recv()
            to_twin(1, half, z).start()

        when_owner(2 * z, go)

    if line == 4:
        for j in range(line):
            add_pair(0, j)
        add_pair(1, 0)
        add_pair(1, 1)
        own(0)
        add_pair(1, 2)
        add_pair(1, 3)
        hop(0, 0)
        from_line(0, 1)
        own(1)
        for work, h, j in (
            (from_line, 0, 2), (from_line, 0, 3), (hop, 0, 1), (hop, 1, 0), (from_line, 1, 1),
            (hop, 0, 2), (from_line, 1, 2), (hop, 0, 3), (from_line, 1, 3), (hop, 1, 1),
            (hop, 1, 2), (hop, 1, 3),
        ):
            work(h, j)
    else:
        for h in range(2):
            each(0, line, functools.partial(add_pair, h))
        for h in range(2):
            own(h)
        for h in range(2):
            each(1, line, functools.partial(from_line, h))
        for h in range(2):
            each(0, line, functools.partial(hop, h))
    def settle(z):
        for h in range(2):
            when_owner(device(z, 1 - low), lambda: pair_sum(h, z, 1 - low).wait_send())

            @pl.when(z != spot)
            def _():
                when_owner(device(z, low), lambda: line_sum(h, z, spot).wait_send())
                when_owner(me, lambda: to_line(h, spot, z).wait_send())

        def go():
            for h in range(2):
                to_pair(h, z, low).wait_send()
                to_half(h, ev, z).wait_send()

        when_owner(2 * z, go)

    def drain(z):
        def go():
            on_half(ev, z).wait_send()
            on_half_two(ev, z).wait_send()
            to_twin(0, ev, z).wait_send()
            to_twin(1, half, z).wait_send()

        when_owner(2 * z, go)

    each(0, line - 1, corner)
    each(0, line, settle)
    corner(line - 1)

    def write_full(z):
        where = pl.ds(2 * z, 2)
        return pltpu.make_async_copy(full.at[:, where], full_h.at[:, where], write_sem.at[z])

    def arrive(j):
        z = near(j)

        def go():
            to_twin(0, twin, z).wait_recv()
            to_twin(1, twin_half, z).wait_recv()
            write_full(z).start()

        when_owner(2 * z, go)

    each(0, line, arrive)
    each(0, line, drain)
    each(0, line, lambda j: when_owner(2 * near(j), lambda: write_full(near(j)).wait()))


def finish(
    feat, full_in, flow_in, lateral_in,
    large, flow_out, lateral_out, w_first, b_first, b_second, w_out,
    full, flow, lateral, small, vectors, sems, small_sems,
):
    last = full.shape[2] - 1
    steps = []
    for side in range(full.shape[0]):
        where = pl.ds(side, 1)
        steps.append((full_in.at[where], full.at[where], full.at[where, :, pl.ds(0, last)], large.at[where]))
    steps.append((lateral_in, lateral, lateral, lateral_out))
    steps.append((flow_in, flow, flow, flow_out))
    reads = [pltpu.make_async_copy(x[0], x[1], sems.at[0, i]) for i, x in enumerate(steps)]
    copies = [pltpu.make_async_copy(x[2], x[3], sems.at[1, i]) for i, x in enumerate(steps)]
    for read in reads:
        read.start()
    for read, copy in zip(reads, copies):
        read.wait()
        copy.start()
    n_event = full.shape[0]
    first_half = lax.broadcasted_iota(jnp.int32, (8, 128), 1) < 64
    for k in range(5):
        columns = []
        for e in range(0, n_event, 2):
            tails = []
            for s in range(2):
                tail = full[e + s, 5 + k // 2, last]
                tails.append(pltpu.roll(tail, 64, 1) if k % 2 != s else tail)
            turned = pltpu.roll(full[e + 1, k, last], 64, 1)
            columns += [
                full[e, k, last],
                jnp.where(first_half, tails[0], turned),
                jnp.where(first_half, turned, tails[1]),
            ]
        rows = jnp.concatenate(columns, axis=1)
        if k < 4:
            small[8 * k : 8 * k + 8, :] = rows
        else:
            for i, held in enumerate(vectors):
                held[...] = rows[i : i + 1].reshape(rows.shape[1])
    pairs = [(small, w_first)] + list(zip(vectors, (b_first, b_second, w_out)))
    for i, (held, target) in enumerate(pairs):
        copies.append(pltpu.make_async_copy(held, target, small_sems.at[i]))
        copies[-1].start()
    for copy in copies:
        copy.wait()


def body(
    n,
    n_event,
    reach_attrs,
    w_first,
    b_first,
    w_second,
    b_second,
    w_out,
    section_factor,
    bed_slope,
    seg_count,
    section_class,
    down_local,
    send_list,
    recv_list,
    area_start,
    lateral,
    cotangent,
):
    f32, bf16 = jnp.float32, jnp.bfloat16
    events, reaches = area_start.shape
    feat, hid = w_first.shape
    part = hid // n_event
    owners = n if part % (8 * n) == 0 else part // 8
    chunk = part // owners
    span = (chunk // 8) * (hid // 128) + 1
    line = n // 2
    scale = 32.0 / math.sqrt(events * n_event * reaches * n)
    vmem = pl.BlockSpec(memory_space=pltpu.VMEM)
    hbm = pl.BlockSpec(memory_space=pltpu.HBM)
    smem = pl.BlockSpec(memory_space=pltpu.SMEM)
    dma = pltpu.SemaphoreType.DMA
    held = lambda x: pltpu.VMEM(x.shape, x.dtype)
    outflow, grad_lateral, full = pl.pallas_call(
        functools.partial(kernel, n, n_event, owners, chunk, scale),
        out_shape=(
            jax.ShapeDtypeStruct((events, reaches), f32),
            jax.ShapeDtypeStruct((STEPS, events, reaches), f32),
            jax.ShapeDtypeStruct((n_event, owners, span, 8, 128), f32),
        ),
        in_specs=[hbm] * 6 + [smem] + [hbm] * 9,
        out_specs=(hbm,) * 3,
        scratch_shapes=[
            pltpu.VMEM((events, reaches), f32),
            pltpu.VMEM((STEPS, events, reaches), f32),
            pltpu.VMEM((n_event, owners, span, 8, 128), f32),
            dma((2,)),
            pltpu.VMEM((PLACES, reaches), bf16),
            held(w_first), held(b_first), held(w_second), held(b_second), held(w_out),
            held(bed_slope), held(seg_count), held(section_class), held(down_local),
            held(send_list), held(recv_list), held(area_start), held(lateral), held(cotangent),
            dma((15,)),
            pltpu.VMEM((hid, feat), bf16),
            pltpu.VMEM((hid, hid), bf16),
            pltpu.VMEM((hid, 8), f32),
            pltpu.VMEM((hid, reaches), f32),
            pltpu.VMEM((hid, reaches), bf16),
            pltpu.VMEM((hid, reaches), bf16),
            pltpu.VMEM((hid, reaches), bf16),
            pltpu.VMEM((part, reaches), f32),
            pltpu.VMEM((n_event, 1, reaches // n_event), f32),
            pltpu.VMEM((LINKS * GROUP, reaches), bf16),
            pltpu.VMEM((LINKS * GROUP, reaches), bf16),
            pltpu.VMEM((LINKS * GROUP, LINKS * GROUP), bf16),
            pltpu.VMEM((HALO + 1, LINKS, 8, 128), f32),
            pltpu.VMEM((HALO + 1, LINKS, 8, 128), f32),
            pltpu.VMEM((1, LINKS * GROUP), f32),
            pltpu.VMEM((LINKS, n_event, 1, LINKS * GROUP), f32),
            dma((LINKS, n_event)),
            dma((LINKS, n_event)),
            pltpu.VMEM((1, reaches), f32),
            pltpu.VMEM((n_event - 1, 1, reaches), f32),
            pltpu.VMEM((owners, span, 8, 128), f32),
            pltpu.VMEM((line, span, 8, 128), f32),
            pltpu.VMEM((line, span, 8, 128), f32),
            dma((n_event - 1,)), dma((n_event - 1,)),
            dma((HALO + 1, LINKS)), dma((HALO + 1, LINKS)),
            dma((n_event - 1,)), dma((n_event - 1,)),
            dma((2, line)), dma((2, line)), dma((2, line)), dma((2, line)),
            dma((2, line)), dma((2, line)), dma((2, line)), dma((2, line)),
            dma((2, line)), dma((2, line)),
            dma((line,)), dma((line,)), dma((line,)), dma((line,)), dma((2, line)), dma((2, line)),
            dma((line,)),
        ],
        compiler_params=pltpu.CompilerParams(
            collective_id=0, has_side_effects=True, vmem_limit_bytes=63 * 1024 * 1024
        ),
    )(
        reach_attrs.T, w_first, b_first, w_second, b_second, w_out, section_factor,
        bed_slope, seg_count, section_class, down_local, send_list, recv_list,
        area_start, lateral, cotangent,
    )
    vector = jax.ShapeDtypeStruct((hid,), f32)
    w_first_f32 = jax.ShapeDtypeStruct((feat, hid), f32)
    large, outflow, grad_lateral, g_first, g_b_first, g_b_second, g_out = pl.pallas_call(
        functools.partial(finish, feat),
        out_shape=(
            jax.ShapeDtypeStruct((n_event, owners, span - 1, 8, 128), f32),
            jax.ShapeDtypeStruct((events, reaches), f32),
            jax.ShapeDtypeStruct((STEPS, events, reaches), f32),
            w_first_f32,
            vector,
            vector,
            vector,
        ),
        in_specs=[hbm] * 3,
        out_specs=(hbm,) * 7,
        scratch_shapes=[
            held(full), held(outflow), held(grad_lateral),
            held(w_first_f32), [held(vector)] * 3, dma((2, n_event + 2)), dma((4,)),
        ],
    )(full, outflow, grad_lateral)
    g_second = large.reshape(hid // 8, hid // 128, 8, 128).transpose(0, 2, 1, 3).reshape(hid, hid)
    return outflow, grad_lateral, g_first, g_b_first, g_second, g_b_second, g_out


def solution(mesh):
    return jax.shard_map(
        functools.partial(body, mesh.shape["basin"], mesh.shape["event"]),
        mesh=mesh,
        in_specs=(
            P("basin", None),
            P(),
            P(),
            P(),
            P(),
            P(),
            P(),
            P("basin"),
            P("basin"),
            P("basin"),
            P("basin"),
            P("basin", None, None),
            P("basin", None, None),
            P("event", "basin"),
            P(None, "event", "basin"),
            P("event", "basin"),
        ),
        out_specs=(P("event", "basin"), P(None, "event", "basin"), P(), P(), P(), P(), P()),
        check_vma=False,
    )
```
